32 devices in a mesh: seq: 16 (over z, y, core), head: 2 (over x).
Axes of the slice: x: 2, y: 2, z: 4, core: 2. Of those that a mesh axis runs over, the one named last changes fastest.
Arguments:
- queries: bfloat16 [2048, 1024], P('seq', 'head'), may hold values from -8 to 8
- keys: bfloat16 [2048, 1024], P('seq', 'head'), may hold values from -8 to 8
- values: bfloat16 [2048, 1024], P('seq', 'head'), may hold values from -6 to 6
- out_grad: bfloat16 [2048, 1024], P('seq', 'head'), may hold values from -6 to 6
- rel_emb: bfloat16 [512, 1024], replicated, may hold values from -6 to 6
- w_query: bfloat16 [1024, 1024], P(None, 'head'), may hold values from -0.1875 to 0.1875
- w_key: bfloat16 [1024, 1024], P(None, 'head'), may hold values from -0.1875 to 0.1875
- doc_lengths: int32 [8], replicated, may hold values from 1 to 512, 2048 in all
- bucket_table: int32 [1024], replicated, may hold values from 0 to 511, as said below
Outputs:
- query_grad: bfloat16 [2048, 1024], P('seq', 'head')
- key_grad: bfloat16 [2048, 1024], P('seq', 'head')
- value_grad: bfloat16 [2048, 1024], P('seq', 'head')
- rel_emb_grad: float32 [512, 1024], P(None, 'head')
- w_query_grad: float32 [1024, 1024], P('seq', 'head')
- w_key_grad: float32 [1024, 1024], P('seq', 'head')
The draws below stay inside these ranges and needn't reach their ends.
Inputs may be any that keep to these rules, and one draw needn't show every extreme that they name: `doc_lengths`: the lengths sum to 2048 and the longest is exactly 512. `bucket_table`: entry o is the bucket of the relative offset o - 512; entries never fall as o grows, and equal o - 512 + 512 // 2 wherever o - 512 lies between -128 and 128.
All inputs are finite; a program needn't handle non-finite values.
Results may differ from the reference program's by a relative error of at most 0.01.
Values may be sent and summed in bfloat16 or wider, within the bound.
No kernel may reach another device: no remote copies, remote signals or barrier semaphores. Data moves between devices by JAX's collectives and lax.ppermute only.
A program may use at most 64 MiB of HBM per device.

```python
import math
import jax
import jax.numpy as jnp
import numpy as np
from jax import lax

D = 1024
HEADS = 16
HD = 64
BUCKETS = 512
TOK_DEV = 128
DOC_MAX = 512
TOKENS = 2048
NDOCS = 8


def draw_queries(key, part):
    shape = (TOKENS, HEADS * HD)
    base = jax.random.truncated_normal(jax.random.fold_in(key, 1), -6.0, 6.0, shape, jnp.float32)
    return base.astype(jnp.bfloat16)


def draw_keys(key, part):
    shape = (TOKENS, HEADS * HD)
    base = jax.random.truncated_normal(jax.random.fold_in(key, 2), -6.0, 6.0, shape, jnp.float32)
    return base.astype(jnp.bfloat16)


def draw_bucket_table(key, part):
    half_count = BUCKETS // 2
    near_count = BUCKETS // 4
    distance = jnp.arange(DOC_MAX + 1, dtype=jnp.int32)

    def one_side(side_key):
        advance = (jax.random.randint(side_key, (DOC_MAX + 1,), 0, 4) == 0).astype(jnp.int32)
        advance = jnp.where(distance > DOC_MAX - half_count, 1, advance)
        advance = jnp.where(distance <= near_count, 0, advance)
        return jnp.where(distance <= near_count, distance, near_count + jnp.cumsum(advance).astype(jnp.int32))
    upper_level = one_side(jax.random.fold_in(key, 21))
    lower_level = one_side(jax.random.fold_in(key, 22))
    upper_side = half_count + jnp.minimum(half_count - 1, upper_level)
    lower_side = half_count - jnp.minimum(half_count, lower_level)
    table = jnp.concatenate([jnp.flip(lower_side[1:]), upper_side[:DOC_MAX]])
    return table.astype(jnp.int32)


def levels(key, shape, cuts, low, high):
    factor_of = 1.0
    for dim, shards_of in cuts:
        heights = jax.random.uniform(jax.random.fold_in(jax.random.fold_in(key, 6), dim), (shards_of,), jnp.float32, low / len(cuts), high / len(cuts))
        factor_of = factor_of * jnp.repeat(jnp.exp(heights), shape[dim] // shards_of).reshape((-1,) + (1,) * (len(shape) - 1 - dim))
    return factor_of


def length_profile(count, total, bound, lean):
    portions = [(1 << 20) // math.isqrt(grade ** lean) + 1 for grade in range(2, count + 1)]
    surplus, holding = total - bound - (count - 1), [1] * (count - 1)
    while surplus > 0:
        movable = [i for i in range(count - 1) if holding[i] < bound]
        pool, remaining = sum([portions[i] for i in movable]), surplus
        for i in movable:
            more = min(bound - holding[i], max(1, remaining * portions[i] // pool), surplus)
            holding[i] = holding[i] + more
            surplus = surplus - more
    return np.array([bound] + holding)


def ragged(key, amount, total, bound, skew):
    if amount == 2:
        one = jax.random.randint(key, (), max(1, total - bound), min(bound, total - 1) + 1)
        return jnp.stack([one, total - one])
    tallies = jnp.asarray(length_profile(amount, total, bound, skew), jnp.int32)
    twos = (amount - 1) // 2
    donor, taker = tallies[1:1 + 2 * twos:2], tallies[2:2 + 2 * twos:2]
    slack = jnp.minimum(donor - 1, bound - taker)
    moved = jax.random.randint(jax.random.fold_in(key, 1), (twos,), 0, 1 << 20) % (slack + 1)
    tallies = tallies.at[1:1 + 2 * twos:2].set(donor - moved).at[2:2 + 2 * twos:2].set(taker + moved)
    return tallies[jax.random.permutation(jax.random.fold_in(key, 2), amount)]


def normal_values(stream_key, dims, scale, most, shards=(), kind=jnp.bfloat16):
    result = scale * jax.random.normal(stream_key, dims, jnp.float32)
    if shards:
        result = result * levels(stream_key, dims, shards, -0.22, 0.18)
    return jnp.clip(result, -most, most).astype(kind)


def setup_inputs(seed: int = 0) -> dict:
    arg_keys = jax.random.split(jax.random.key(seed), 10)
    queries = draw_queries(jax.random.fold_in(arg_keys[9], 71), 0)
    keys = draw_keys(jax.random.fold_in(arg_keys[9], 71), 0)
    values = normal_values(arg_keys[2], (TOKENS, HEADS * HD), 1.0, 6.0, ((0, 16), (1, 2)))
    out_grad = normal_values(arg_keys[3], (TOKENS, HEADS * HD), 1.0, 6.0, ((0, 16), (1, 2)))
    rel_emb = normal_values(arg_keys[4], (BUCKETS, D), 1.0, 6.0)
    w_query = normal_values(arg_keys[5], (D, HEADS * HD), D ** -0.5, 0.1875, ((1, 2),))
    w_key = normal_values(arg_keys[6], (D, HEADS * HD), D ** -0.5, 0.1875, ((1, 2),))
    doc_lengths = ragged(arg_keys[7], NDOCS, TOKENS, DOC_MAX, 2).astype(jnp.int32)
    bucket_table = draw_bucket_table(jax.random.fold_in(arg_keys[9], 71), 0)
    return {"queries": queries, "keys": keys, "values": values, "out_grad": out_grad, "rel_emb": rel_emb, "w_query": w_query, "w_key": w_key, "doc_lengths": doc_lengths, "bucket_table": bucket_table}


masked_score = -1e+30

def contract(left, right, left_dim, right_dim):
    return lax.dot_general(left, right, (((left_dim,), (right_dim,)), ((), ())), preferred_element_type=jnp.float32)

def doc_index(position, doc_ends, extent):
    inside = (position >= 0) & (position < extent)
    owner = lax.optimization_barrier(jnp.sum((doc_ends[None, :] <= position[:, None]).astype(jnp.int32), axis=1))
    return jnp.where(inside, owner, -1)

def pair_tables(query_pos, key_pos, doc_ends, bucket_table, extent):
    offset_span = bucket_table.shape[0] // 2
    query_doc = doc_index(query_pos, doc_ends, extent)
    key_doc = doc_index(key_pos, doc_ends, extent)
    same_doc = query_doc[:, None] == key_doc[None, :]
    relative = query_pos[:, None] - key_pos[None, :]
    ahead_bucket = bucket_table[jnp.clip(relative + offset_span, 0, 2 * offset_span - 1)]
    behind_bucket = bucket_table[jnp.clip(offset_span - relative, 0, 2 * offset_span - 1)]
    return (same_doc, ahead_bucket, behind_bucket)

def pair_scores(query_rows, key_rows, pos_keys, pos_queries, ahead_bucket, behind_bucket, same_doc, score_scale):
    row_number = jnp.arange(query_rows.shape[0])[:, None]
    key_number = jnp.arange(key_rows.shape[0])[None, :]
    content = contract(query_rows, key_rows, 1, 1)
    query_term = contract(query_rows, pos_keys, 1, 1)[row_number, ahead_bucket]
    key_term = contract(key_rows, pos_queries, 1, 1)[key_number, behind_bucket]
    return jnp.where(same_doc, score_scale * (content + query_term + key_term), masked_score)

def query_side(query_rows, key_rows, value_rows, grad_rows, pos_keys, pos_queries, ahead_bucket, behind_bucket, same_doc, score_scale):
    scores = pair_scores(query_rows, key_rows, pos_keys, pos_queries, ahead_bucket, behind_bucket, same_doc, score_scale)
    row_max = lax.optimization_barrier(jnp.max(scores, axis=1, keepdims=True))
    expd = jnp.where(same_doc, jnp.exp(scores - row_max), 0.0)
    row_sum = lax.optimization_barrier(jnp.sum(expd, axis=1, keepdims=True))
    probs = expd / row_sum
    probs_low = probs.astype(jnp.bfloat16)
    dprobs = contract(grad_rows, value_rows, 1, 1)
    row_dot = lax.optimization_barrier(jnp.sum(probs * dprobs, axis=1, keepdims=True))
    dscores = probs * (dprobs - row_dot)
    dscores_low = dscores.astype(jnp.bfloat16)
    dscores_back = dscores_low.astype(jnp.float32)
    row_number = jnp.arange(query_rows.shape[0])[:, None]
    key_number = jnp.arange(key_rows.shape[0])[None, :]
    buckets = pos_keys.shape[0]
    ahead_grad = jnp.zeros((query_rows.shape[0], buckets), jnp.float32).at[row_number, ahead_bucket].add(dscores_back)
    ahead_low = ahead_grad.astype(jnp.bfloat16)
    behind_grad = jnp.zeros((key_rows.shape[0], buckets), jnp.float32).at[key_number, behind_bucket].add(dscores_back)
    behind_low = behind_grad.astype(jnp.bfloat16)
    query_grad = score_scale * (contract(dscores_low, key_rows, 1, 0) + contract(ahead_low, pos_keys, 1, 0))
    key_grad = score_scale * (contract(dscores_low, query_rows, 0, 0) + contract(behind_low, pos_queries, 1, 0))
    value_grad = contract(probs_low, grad_rows, 0, 0)
    bucket_key = score_scale * contract(ahead_low, query_rows, 0, 0)
    bucket_query = score_scale * contract(behind_low, key_rows, 0, 0)
    return (query_grad, key_grad, value_grad, bucket_key, bucket_query)

def split_heads(matrix):
    return matrix.reshape(matrix.shape[0], HEADS, HD).transpose(1, 0, 2)

def join_heads(stacked):
    return stacked.transpose(1, 0, 2).reshape(stacked.shape[1], HEADS * HD)

def reference(queries, keys, values, out_grad, rel_emb, w_query, w_key, doc_lengths, bucket_table):
    score_scale = 1.0 / math.sqrt(3.0 * HD)
    feature_count = HEADS * HD
    pos_key = jnp.dot(rel_emb, w_key, preferred_element_type=jnp.float32).astype(jnp.bfloat16)
    pos_query = jnp.dot(rel_emb, w_query, preferred_element_type=jnp.float32).astype(jnp.bfloat16)
    pos_key_heads = split_heads(pos_key)
    pos_query_heads = split_heads(pos_query)
    doc_ends = jnp.cumsum(doc_lengths).astype(jnp.int32)
    keys_padded = jnp.pad(keys, ((DOC_MAX, DOC_MAX), (0, 0)))
    values_padded = jnp.pad(values, ((DOC_MAX, DOC_MAX), (0, 0)))
    window = TOK_DEV + 2 * DOC_MAX
    block_count = TOKENS // TOK_DEV

    def advance(running, block_index):
        key_acc, value_acc, bucket_key_acc, bucket_query_acc = running
        first_token = (block_index * TOK_DEV).astype(jnp.int32)
        query_block = lax.dynamic_slice_in_dim(queries, first_token, TOK_DEV, 0)
        grad_block = lax.dynamic_slice_in_dim(out_grad, first_token, TOK_DEV, 0)
        key_window = lax.dynamic_slice_in_dim(keys_padded, first_token, window, 0)
        value_window = lax.dynamic_slice_in_dim(values_padded, first_token, window, 0)
        query_pos = first_token + jnp.arange(TOK_DEV, dtype=jnp.int32)
        key_pos = first_token - DOC_MAX + jnp.arange(window, dtype=jnp.int32)
        same_doc, ahead_bucket, behind_bucket = pair_tables(query_pos, key_pos, doc_ends, bucket_table, TOKENS)

        def per_head(query_rows, key_rows, value_rows, grad_rows, pos_keys, pos_queries):
            return query_side(query_rows, key_rows, value_rows, grad_rows, pos_keys, pos_queries, ahead_bucket, behind_bucket, same_doc, score_scale)
        query_grad, key_grad, value_grad, bucket_key, bucket_query = jax.vmap(per_head)(split_heads(query_block), split_heads(key_window), split_heads(value_window), split_heads(grad_block), pos_key_heads, pos_query_heads)
        old_keys = lax.dynamic_slice_in_dim(key_acc, first_token, window, 0)
        key_acc = lax.dynamic_update_slice_in_dim(key_acc, old_keys + join_heads(key_grad), first_token, 0)
        old_values = lax.dynamic_slice_in_dim(value_acc, first_token, window, 0)
        value_acc = lax.dynamic_update_slice_in_dim(value_acc, old_values + join_heads(value_grad), first_token, 0)
        running = (key_acc, value_acc, bucket_key_acc + bucket_key, bucket_query_acc + bucket_query)
        return (running, join_heads(query_grad))
    start_state = (jnp.zeros((TOKENS + 2 * DOC_MAX, feature_count), jnp.float32), jnp.zeros((TOKENS + 2 * DOC_MAX, feature_count), jnp.float32), jnp.zeros((HEADS, BUCKETS, HD), jnp.float32), jnp.zeros((HEADS, BUCKETS, HD), jnp.float32))
    final_state, query_blocks = lax.scan(advance, start_state, jnp.arange(block_count, dtype=jnp.int32))
    key_acc, value_acc, bucket_key_acc, bucket_query_acc = final_state
    query_grad = query_blocks.reshape(TOKENS, feature_count).astype(jnp.bfloat16)
    key_grad = key_acc[DOC_MAX:DOC_MAX + TOKENS].astype(jnp.bfloat16)
    value_grad = value_acc[DOC_MAX:DOC_MAX + TOKENS].astype(jnp.bfloat16)
    bucket_key = join_heads(bucket_key_acc).astype(jnp.bfloat16)
    bucket_query = join_heads(bucket_query_acc).astype(jnp.bfloat16)
    rel_emb_grad = contract(bucket_key, w_key, 1, 1) + contract(bucket_query, w_query, 1, 1)
    w_key_grad = contract(rel_emb, bucket_key, 0, 0)
    w_query_grad = contract(rel_emb, bucket_query, 0, 0)
    return (query_grad, key_grad, value_grad, rel_emb_grad, w_query_grad, w_key_grad)
```

```python
import math

import jax
import jax.numpy as jnp
from jax import lax
from jax.experimental import pallas as pl
from jax.experimental.pallas import tpu as pltpu
from jax.sharding import PartitionSpec as P

HD = 64
SPAN = 4
TILE = 128
BF = jnp.bfloat16
F32 = jnp.float32


masked_score = -1e30


def shifted(block, axis, distance):
    devices = range(lax.axis_size(axis))
    route = [(i - distance, i) for i in devices if i - distance in devices]
    return lax.ppermute(block, axis, route)


def contract(left, right, left_dim, right_dim):
    return lax.dot_general(
        left, right, (((left_dim,), (right_dim,)), ((), ())), preferred_element_type=jnp.float32
    )


def doc_index(position, doc_ends, extent):
    inside = (position >= 0) & (position < extent)
    owner = jnp.sum((doc_ends[None, :] <= position[:, None]).astype(jnp.int32), axis=1)
    return jnp.where(inside, owner, -1)


def same_document(row_pos, col_pos, doc_ends, extent):
    return (
        doc_index(row_pos, doc_ends, extent)[:, None]
        == doc_index(col_pos, doc_ends, extent)[None, :]
    )


def tile_tables(bucket_table, shift, rows, buckets):
    offset_span = bucket_table.shape[0] // 2
    spread = jnp.arange(2 * rows - 1, dtype=jnp.int32) - (rows - 1)
    ahead_index = bucket_table[jnp.clip(shift - spread + offset_span, 0, 2 * offset_span - 1)]
    behind_index = bucket_table[jnp.clip(offset_span - shift - spread, 0, 2 * offset_span - 1)]
    bucket_ids = jnp.arange(buckets, dtype=jnp.int32)[None, :]
    ahead_onehot = (ahead_index[:, None] == bucket_ids).astype(jnp.bfloat16)
    behind_onehot = (behind_index[:, None] == bucket_ids).astype(jnp.bfloat16)
    return (ahead_index, behind_index, ahead_onehot, behind_onehot)


def skew_in(spread, width):
    rows = spread.shape[0]
    line = rows + width - 1
    flat = jnp.pad(spread, ((0, 0), (0, 1))).reshape(-1)
    return flat[rows - 1 : rows - 1 + rows * line].reshape(rows, line)[:, :width]


def skew_out(dense):
    rows, width = dense.shape
    line = rows + width - 1
    padded = jnp.pad(dense, ((0, 0), (0, rows - 1))).reshape(-1)
    flat = jnp.pad(padded, (rows - 1, 1))
    return flat.reshape(rows, line + 1)[:, :line]


def tile_scores(
    query_rows, key_rows, pos_keys, pos_queries, ahead_onehot, behind_onehot, score_scale
):
    content = contract(query_rows, key_rows, 1, 1)
    ahead_band = contract(ahead_onehot, pos_keys, 1, 0).astype(jnp.bfloat16)
    behind_band = contract(behind_onehot, pos_queries, 1, 0).astype(jnp.bfloat16)
    query_term = skew_in(contract(query_rows, ahead_band, 1, 1), key_rows.shape[0])
    key_term = skew_in(contract(key_rows, behind_band, 1, 1), query_rows.shape[0]).T
    return score_scale * (content + query_term + key_term)


def query_side(
    query_rows,
    key_rows,
    value_rows,
    grad_rows,
    pos_keys,
    pos_queries,
    same_doc,
    tables,
    score_scale,
):
    tile_rows = query_rows.shape[0]
    tile_count = key_rows.shape[0] // tile_rows
    pieces = []
    for tile in range(tile_count):
        key_tile = key_rows[tile * tile_rows : (tile + 1) * tile_rows]
        pieces.append(
            tile_scores(
                query_rows,
                key_tile,
                pos_keys,
                pos_queries,
                tables[tile][2],
                tables[tile][3],
                score_scale,
            )
        )
    scores = jnp.where(same_doc, jnp.concatenate(pieces, 1), masked_score)
    row_max = jnp.max(scores, axis=1, keepdims=True)
    expd = jnp.where(same_doc, jnp.exp(scores - row_max), 0.0)
    row_sum = jnp.sum(expd, axis=1, keepdims=True)
    probs = expd / row_sum
    dprobs = contract(grad_rows, value_rows, 1, 1)
    row_dot = jnp.sum(probs * dprobs, axis=1, keepdims=True)
    dscores = probs * (dprobs - row_dot)
    dscores_low = dscores.astype(jnp.bfloat16)
    ahead_grad = jnp.zeros((tile_rows, pos_keys.shape[0]), jnp.float32)
    for tile in range(tile_count):
        band = dscores_low[:, tile * tile_rows : (tile + 1) * tile_rows]
        ahead_grad = ahead_grad + contract(skew_out(band), tables[tile][2], 1, 0)
    ahead_low = ahead_grad.astype(jnp.bfloat16)
    query_grad = score_scale * (
        contract(dscores_low, key_rows, 1, 0) + contract(ahead_low, pos_keys, 1, 0)
    )
    bucket_key = score_scale * contract(ahead_low, query_rows, 0, 0)
    probs_low = probs.astype(jnp.bfloat16)
    behind_parts = []
    for tile in range(tile_count):
        band = dscores_low[:, tile * tile_rows : (tile + 1) * tile_rows]
        behind_parts.append(contract(skew_out(band.T), tables[tile][3], 1, 0).astype(jnp.bfloat16))
    behind_low = jnp.concatenate(behind_parts, 0)
    key_grad = score_scale * (
        contract(dscores_low, query_rows, 0, 0) + contract(behind_low, pos_queries, 1, 0)
    )
    value_grad = contract(probs_low, grad_rows, 0, 0)
    bucket_query = score_scale * contract(behind_low, key_rows, 0, 0)
    return (query_grad, key_grad, value_grad, bucket_key, bucket_query)


def split_heads(matrix):
    return matrix.reshape(matrix.shape[0], matrix.shape[1] // HD, HD).transpose(1, 0, 2)


def join_heads(stacked):
    return stacked.transpose(1, 0, 2).reshape(stacked.shape[1], stacked.shape[0] * HD)


def body(queries, keys, values, out_grad, rel_emb, w_query, w_key, doc_lengths, bucket_table):
    tokens_dev = queries.shape[0]
    seq_count = lax.axis_size("seq")
    neighbours = min(SPAN, seq_count // 4)
    extent = tokens_dev * seq_count
    seq_index = lax.axis_index("seq")
    first_token = seq_index * tokens_dev
    score_scale = 1.0 / math.sqrt(3.0 * HD)
    pos_key = jnp.dot(rel_emb, w_key, preferred_element_type=jnp.float32).astype(jnp.bfloat16)
    pos_query = jnp.dot(rel_emb, w_query, preferred_element_type=jnp.float32).astype(jnp.bfloat16)
    doc_ends = jnp.cumsum(doc_lengths)
    buckets = rel_emb.shape[0]
    tables = [
        tile_tables(bucket_table, (neighbours - tile) * tokens_dev, tokens_dev, buckets)
        for tile in range(2 * neighbours + 1)
    ]
    hop_list = list(range(neighbours, 0, -1)) + list(range(-1, -neighbours - 1, -1))
    fetched = []
    for distance in hop_list:
        fetched.append(shifted((keys, values), "seq", distance))
    lower_side = fetched[:neighbours]
    upper_side = fetched[neighbours:]
    key_window = jnp.concatenate(
        [pair[0] for pair in lower_side] + [keys] + [pair[0] for pair in upper_side], 0
    )
    value_window = jnp.concatenate(
        [pair[1] for pair in lower_side] + [values] + [pair[1] for pair in upper_side], 0
    )
    window = key_window.shape[0]
    query_pos = first_token + jnp.arange(tokens_dev, dtype=jnp.int32)
    window_pos = first_token - neighbours * tokens_dev + jnp.arange(window, dtype=jnp.int32)
    same_doc = same_document(query_pos, window_pos, doc_ends, extent)
    query_heads = split_heads(queries)
    grad_heads = split_heads(out_grad)
    pos_key_heads = split_heads(pos_key)
    pos_query_heads = split_heads(pos_query)

    def every_pair(operands):
        query_rows, key_rows, value_rows, grad_rows, pos_keys, pos_queries = operands
        return query_side(
            query_rows,
            key_rows,
            value_rows,
            grad_rows,
            pos_keys,
            pos_queries,
            same_doc,
            tables,
            score_scale,
        )

    query_grad, key_part, value_part, bucket_key, bucket_query = lax.map(
        every_pair,
        (
            query_heads,
            split_heads(key_window),
            split_heads(value_window),
            grad_heads,
            pos_key_heads,
            pos_query_heads,
        ),
    )
    key_flat = join_heads(key_part)
    value_flat = join_heads(value_part)
    key_total = key_flat[neighbours * tokens_dev : (neighbours + 1) * tokens_dev]
    value_total = value_flat[neighbours * tokens_dev : (neighbours + 1) * tokens_dev]
    for distance in hop_list:
        segment = neighbours - distance
        returned = (
            key_flat[segment * tokens_dev : (segment + 1) * tokens_dev],
            value_flat[segment * tokens_dev : (segment + 1) * tokens_dev],
        )
        arrived = shifted((returned[0], returned[1]), "seq", -distance)
        key_total = key_total + arrived[0]
        value_total = value_total + arrived[1]
    key_grad = key_total.astype(jnp.bfloat16)
    value_grad = value_total.astype(jnp.bfloat16)
    query_out = join_heads(query_grad).astype(jnp.bfloat16)
    summed = lax.psum((join_heads(bucket_key), join_heads(bucket_query)), "seq")
    bucket_key_low = summed[0].astype(jnp.bfloat16)
    bucket_query_low = summed[1].astype(jnp.bfloat16)
    rows_dev = rel_emb.shape[1] // seq_count
    rel_columns = lax.dynamic_slice_in_dim(rel_emb, seq_index * rows_dev, rows_dev, 1)
    w_key_grad = contract(rel_columns, bucket_key_low, 0, 0)
    w_query_grad = contract(rel_columns, bucket_query_low, 0, 0)
    rel_partial = contract(bucket_key_low, w_key, 1, 1) + contract(bucket_query_low, w_query, 1, 1)
    rel_emb_grad = lax.psum_scatter(
        rel_partial.astype(jnp.bfloat16), "head", scatter_dimension=1, tiled=True
    ).astype(jnp.float32)
    return (query_out, key_grad, value_grad, rel_emb_grad, w_query_grad, w_key_grad)


def nn(left, right):
    return contract(left, right, 1, 0)


def nt(left, right):
    return contract(left, right, 1, 1)


def grid_of(shape):
    return (
        lax.broadcasted_iota(jnp.int32, shape, 0),
        lax.broadcasted_iota(jnp.int32, shape, 1),
    )


def pack_kernel(q_ref, g_ref, k_ref, v_ref, out_ref):
    for head in range(out_ref.shape[0] // 2):
        cols = slice(head * HD, (head + 1) * HD)
        piece = jnp.concatenate(
            [q_ref[:, cols], g_ref[:, cols], k_ref[:, cols], v_ref[:, cols]], 1
        )
        out_ref[2 * head] = piece
        out_ref[2 * head + 1] = piece


def head_kernel(
    lens_ref, half_ref, all_ref, pos_ref, table_ref, rel_ref, out_ref,
    onehot, pk, pq, acc, acc_pos, g_key, g_query, k_t, k_rev, s_q, st, dp, dtile, dq_nat, dq_pos,
):
    tiles = all_ref.shape[0]
    halo = table_ref.shape[1] // 2 // TILE
    span = 2 * halo + 1
    scale = 1.0 / math.sqrt(3.0 * HD)
    valid0 = (halo + 1) * TILE
    valid = table_ref.shape[1]
    buckets = pos_ref.shape[0]
    half = half_ref[0]
    row, col = grid_of((TILE, TILE))
    swap = jnp.where(row + col == TILE - 1, 1.0, 0.0).astype(BF)
    wrap = row + col >= TILE - 1
    wrap_rev = col >= row
    low = col < HD

    for part in range(buckets // TILE):
        ids = lax.broadcasted_iota(jnp.int32, (TILE, valid), 0) + part * TILE
        onehot[pl.ds(part * TILE, TILE), :] = jnp.where(ids == table_ref[...], 1.0, 0.0).astype(BF)
    pos_t = pos_ref[...].astype(F32).T.astype(BF)
    expanded = nn(pos_t, onehot[...]).astype(BF)
    pk[...] = jnp.zeros_like(pk)
    pq[...] = jnp.zeros_like(pq)
    pk[0:HD, valid0 : valid0 + valid] = expanded[:HD]
    pq[0:HD, valid0 : valid0 + valid] = expanded[HD:]
    acc[...] = jnp.zeros_like(acc)
    acc_pos[...] = jnp.zeros_like(acc_pos)
    g_key[...] = jnp.zeros_like(g_key)
    g_query[...] = jnp.zeros_like(g_query)

    def transpose_tile(tile, carry):
        turned = all_ref[tile, :, 2 * HD : 4 * HD].astype(F32).T.astype(BF)
        k_t[tile] = turned
        k_rev[tile] = nn(turned[:HD], swap).astype(BF)
        return carry

    lax.fori_loop(0, tiles, transpose_tile, 0)

    def block(b, carry):
        own = 2 * b + half
        first = jnp.clip(own - halo, 0, tiles - span)
        delta = (own - first) * TILE
        qd = all_ref[own, :, 0 : 2 * HD]
        turned = qd.astype(F32).T
        upper = row < HD
        right = jnp.concatenate(
            [jnp.where(upper, turned, 0.0), jnp.where(upper, 0.0, turned)], 1
        ).astype(BF)
        q_rev = nn(turned[:HD].astype(BF), swap).astype(BF)

        position = own * TILE + lax.broadcasted_iota(jnp.int32, (1, TILE), 1)

        def next_doc(d, state):
            end, start, stop = state
            end = end + lens_ref[d]
            start = jnp.where(end <= position, end, start)
            stop = jnp.where((end > position) & (stop < 0), end, stop)
            return (end, start, stop)

        _, start, stop = lax.fori_loop(
            0,
            lens_ref.shape[0],
            next_doc,
            (jnp.int32(0), jnp.zeros((1, TILE), jnp.int32), jnp.full((1, TILE), -1, jnp.int32)),
        )
        start = start - first * TILE
        stop = stop - first * TILE

        key_x = pl.multiple_of(halo * 2 * TILE - delta, TILE)
        s_q[...] = nn(qd, pk[:, pl.ds(key_x, (span + 1) * TILE)])
        best = jnp.full((8, TILE), masked_score, F32)
        for t in range(span):
            kv = all_ref[first + t, :, 2 * HD : 4 * HD]
            both = nn(kv, right)
            query_x = pl.multiple_of(2 * halo * TILE + delta - t * TILE, TILE)
            s_k = nn(kv, pq[:, pl.ds(query_x, 2 * TILE)])
            key_term = pltpu.roll(
                jnp.where(wrap, s_k[:, :TILE], s_k[:, TILE:]), 1, 1, stride=1, stride_axis=0
            )
            query_term = pltpu.roll(
                jnp.where(
                    wrap,
                    s_q[:, t * TILE : (t + 1) * TILE],
                    s_q[:, (t + 1) * TILE : (t + 2) * TILE],
                ),
                1,
                1,
                stride=1,
                stride_axis=0,
            )
            score = both[:, :TILE] + key_term + query_term.T
            place = row + t * TILE
            score = jnp.where((place >= start) & (place < stop), score, masked_score)
            st[t] = score
            dp[t] = both[:, TILE:]
            best = jnp.maximum(best, jnp.max(score.reshape(TILE // 8, 8, TILE), 0))
        top = jnp.max(best, 0, keepdims=True)
        total = jnp.zeros((8, TILE), F32)
        dot = jnp.zeros((8, TILE), F32)
        for t in range(span):
            expd = jnp.exp((st[t] - top) * scale)
            st[t] = expd
            total = total + jnp.sum(expd.reshape(TILE // 8, 8, TILE), 0)
            dot = dot + jnp.sum((expd * dp[t]).reshape(TILE // 8, 8, TILE), 0)
        inverse = 1.0 / jnp.sum(total, 0, keepdims=True)
        row_dot = jnp.sum(dot, 0, keepdims=True) * inverse

        lows = jnp.where(low, qd, jnp.zeros_like(qd))
        pair = jnp.concatenate([lows, jnp.where(low, jnp.zeros_like(qd), qd)], 0)
        dq_t = jnp.zeros((HD, TILE), F32)
        before = jnp.zeros((TILE, TILE), F32)
        for t in range(span):
            prob = st[t] * inverse
            dscore = (prob * (dp[t] - row_dot)).astype(BF)
            query_x = pl.multiple_of(2 * halo * TILE + delta - t * TILE, TILE)
            lhs = jnp.concatenate([dscore, prob.astype(BF)], 1)
            acc[first + t] += nn(lhs, pair)
            stacked = nn(jnp.concatenate([k_t[first + t][:HD], swap], 0), dscore)
            dq_t = dq_t + stacked[:HD]
            y = pltpu.roll(stacked[HD:], 0, 1, stride=1, stride_axis=0)
            spread = jnp.concatenate(
                [jnp.where(wrap_rev, y, 0.0), jnp.where(wrap_rev, 0.0, y)], 1
            ).astype(BF)
            acc_pos[first + t] += nt(spread, pq[0:HD, pl.ds(query_x, 2 * TILE)])
            g_query[:, pl.ds(query_x, 2 * TILE)] += nn(k_rev[first + t], spread)
            z = pltpu.roll(nt(swap, dscore), 0, 1, stride=1, stride_axis=0)
            dtile[:, t * TILE : (t + 1) * TILE] = jnp.where(wrap_rev, z, before).astype(BF)
            before = z
        dtile[:, span * TILE :] = jnp.where(wrap_rev, 0.0, before).astype(BF)
        spread_q = dtile[...]
        window = pl.ds(key_x, (span + 1) * TILE)
        g_key[:, window] += nn(q_rev, spread_q)
        back = nt(spread_q, pk[0:HD, window])
        high = back.astype(BF)
        dq_pos[b] = jnp.concatenate([high, (back - high.astype(F32)).astype(BF)], 1)
        dq_nat[b] = dq_t
        return carry

    lax.fori_loop(0, tiles // 2, block, 0)

    parts = []
    for g in (g_key, g_query):
        band = g[:, valid0 : valid0 + valid]
        high = band.astype(BF)
        parts += [high, (band - high.astype(F32)).astype(BF)]
    summed = nt(jnp.concatenate(parts, 0), onehot[...])
    bucket_t = scale * jnp.concatenate(
        [summed[:HD] + summed[HD : 2 * HD], summed[2 * HD : 3 * HD] + summed[3 * HD :]], 0
    )
    bucket_low = bucket_t.astype(BF)
    weight_t = nn(bucket_low, rel_ref[...])
    w_rows = rel_ref.shape[1] // tiles
    b_rows = buckets // tiles
    weight = weight_t.T.astype(BF)
    bucket = bucket_t.T.astype(BF)
    base_w = TILE + TILE // 2
    base_b = base_w + w_rows
    for tile in range(tiles):
        out_ref[tile, base_w:base_b, :] = weight[tile * w_rows : (tile + 1) * w_rows]
        out_ref[tile, base_b : base_b + b_rows, :] = bucket[tile * b_rows : (tile + 1) * b_rows]
    factor = jnp.where(low, scale, 1.0)

    def finish_keys(tile, carry):
        back = acc_pos[tile]
        high = back.astype(BF)
        both = nn(swap, jnp.concatenate([high, (back - high.astype(F32)).astype(BF)], 1))
        extra = both[:, :HD] + both[:, HD:]
        extra = jnp.concatenate([extra, jnp.zeros_like(extra)], 1)
        out_ref[tile, 0:TILE, :] = ((acc[tile] + extra) * factor).astype(BF)
        return carry

    lax.fori_loop(0, tiles, finish_keys, 0)

    def finish_queries(b, carry):
        both = nn(swap, dq_pos[b])
        extra = both[:, :HD] + both[:, HD:]
        grad = scale * (dq_nat[b].T + extra)
        piece = jnp.concatenate([grad[: TILE // 2], grad[TILE // 2 :]], 1).astype(BF)
        out_ref[2 * b, TILE:base_w, :] = piece
        out_ref[2 * b + 1, TILE:base_w, :] = piece
        return carry

    lax.fori_loop(0, tiles // 2, finish_queries, 0)


def unpack_kernel(
    half_ref, got_ref, wk_ref, wq_ref, dq_ref, dk_ref, dv_ref, dwq_ref, dwk_ref, rel_ref,
):
    heads = got_ref.shape[0] // 2
    w_rows = dwk_ref.shape[0]
    base_w = TILE + TILE // 2
    base_b = base_w + w_rows
    half = half_ref[0]
    keys_low, queries_low = [], []
    for g in range(heads // 2):
        cols = slice(2 * g * HD, 2 * (g + 1) * HD)
        sums, weights, grads = [], [], []
        for head in (2 * g, 2 * g + 1):
            two = got_ref[2 * head, 0:TILE, :].astype(F32) + got_ref[2 * head + 1, 0:TILE, :].astype(F32)
            sums.append(two.astype(BF))
            rest = got_ref[2 * head, base_w:, :].astype(F32) + got_ref[2 * head + 1, base_w:, :].astype(F32)
            weights.append(rest)
            piece = got_ref[2 * head + half, TILE:base_w, :]
            grads.append(jnp.concatenate([piece[:, :HD], piece[:, HD:]], 0))
        dq_ref[:, cols] = jnp.concatenate(grads, 1)
        dk_ref[:, cols] = jnp.concatenate([part[:, :HD] for part in sums], 1)
        dv_ref[:, cols] = jnp.concatenate([part[:, HD:] for part in sums], 1)
        dwk_ref[:, cols] = jnp.concatenate([part[:w_rows, :HD] for part in weights], 1)
        dwq_ref[:, cols] = jnp.concatenate([part[:w_rows, HD:] for part in weights], 1)
        keys_low += [part[w_rows:, :HD].astype(BF) for part in weights]
        queries_low += [part[w_rows:, HD:].astype(BF) for part in weights]
    rel = nt(jnp.concatenate(keys_low, 1), wk_ref[...]) + nt(
        jnp.concatenate(queries_low, 1), wq_ref[...]
    )
    rel_ref[...] = rel.astype(BF)


def whole_call(kernel, inputs, outputs, scratch=(), scalars=0, limit=48):
    vmem = pl.BlockSpec(memory_space=pltpu.VMEM)
    smem = pl.BlockSpec(memory_space=pltpu.SMEM)
    return pl.pallas_call(
        kernel,
        out_shape=outputs,
        in_specs=[smem] * scalars + [vmem] * (len(inputs) - scalars),
        out_specs=jax.tree.map(lambda _: vmem, outputs),
        scratch_shapes=list(scratch),
        compiler_params=pltpu.CompilerParams(vmem_limit_bytes=limit << 20),
    )(*inputs)


def head_body(queries, keys, values, out_grad, rel_emb, w_query, w_key, doc_lengths, bucket_table):
    tokens_dev, width = queries.shape
    heads = width // HD
    seq_count = lax.axis_size("seq")
    seq_index = lax.axis_index("seq")
    buckets, depth = rel_emb.shape
    halo = bucket_table.shape[0] // 2 // TILE
    span = 2 * halo + 1
    mine = seq_index // 2
    half = lax.rem(seq_index, 2).astype(jnp.int32).reshape(1)
    shape = jax.ShapeDtypeStruct
    packed = whole_call(
        pack_kernel,
        (queries, out_grad, keys, values),
        shape((seq_count, tokens_dev, 4 * HD), BF),
    )
    arrived = lax.all_to_all(packed, "seq", 0, 0, tiled=True)
    w_own = jnp.concatenate(
        [
            lax.dynamic_slice_in_dim(w_key, mine * HD, HD, 1),
            lax.dynamic_slice_in_dim(w_query, mine * HD, HD, 1),
        ],
        1,
    )
    pos = nn(rel_emb, w_own).astype(BF)
    table = jnp.flip(bucket_table).reshape(1, -1)
    w_rows, b_rows = depth // seq_count, buckets // seq_count
    rows = TILE + TILE // 2 + w_rows + b_rows
    line = (2 * span - 1 + 1) * TILE
    vm = pltpu.VMEM
    results = whole_call(
        head_kernel,
        (doc_lengths, half, arrived, pos, table, rel_emb),
        shape((seq_count, rows, 2 * HD), BF),
        [
            vm((buckets, table.shape[1]), BF),
            vm((2 * HD, line), BF),
            vm((2 * HD, line), BF),
            vm((seq_count, TILE, 2 * HD), F32),
            vm((seq_count, TILE, HD), F32),
            vm((HD, line), F32),
            vm((HD, line), F32),
            vm((seq_count, 2 * HD, TILE), BF),
            vm((seq_count, HD, TILE), BF),
            vm((TILE, (span + 1) * TILE), F32),
            vm((span, TILE, TILE), F32),
            vm((span, TILE, TILE), F32),
            vm((TILE, (span + 1) * TILE), BF),
            vm((seq_count // 2, HD, TILE), F32),
            vm((seq_count // 2, TILE, 2 * HD), BF),
        ],
        scalars=2,
    )
    returned = lax.all_to_all(results, "seq", 0, 0, tiled=True)
    tokens = shape((tokens_dev, width), BF)
    weights = shape((w_rows, width), F32)
    query_grad, key_grad, value_grad, w_query_grad, w_key_grad, rel_rows = whole_call(
        unpack_kernel,
        (half, returned, w_key, w_query),
        [tokens, tokens, tokens, weights, weights, shape((b_rows, depth), BF)],
        scalars=1,
    )
    head_index = lax.axis_index("head")
    kept = lax.dynamic_slice_in_dim(rel_rows, head_index * width, width, 1)
    other = lax.dynamic_slice_in_dim(rel_rows, (1 - head_index) * width, width, 1)
    other = lax.ppermute(other, "head", [(0, 1), (1, 0)])
    rel_own = (kept.astype(F32) + other.astype(F32)).astype(BF)
    rel_emb_grad = lax.all_gather(rel_own, "seq", axis=0, tiled=True).astype(F32)
    return (query_grad, key_grad, value_grad, rel_emb_grad, w_query_grad, w_key_grad)


def fits_heads(mesh, queries, rel_emb, bucket_table):
    seq, head = mesh.shape["seq"], mesh.shape["head"]
    heads = queries.shape[1] // HD // head
    return (
        head == 2
        and seq == 2 * heads
        and heads % 2 == 0
        and queries.shape[0] == seq * TILE
        and bucket_table.shape[0] % (2 * TILE) == 0
        and seq >= bucket_table.shape[0] // TILE + 1
        and rel_emb.shape[0] % (16 * seq) == 0
        and rel_emb.shape[1] % (16 * seq) == 0
        and rel_emb.shape[0] % TILE == 0
    )


def solution(mesh):
    in_specs = (
        P("seq", "head"),
        P("seq", "head"),
        P("seq", "head"),
        P("seq", "head"),
        P(),
        P(None, "head"),
        P(None, "head"),
        P(),
        P(),
    )
    out_specs = (
        P("seq", "head"),
        P("seq", "head"),
        P("seq", "head"),
        P(None, "head"),
        P("seq", "head"),
        P("seq", "head"),
    )

    def run(queries, keys, values, out_grad, rel_emb, w_query, w_key, doc_lengths, bucket_table):
        chosen = head_body if fits_heads(mesh, queries, rel_emb, bucket_table) else body
        return jax.shard_map(
            chosen, mesh=mesh, in_specs=in_specs, out_specs=out_specs, check_vma=False
        )(queries, keys, values, out_grad, rel_emb, w_query, w_key, doc_lengths, bucket_table)

    return run
```

```python
import math

import jax
import jax.numpy as jnp
from jax import lax
from jax.experimental import pallas as pl
from jax.experimental.pallas import tpu as pltpu
from jax.sharding import PartitionSpec as P

HD = 64
SPAN = 4
TILE = 128
SPANS = (3, 5, 7)
BF = jnp.bfloat16
F32 = jnp.float32


masked_score = -1e30


def shifted(block, axis, distance):
    devices = range(lax.axis_size(axis))
    route = [(i - distance, i) for i in devices if i - distance in devices]
    return lax.ppermute(block, axis, route)


def contract(left, right, left_dim, right_dim):
    return lax.dot_general(
        left, right, (((left_dim,), (right_dim,)), ((), ())), preferred_element_type=jnp.float32
    )


def doc_index(position, doc_ends, extent):
    inside = (position >= 0) & (position < extent)
    owner = jnp.sum((doc_ends[None, :] <= position[:, None]).astype(jnp.int32), axis=1)
    return jnp.where(inside, owner, -1)


def same_document(row_pos, col_pos, doc_ends, extent):
    return (
        doc_index(row_pos, doc_ends, extent)[:, None]
        == doc_index(col_pos, doc_ends, extent)[None, :]
    )


def tile_tables(bucket_table, shift, rows, buckets):
    offset_span = bucket_table.shape[0] // 2
    spread = jnp.arange(2 * rows - 1, dtype=jnp.int32) - (rows - 1)
    ahead_index = bucket_table[jnp.clip(shift - spread + offset_span, 0, 2 * offset_span - 1)]
    behind_index = bucket_table[jnp.clip(offset_span - shift - spread, 0, 2 * offset_span - 1)]
    bucket_ids = jnp.arange(buckets, dtype=jnp.int32)[None, :]
    ahead_onehot = (ahead_index[:, None] == bucket_ids).astype(jnp.bfloat16)
    behind_onehot = (behind_index[:, None] == bucket_ids).astype(jnp.bfloat16)
    return (ahead_index, behind_index, ahead_onehot, behind_onehot)


def skew_in(spread, width):
    rows = spread.shape[0]
    line = rows + width - 1
    flat = jnp.pad(spread, ((0, 0), (0, 1))).reshape(-1)
    return flat[rows - 1 : rows - 1 + rows * line].reshape(rows, line)[:, :width]


def skew_out(dense):
    rows, width = dense.shape
    line = rows + width - 1
    padded = jnp.pad(dense, ((0, 0), (0, rows - 1))).reshape(-1)
    flat = jnp.pad(padded, (rows - 1, 1))
    return flat.reshape(rows, line + 1)[:, :line]


def tile_scores(
    query_rows, key_rows, pos_keys, pos_queries, ahead_onehot, behind_onehot, score_scale
):
    content = contract(query_rows, key_rows, 1, 1)
    ahead_band = contract(ahead_onehot, pos_keys, 1, 0).astype(jnp.bfloat16)
    behind_band = contract(behind_onehot, pos_queries, 1, 0).astype(jnp.bfloat16)
    query_term = skew_in(contract(query_rows, ahead_band, 1, 1), key_rows.shape[0])
    key_term = skew_in(contract(key_rows, behind_band, 1, 1), query_rows.shape[0]).T
    return score_scale * (content + query_term + key_term)


def query_side(
    query_rows,
    key_rows,
    value_rows,
    grad_rows,
    pos_keys,
    pos_queries,
    same_doc,
    tables,
    score_scale,
):
    tile_rows = query_rows.shape[0]
    tile_count = key_rows.shape[0] // tile_rows
    pieces = []
    for tile in range(tile_count):
        key_tile = key_rows[tile * tile_rows : (tile + 1) * tile_rows]
        pieces.append(
            tile_scores(
                query_rows,
                key_tile,
                pos_keys,
                pos_queries,
                tables[tile][2],
                tables[tile][3],
                score_scale,
            )
        )
    scores = jnp.where(same_doc, jnp.concatenate(pieces, 1), masked_score)
    row_max = jnp.max(scores, axis=1, keepdims=True)
    expd = jnp.where(same_doc, jnp.exp(scores - row_max), 0.0)
    row_sum = jnp.sum(expd, axis=1, keepdims=True)
    probs = expd / row_sum
    dprobs = contract(grad_rows, value_rows, 1, 1)
    row_dot = jnp.sum(probs * dprobs, axis=1, keepdims=True)
    dscores = probs * (dprobs - row_dot)
    dscores_low = dscores.astype(jnp.bfloat16)
    ahead_grad = jnp.zeros((tile_rows, pos_keys.shape[0]), jnp.float32)
    for tile in range(tile_count):
        band = dscores_low[:, tile * tile_rows : (tile + 1) * tile_rows]
        ahead_grad = ahead_grad + contract(skew_out(band), tables[tile][2], 1, 0)
    ahead_low = ahead_grad.astype(jnp.bfloat16)
    query_grad = score_scale * (
        contract(dscores_low, key_rows, 1, 0) + contract(ahead_low, pos_keys, 1, 0)
    )
    bucket_key = score_scale * contract(ahead_low, query_rows, 0, 0)
    probs_low = probs.astype(jnp.bfloat16)
    behind_parts = []
    for tile in range(tile_count):
        band = dscores_low[:, tile * tile_rows : (tile + 1) * tile_rows]
        behind_parts.append(contract(skew_out(band.T), tables[tile][3], 1, 0).astype(jnp.bfloat16))
    behind_low = jnp.concatenate(behind_parts, 0)
    key_grad = score_scale * (
        contract(dscores_low, query_rows, 0, 0) + contract(behind_low, pos_queries, 1, 0)
    )
    value_grad = contract(probs_low, grad_rows, 0, 0)
    bucket_query = score_scale * contract(behind_low, key_rows, 0, 0)
    return (query_grad, key_grad, value_grad, bucket_key, bucket_query)


def split_heads(matrix):
    return matrix.reshape(matrix.shape[0], matrix.shape[1] // HD, HD).transpose(1, 0, 2)


def join_heads(stacked):
    return stacked.transpose(1, 0, 2).reshape(stacked.shape[1], stacked.shape[0] * HD)


def body(queries, keys, values, out_grad, rel_emb, w_query, w_key, doc_lengths, bucket_table):
    tokens_dev = queries.shape[0]
    seq_count = lax.axis_size("seq")
    neighbours = min(SPAN, seq_count // 4)
    extent = tokens_dev * seq_count
    seq_index = lax.axis_index("seq")
    first_token = seq_index * tokens_dev
    score_scale = 1.0 / math.sqrt(3.0 * HD)
    pos_key = jnp.dot(rel_emb, w_key, preferred_element_type=jnp.float32).astype(jnp.bfloat16)
    pos_query = jnp.dot(rel_emb, w_query, preferred_element_type=jnp.float32).astype(jnp.bfloat16)
    doc_ends = jnp.cumsum(doc_lengths)
    buckets = rel_emb.shape[0]
    tables = [
        tile_tables(bucket_table, (neighbours - tile) * tokens_dev, tokens_dev, buckets)
        for tile in range(2 * neighbours + 1)
    ]
    hop_list = list(range(neighbours, 0, -1)) + list(range(-1, -neighbours - 1, -1))
    fetched = []
    for distance in hop_list:
        fetched.append(shifted((keys, values), "seq", distance))
    lower_side = fetched[:neighbours]
    upper_side = fetched[neighbours:]
    key_window = jnp.concatenate(
        [pair[0] for pair in lower_side] + [keys] + [pair[0] for pair in upper_side], 0
    )
    value_window = jnp.concatenate(
        [pair[1] for pair in lower_side] + [values] + [pair[1] for pair in upper_side], 0
    )
    window = key_window.shape[0]
    query_pos = first_token + jnp.arange(tokens_dev, dtype=jnp.int32)
    window_pos = first_token - neighbours * tokens_dev + jnp.arange(window, dtype=jnp.int32)
    same_doc = same_document(query_pos, window_pos, doc_ends, extent)
    query_heads = split_heads(queries)
    grad_heads = split_heads(out_grad)
    pos_key_heads = split_heads(pos_key)
    pos_query_heads = split_heads(pos_query)

    def every_pair(operands):
        query_rows, key_rows, value_rows, grad_rows, pos_keys, pos_queries = operands
        return query_side(
            query_rows,
            key_rows,
            value_rows,
            grad_rows,
            pos_keys,
            pos_queries,
            same_doc,
            tables,
            score_scale,
        )

    query_grad, key_part, value_part, bucket_key, bucket_query = lax.map(
        every_pair,
        (
            query_heads,
            split_heads(key_window),
            split_heads(value_window),
            grad_heads,
            pos_key_heads,
            pos_query_heads,
        ),
    )
    key_flat = join_heads(key_part)
    value_flat = join_heads(value_part)
    key_total = key_flat[neighbours * tokens_dev : (neighbours + 1) * tokens_dev]
    value_total = value_flat[neighbours * tokens_dev : (neighbours + 1) * tokens_dev]
    for distance in hop_list:
        segment = neighbours - distance
        returned = (
            key_flat[segment * tokens_dev : (segment + 1) * tokens_dev],
            value_flat[segment * tokens_dev : (segment + 1) * tokens_dev],
        )
        arrived = shifted((returned[0], returned[1]), "seq", -distance)
        key_total = key_total + arrived[0]
        value_total = value_total + arrived[1]
    key_grad = key_total.astype(jnp.bfloat16)
    value_grad = value_total.astype(jnp.bfloat16)
    query_out = join_heads(query_grad).astype(jnp.bfloat16)
    summed = lax.psum((join_heads(bucket_key), join_heads(bucket_query)), "seq")
    bucket_key_low = summed[0].astype(jnp.bfloat16)
    bucket_query_low = summed[1].astype(jnp.bfloat16)
    rows_dev = rel_emb.shape[1] // seq_count
    rel_columns = lax.dynamic_slice_in_dim(rel_emb, seq_index * rows_dev, rows_dev, 1)
    w_key_grad = contract(rel_columns, bucket_key_low, 0, 0)
    w_query_grad = contract(rel_columns, bucket_query_low, 0, 0)
    rel_partial = contract(bucket_key_low, w_key, 1, 1) + contract(bucket_query_low, w_query, 1, 1)
    rel_emb_grad = lax.psum_scatter(
        rel_partial.astype(jnp.bfloat16), "head", scatter_dimension=1, tiled=True
    ).astype(jnp.float32)
    return (query_out, key_grad, value_grad, rel_emb_grad, w_query_grad, w_key_grad)


def nn(left, right):
    return contract(left, right, 1, 0)


def nt(left, right):
    return contract(left, right, 1, 1)


def grid_of(shape):
    return (
        lax.broadcasted_iota(jnp.int32, shape, 0),
        lax.broadcasted_iota(jnp.int32, shape, 1),
    )


def pack_kernel(q_ref, g_ref, k_ref, v_ref, out_ref):
    for head in range(out_ref.shape[0]):
        cols = slice(head * HD, (head + 1) * HD)
        out_ref[head] = jnp.concatenate(
            [q_ref[:, cols], g_ref[:, cols], k_ref[:, cols], v_ref[:, cols]], 1
        )


def table_kernel(pos_ref, table_ref, onehot, pk, pq):
    buckets, valid = onehot.shape
    valid0 = valid // 2 + TILE
    for part in range(buckets // TILE):
        ids = lax.broadcasted_iota(jnp.int32, (TILE, valid), 0) + part * TILE
        onehot[pl.ds(part * TILE, TILE), :] = jnp.where(ids == table_ref[...], 1.0, 0.0).astype(BF)
    pos_t = pos_ref[...].astype(F32).T.astype(BF)
    expanded = nn(pos_t, onehot[...]).astype(BF)
    pk[...] = jnp.zeros_like(pk)
    pq[...] = jnp.zeros_like(pq)
    pk[0:HD, valid0 : valid0 + valid] = expanded[:HD]
    pq[0:HD, valid0 : valid0 + valid] = expanded[HD:]


def head_kernel(
    lens_ref, half_ref, own_ref, other_ref, onehot, pk, pq,
    send_ref, keep_ref, bucket_ref, query_ref,
    kvs, acc, acc_pos, g_key, g_query, k_t, k_rev, s_q, st, dp, dtile, dq_nat, dq_pos,
):
    blocks = own_ref.shape[0]
    tiles = 2 * blocks
    buckets, valid = onehot.shape
    halo = valid // 2 // TILE
    longest = 2 * halo + 1
    scale = 1.0 / math.sqrt(3.0 * HD)
    valid0 = (halo + 1) * TILE
    half = half_ref[0]
    row, col = grid_of((TILE, TILE))
    swap = jnp.where(row + col == TILE - 1, 1.0, 0.0).astype(BF)
    wrap = row + col >= TILE - 1
    wrap_rev = col >= row
    low = col < HD
    acc[...] = jnp.zeros_like(acc)
    acc_pos[...] = jnp.zeros_like(acc_pos)
    g_key[...] = jnp.zeros_like(g_key)
    g_query[...] = jnp.zeros_like(g_query)

    def transpose_tile(b, carry):
        for ref, tile in ((own_ref, 2 * b + half), (other_ref, 2 * b + 1 - half)):
            kv = ref[b, :, 2 * HD : 4 * HD]
            kvs[tile] = kv
            turned = kv.astype(F32).T.astype(BF)
            k_t[tile] = turned[:HD]
            k_rev[tile] = nn(turned[:HD], swap).astype(BF)
        return carry

    lax.fori_loop(0, blocks, transpose_tile, 0)

    def block(b, carry):
        own = 2 * b + half
        token = own * TILE

        def next_end(d, state):
            end, start, stop = state
            stop = jnp.where(end < token + TILE, end + lens_ref[d], stop)
            end = end + lens_ref[d]
            start = jnp.where(end <= token, end, start)
            return (end, start, stop)

        zero = jnp.int32(0)
        _, reach_low, reach_high = lax.fori_loop(
            0, lens_ref.shape[0], next_end, (zero, zero, zero)
        )
        lowest = reach_low // TILE
        count = (reach_high + TILE - 1) // TILE - lowest
        shorter = 0
        for span in SPANS:
            if span < longest:
                pl.when((count > shorter) & (count <= span))(
                    lambda span=span: work(b, own, lowest, span)
                )
                shorter = span
        pl.when(count > shorter)(lambda: work(b, own, lowest, longest))
        return carry

    def work(b, own, lowest, span):
        first = jnp.clip(lowest, 0, tiles - span)
        delta = (own - first) * TILE
        qd = own_ref[b, :, 0 : 2 * HD]
        turned = qd.astype(F32).T
        upper = row < HD
        right = jnp.concatenate(
            [jnp.where(upper, turned, 0.0), jnp.where(upper, 0.0, turned)], 1
        ).astype(BF)
        q_rev = nn(turned[:HD].astype(BF), swap).astype(BF)

        position = own * TILE + lax.broadcasted_iota(jnp.int32, (1, TILE), 1)

        def next_doc(d, state):
            end, start, stop = state
            stop = jnp.where(end <= position, end + lens_ref[d], stop)
            end = end + lens_ref[d]
            start = jnp.where(end <= position, end, start)
            return (end, start, stop)

        nothing = jnp.zeros((1, TILE), jnp.int32)
        _, start, stop = lax.fori_loop(
            0, lens_ref.shape[0], next_doc, (jnp.int32(0), nothing, nothing)
        )
        start = start - first * TILE
        stop = stop - first * TILE

        key_x = pl.multiple_of(halo * 2 * TILE - delta, TILE)
        s_q[:, 0 : (span + 1) * TILE] = nn(qd, pk[:, pl.ds(key_x, (span + 1) * TILE)])
        best = jnp.full((8, TILE), masked_score, F32)
        for t in range(span):
            kv = kvs[first + t]
            both = nn(kv, right)
            query_x = pl.multiple_of(2 * halo * TILE + delta - t * TILE, TILE)
            s_k = nn(kv, pq[:, pl.ds(query_x, 2 * TILE)])
            key_term = pltpu.roll(
                jnp.where(wrap, s_k[:, :TILE], s_k[:, TILE:]), 1, 1, stride=1, stride_axis=0
            )
            query_term = pltpu.roll(
                jnp.where(
                    wrap,
                    s_q[:, t * TILE : (t + 1) * TILE],
                    s_q[:, (t + 1) * TILE : (t + 2) * TILE],
                ),
                1,
                1,
                stride=1,
                stride_axis=0,
            )
            score = both[:, :TILE] + key_term + query_term.T
            place = row + t * TILE
            score = jnp.where((place >= start) & (place < stop), score, masked_score)
            st[t] = score
            dp[t] = both[:, TILE:]
            best = jnp.maximum(best, jnp.max(score.reshape(TILE // 8, 8, TILE), 0))
        top = jnp.max(best, 0, keepdims=True)
        total = jnp.zeros((8, TILE), F32)
        dot = jnp.zeros((8, TILE), F32)
        for t in range(span):
            expd = jnp.exp((st[t] - top) * scale)
            st[t] = expd
            total = total + jnp.sum(expd.reshape(TILE // 8, 8, TILE), 0)
            dot = dot + jnp.sum((expd * dp[t]).reshape(TILE // 8, 8, TILE), 0)
        inverse = 1.0 / jnp.sum(total, 0, keepdims=True)
        row_dot = jnp.sum(dot, 0, keepdims=True) * inverse

        lows = jnp.where(low, qd, jnp.zeros_like(qd))
        pair = jnp.concatenate([lows, jnp.where(low, jnp.zeros_like(qd), qd)], 0)
        dq_t = jnp.zeros((HD, TILE), F32)
        before = jnp.zeros((TILE, TILE), F32)
        for t in range(span):
            prob = st[t] * inverse
            dscore = (prob * (dp[t] - row_dot)).astype(BF)
            query_x = pl.multiple_of(2 * halo * TILE + delta - t * TILE, TILE)
            lhs = jnp.concatenate([dscore, prob.astype(BF)], 1)
            acc[first + t] += nn(lhs, pair)
            stacked = nn(jnp.concatenate([k_t[first + t], swap], 0), dscore)
            dq_t = dq_t + stacked[:HD]
            y = pltpu.roll(stacked[HD:], 0, 1, stride=1, stride_axis=0)
            spread = jnp.concatenate(
                [jnp.where(wrap_rev, y, 0.0), jnp.where(wrap_rev, 0.0, y)], 1
            ).astype(BF)
            acc_pos[first + t] += nt(spread, pq[0:HD, pl.ds(query_x, 2 * TILE)])
            g_query[:, pl.ds(query_x, 2 * TILE)] += nn(k_rev[first + t], spread)
            z = pltpu.roll(nt(swap, dscore), 0, 1, stride=1, stride_axis=0)
            dtile[:, t * TILE : (t + 1) * TILE] = jnp.where(wrap_rev, z, before).astype(BF)
            before = z
        dtile[:, span * TILE : (span + 1) * TILE] = jnp.where(wrap_rev, 0.0, before).astype(BF)
        spread_q = dtile[:, 0 : (span + 1) * TILE]
        window = pl.ds(key_x, (span + 1) * TILE)
        g_key[:, window] += nn(q_rev, spread_q)
        back = nt(spread_q, pk[0:HD, window])
        high = back.astype(BF)
        dq_pos[b] = jnp.concatenate([high, (back - high.astype(F32)).astype(BF)], 1)
        dq_nat[b] = dq_t

    lax.fori_loop(0, blocks, block, 0)

    parts = []
    for g in (g_key, g_query):
        band = g[:, valid0 : valid0 + valid]
        high = band.astype(BF)
        parts += [high, (band - high.astype(F32)).astype(BF)]
    summed = nt(jnp.concatenate(parts, 0), onehot[...])
    bucket_t = scale * jnp.concatenate(
        [summed[:HD] + summed[HD : 2 * HD], summed[2 * HD : 3 * HD] + summed[3 * HD :]], 0
    )
    bucket = bucket_t.T.astype(BF)
    bucket_ref[...] = bucket
    send_ref[blocks * TILE :, :] = bucket
    factor = jnp.where(low, scale, 1.0)

    def gradients(tile):
        back = acc_pos[tile]
        high = back.astype(BF)
        both = nn(swap, jnp.concatenate([high, (back - high.astype(F32)).astype(BF)], 1))
        extra = both[:, :HD] + both[:, HD:]
        extra = jnp.concatenate([extra, jnp.zeros_like(extra)], 1)
        return (acc[tile] + extra) * factor

    def finish(b, carry):
        keep_ref[b] = gradients(2 * b + half)
        send_ref[pl.ds(b * TILE, TILE), :] = gradients(2 * b + 1 - half).astype(BF)
        both = nn(swap, dq_pos[b])
        extra = both[:, :HD] + both[:, HD:]
        grad = scale * (dq_nat[b].T + extra)
        query_ref[b] = jnp.concatenate([grad[: TILE // 2], grad[TILE // 2 :]], 1).astype(BF)
        return carry

    lax.fori_loop(0, blocks, finish, 0)


def join_kernel(half_ref, keep_ref, bucket_ref, query_ref, came_ref, rel_ref, out_ref, weight, bucket):
    blocks = keep_ref.shape[0]
    tiles = 2 * blocks
    half = half_ref[0]
    w_rows = weight.shape[0] // tiles
    b_rows = bucket.shape[0] // tiles
    base_w = TILE + TILE // 2
    base_b = base_w + w_rows
    total = bucket_ref[...].astype(F32) + came_ref[blocks * TILE :, :].astype(F32)
    bucket[...] = total
    weight[...] = nn(total.T.astype(BF), rel_ref[...]).T
    for b in range(blocks):
        came = came_ref[b * TILE : (b + 1) * TILE, :].astype(F32)
        tile = 2 * b + half
        out_ref[b, 0:TILE, :] = (keep_ref[b] + came).astype(BF)
        out_ref[b, TILE:base_w, :] = query_ref[b]
        out_ref[b, base_w:base_b, :] = weight[pl.ds(tile * w_rows, w_rows), :].astype(BF)
        out_ref[b, base_b:, :] = bucket[pl.ds(tile * b_rows, b_rows), :].astype(BF)


def unpack_kernel(
    got_ref, wk_ref, wq_ref, dq_ref, dk_ref, dv_ref, dwq_ref, dwk_ref, rel_ref,
):
    w_rows = dwk_ref.shape[0]
    base_w = TILE + TILE // 2
    base_b = base_w + w_rows
    keys_low, queries_low = [], []
    for g in range(got_ref.shape[0] // 2):
        cols = slice(2 * g * HD, 2 * (g + 1) * HD)
        two = [got_ref[2 * g], got_ref[2 * g + 1]]
        dq_ref[:, cols] = jnp.concatenate(
            [
                jnp.concatenate([one[TILE:base_w, :HD], one[TILE:base_w, HD:]], 0)
                for one in two
            ],
            1,
        )
        dk_ref[:, cols] = jnp.concatenate([one[:TILE, :HD] for one in two], 1)
        dv_ref[:, cols] = jnp.concatenate([one[:TILE, HD:] for one in two], 1)
        dwk_ref[:, cols] = jnp.concatenate([one[base_w:base_b, :HD] for one in two], 1).astype(F32)
        dwq_ref[:, cols] = jnp.concatenate([one[base_w:base_b, HD:] for one in two], 1).astype(F32)
        keys_low += [one[base_b:, :HD] for one in two]
        queries_low += [one[base_b:, HD:] for one in two]
    rel = nt(jnp.concatenate(keys_low, 1), wk_ref[...]) + nt(
        jnp.concatenate(queries_low, 1), wq_ref[...]
    )
    rel_ref[...] = rel.astype(BF)


def whole_call(kernel, inputs, outputs, scratch=(), scalars=0, limit=48):
    vmem = pl.BlockSpec(memory_space=pltpu.VMEM)
    smem = pl.BlockSpec(memory_space=pltpu.SMEM)
    return pl.pallas_call(
        kernel,
        out_shape=outputs,
        in_specs=[smem] * scalars + [vmem] * (len(inputs) - scalars),
        out_specs=jax.tree.map(lambda _: vmem, outputs),
        scratch_shapes=list(scratch),
        compiler_params=pltpu.CompilerParams(vmem_limit_bytes=limit << 20),
    )(*inputs)


def staged_call(kernel, inputs, outputs):
    def spec(array):
        return pl.BlockSpec(array.shape, lambda step: (0,) * len(array.shape))

    return pl.pallas_call(
        kernel,
        grid=(1,),
        out_shape=outputs,
        in_specs=[spec(array) for array in inputs],
        out_specs=jax.tree.map(spec, outputs),
        compiler_params=pltpu.CompilerParams(vmem_limit_bytes=32 << 20),
    )(*inputs)


def head_body(queries, keys, values, out_grad, rel_emb, w_query, w_key, doc_lengths, bucket_table):
    tokens_dev, width = queries.shape
    heads = width // HD
    seq_count = lax.axis_size("seq")
    seq_index = lax.axis_index("seq")
    buckets, depth = rel_emb.shape
    halo = bucket_table.shape[0] // 2 // TILE
    span = 2 * halo + 1
    mine = seq_index // 2
    half = lax.rem(seq_index, 2).astype(jnp.int32).reshape(1)
    halves = [list(range(0, seq_count, 2)), list(range(1, seq_count, 2))]
    partners = [(i, i ^ 1) for i in range(seq_count)]
    shape = jax.ShapeDtypeStruct
    vm = pltpu.VMEM

    def spread(pieces):
        return lax.all_to_all(pieces, "seq", 0, 0, axis_index_groups=halves, tiled=True)

    packed = staged_call(
        pack_kernel,
        (queries, out_grad, keys, values),
        shape((heads, tokens_dev, 4 * HD), BF),
    )
    own = spread(packed)
    other = lax.ppermute(own, "seq", partners)
    w_own = jnp.concatenate(
        [
            lax.dynamic_slice_in_dim(w_key, mine * HD, HD, 1),
            lax.dynamic_slice_in_dim(w_query, mine * HD, HD, 1),
        ],
        1,
    )
    pos = nn(rel_emb, w_own).astype(BF)
    table = jnp.flip(bucket_table).reshape(1, -1)
    w_rows, b_rows = depth // seq_count, buckets // seq_count
    rows = TILE + TILE // 2 + w_rows + b_rows
    line = 2 * span * TILE
    tables = whole_call(
        table_kernel,
        (pos, table),
        [
            shape((buckets, table.shape[1]), BF),
            shape((2 * HD, line), BF),
            shape((2 * HD, line), BF),
        ],
    )
    sent, kept, bucket, query = whole_call(
        head_kernel,
        (doc_lengths, half, own, other, *tables),
        [
            shape((heads * TILE + buckets, 2 * HD), BF),
            shape((heads, TILE, 2 * HD), F32),
            shape((buckets, 2 * HD), BF),
            shape((heads, TILE // 2, 2 * HD), BF),
        ],
        [
            vm((seq_count, TILE, 2 * HD), BF),
            vm((seq_count, TILE, 2 * HD), F32),
            vm((seq_count, TILE, HD), F32),
            vm((HD, line), F32),
            vm((HD, line), F32),
            vm((seq_count, HD, TILE), BF),
            vm((seq_count, HD, TILE), BF),
            vm((TILE, (span + 1) * TILE), F32),
            vm((span, TILE, TILE), F32),
            vm((span, TILE, TILE), F32),
            vm((TILE, (span + 1) * TILE), BF),
            vm((heads, HD, TILE), F32),
            vm((heads, TILE, 2 * HD), BF),
        ],
        scalars=2,
    )
    came = lax.ppermute(sent, "seq", partners)
    joined = whole_call(
        join_kernel,
        (half, kept, bucket, query, came, rel_emb),
        shape((heads, rows, 2 * HD), BF),
        [vm((depth, 2 * HD), F32), vm((buckets, 2 * HD), F32)],
        scalars=1,
    )
    returned = spread(joined)
    tokens = shape((tokens_dev, width), BF)
    weights = shape((w_rows, width), F32)
    query_grad, key_grad, value_grad, w_query_grad, w_key_grad, rel_rows = whole_call(
        unpack_kernel,
        (returned, w_key, w_query),
        [tokens, tokens, tokens, weights, weights, shape((b_rows, depth), BF)],
    )
    head_index = lax.axis_index("head")
    mine_rel = lax.dynamic_slice_in_dim(rel_rows, head_index * width, width, 1)
    far_rel = lax.dynamic_slice_in_dim(rel_rows, (1 - head_index) * width, width, 1)
    far_rel = lax.ppermute(far_rel, "head", [(0, 1), (1, 0)])
    rel_own = (mine_rel.astype(F32) + far_rel.astype(F32)).astype(BF)
    near = spread(jnp.broadcast_to(rel_own[None], (heads, b_rows, width)))
    far = lax.ppermute(near, "seq", partners)
    even = jnp.where(half[0] == 0, near, far)
    odd = jnp.where(half[0] == 0, far, near)
    rel_emb_grad = jnp.stack([even, odd], 1).reshape(buckets, width).astype(F32)
    return (query_grad, key_grad, value_grad, rel_emb_grad, w_query_grad, w_key_grad)


def fits_heads(mesh, queries, rel_emb, bucket_table):
    seq, head = mesh.shape["seq"], mesh.shape["head"]
    heads = queries.shape[1] // HD // head
    return (
        head == 2
        and seq == 2 * heads
        and heads % 2 == 0
        and queries.shape[0] == seq * TILE
        and bucket_table.shape[0] % (2 * TILE) == 0
        and seq >= bucket_table.shape[0] // TILE + 1
        and rel_emb.shape[0] % (16 * seq) == 0
        and rel_emb.shape[1] % (16 * seq) == 0
        and rel_emb.shape[0] % TILE == 0
    )


def solution(mesh):
    in_specs = (
        P("seq", "head"),
        P("seq", "head"),
        P("seq", "head"),
        P("seq", "head"),
        P(),
        P(None, "head"),
        P(None, "head"),
        P(),
        P(),
    )
    out_specs = (
        P("seq", "head"),
        P("seq", "head"),
        P("seq", "head"),
        P(None, "head"),
        P("seq", "head"),
        P("seq", "head"),
    )

    def run(queries, keys, values, out_grad, rel_emb, w_query, w_key, doc_lengths, bucket_table):
        chosen = head_body if fits_heads(mesh, queries, rel_emb, bucket_table) else body
        return jax.shard_map(
            chosen, mesh=mesh, in_specs=in_specs, out_specs=out_specs, check_vma=False
        )(queries, keys, values, out_grad, rel_emb, w_query, w_key, doc_lengths, bucket_table)

    return run
```

```python
import math

import jax
import jax.numpy as jnp
from jax import lax
from jax.experimental import pallas as pl
from jax.experimental.pallas import tpu as pltpu
from jax.sharding import PartitionSpec as P

HD = 64
SPAN = 4
TILE = 128
SPANS = (2, 3, 4, 5, 6, 7)
BF = jnp.bfloat16
F32 = jnp.float32


masked_score = -1e30


def shifted(block, axis, distance):
    devices = range(lax.axis_size(axis))
    route = [(i - distance, i) for i in devices if i - distance in devices]
    return lax.ppermute(block, axis, route)


def contract(left, right, left_dim, right_dim):
    return lax.dot_general(
        left, right, (((left_dim,), (right_dim,)), ((), ())), preferred_element_type=jnp.float32
    )


def doc_index(position, doc_ends, extent):
    inside = (position >= 0) & (position < extent)
    owner = jnp.sum((doc_ends[None, :] <= position[:, None]).astype(jnp.int32), axis=1)
    return jnp.where(inside, owner, -1)


def same_document(row_pos, col_pos, doc_ends, extent):
    return (
        doc_index(row_pos, doc_ends, extent)[:, None]
        == doc_index(col_pos, doc_ends, extent)[None, :]
    )


def tile_tables(bucket_table, shift, rows, buckets):
    offset_span = bucket_table.shape[0] // 2
    spread = jnp.arange(2 * rows - 1, dtype=jnp.int32) - (rows - 1)
    ahead_index = bucket_table[jnp.clip(shift - spread + offset_span, 0, 2 * offset_span - 1)]
    behind_index = bucket_table[jnp.clip(offset_span - shift - spread, 0, 2 * offset_span - 1)]
    bucket_ids = jnp.arange(buckets, dtype=jnp.int32)[None, :]
    ahead_onehot = (ahead_index[:, None] == bucket_ids).astype(jnp.bfloat16)
    behind_onehot = (behind_index[:, None] == bucket_ids).astype(jnp.bfloat16)
    return (ahead_index, behind_index, ahead_onehot, behind_onehot)


def skew_in(spread, width):
    rows = spread.shape[0]
    line = rows + width - 1
    flat = jnp.pad(spread, ((0, 0), (0, 1))).reshape(-1)
    return flat[rows - 1 : rows - 1 + rows * line].reshape(rows, line)[:, :width]


def skew_out(dense):
    rows, width = dense.shape
    line = rows + width - 1
    padded = jnp.pad(dense, ((0, 0), (0, rows - 1))).reshape(-1)
    flat = jnp.pad(padded, (rows - 1, 1))
    return flat.reshape(rows, line + 1)[:, :line]


def tile_scores(
    query_rows, key_rows, pos_keys, pos_queries, ahead_onehot, behind_onehot, score_scale
):
    content = contract(query_rows, key_rows, 1, 1)
    ahead_band = contract(ahead_onehot, pos_keys, 1, 0).astype(jnp.bfloat16)
    behind_band = contract(behind_onehot, pos_queries, 1, 0).astype(jnp.bfloat16)
    query_term = skew_in(contract(query_rows, ahead_band, 1, 1), key_rows.shape[0])
    key_term = skew_in(contract(key_rows, behind_band, 1, 1), query_rows.shape[0]).T
    return score_scale * (content + query_term + key_term)


def query_side(
    query_rows,
    key_rows,
    value_rows,
    grad_rows,
    pos_keys,
    pos_queries,
    same_doc,
    tables,
    score_scale,
):
    tile_rows = query_rows.shape[0]
    tile_count = key_rows.shape[0] // tile_rows
    pieces = []
    for tile in range(tile_count):
        key_tile = key_rows[tile * tile_rows : (tile + 1) * tile_rows]
        pieces.append(
            tile_scores(
                query_rows,
                key_tile,
                pos_keys,
                pos_queries,
                tables[tile][2],
                tables[tile][3],
                score_scale,
            )
        )
    scores = jnp.where(same_doc, jnp.concatenate(pieces, 1), masked_score)
    row_max = jnp.max(scores, axis=1, keepdims=True)
    expd = jnp.where(same_doc, jnp.exp(scores - row_max), 0.0)
    row_sum = jnp.sum(expd, axis=1, keepdims=True)
    probs = expd / row_sum
    dprobs = contract(grad_rows, value_rows, 1, 1)
    row_dot = jnp.sum(probs * dprobs, axis=1, keepdims=True)
    dscores = probs * (dprobs - row_dot)
    dscores_low = dscores.astype(jnp.bfloat16)
    ahead_grad = jnp.zeros((tile_rows, pos_keys.shape[0]), jnp.float32)
    for tile in range(tile_count):
        band = dscores_low[:, tile * tile_rows : (tile + 1) * tile_rows]
        ahead_grad = ahead_grad + contract(skew_out(band), tables[tile][2], 1, 0)
    ahead_low = ahead_grad.astype(jnp.bfloat16)
    query_grad = score_scale * (
        contract(dscores_low, key_rows, 1, 0) + contract(ahead_low, pos_keys, 1, 0)
    )
    bucket_key = score_scale * contract(ahead_low, query_rows, 0, 0)
    probs_low = probs.astype(jnp.bfloat16)
    behind_parts = []
    for tile in range(tile_count):
        band = dscores_low[:, tile * tile_rows : (tile + 1) * tile_rows]
        behind_parts.append(contract(skew_out(band.T), tables[tile][3], 1, 0).astype(jnp.bfloat16))
    behind_low = jnp.concatenate(behind_parts, 0)
    key_grad = score_scale * (
        contract(dscores_low, query_rows, 0, 0) + contract(behind_low, pos_queries, 1, 0)
    )
    value_grad = contract(probs_low, grad_rows, 0, 0)
    bucket_query = score_scale * contract(behind_low, key_rows, 0, 0)
    return (query_grad, key_grad, value_grad, bucket_key, bucket_query)


def split_heads(matrix):
    return matrix.reshape(matrix.shape[0], matrix.shape[1] // HD, HD).transpose(1, 0, 2)


def join_heads(stacked):
    return stacked.transpose(1, 0, 2).reshape(stacked.shape[1], stacked.shape[0] * HD)


def body(queries, keys, values, out_grad, rel_emb, w_query, w_key, doc_lengths, bucket_table):
    tokens_dev = queries.shape[0]
    seq_count = lax.axis_size("seq")
    neighbours = min(SPAN, seq_count // 4)
    extent = tokens_dev * seq_count
    seq_index = lax.axis_index("seq")
    first_token = seq_index * tokens_dev
    score_scale = 1.0 / math.sqrt(3.0 * HD)
    pos_key = jnp.dot(rel_emb, w_key, preferred_element_type=jnp.float32).astype(jnp.bfloat16)
    pos_query = jnp.dot(rel_emb, w_query, preferred_element_type=jnp.float32).astype(jnp.bfloat16)
    doc_ends = jnp.cumsum(doc_lengths)
    buckets = rel_emb.shape[0]
    tables = [
        tile_tables(bucket_table, (neighbours - tile) * tokens_dev, tokens_dev, buckets)
        for tile in range(2 * neighbours + 1)
    ]
    hop_list = list(range(neighbours, 0, -1)) + list(range(-1, -neighbours - 1, -1))
    fetched = []
    for distance in hop_list:
        fetched.append(shifted((keys, values), "seq", distance))
    lower_side = fetched[:neighbours]
    upper_side = fetched[neighbours:]
    key_window = jnp.concatenate(
        [pair[0] for pair in lower_side] + [keys] + [pair[0] for pair in upper_side], 0
    )
    value_window = jnp.concatenate(
        [pair[1] for pair in lower_side] + [values] + [pair[1] for pair in upper_side], 0
    )
    window = key_window.shape[0]
    query_pos = first_token + jnp.arange(tokens_dev, dtype=jnp.int32)
    window_pos = first_token - neighbours * tokens_dev + jnp.arange(window, dtype=jnp.int32)
    same_doc = same_document(query_pos, window_pos, doc_ends, extent)
    query_heads = split_heads(queries)
    grad_heads = split_heads(out_grad)
    pos_key_heads = split_heads(pos_key)
    pos_query_heads = split_heads(pos_query)

    def every_pair(operands):
        query_rows, key_rows, value_rows, grad_rows, pos_keys, pos_queries = operands
        return query_side(
            query_rows,
            key_rows,
            value_rows,
            grad_rows,
            pos_keys,
            pos_queries,
            same_doc,
            tables,
            score_scale,
        )

    query_grad, key_part, value_part, bucket_key, bucket_query = lax.map(
        every_pair,
        (
            query_heads,
            split_heads(key_window),
            split_heads(value_window),
            grad_heads,
            pos_key_heads,
            pos_query_heads,
        ),
    )
    key_flat = join_heads(key_part)
    value_flat = join_heads(value_part)
    key_total = key_flat[neighbours * tokens_dev : (neighbours + 1) * tokens_dev]
    value_total = value_flat[neighbours * tokens_dev : (neighbours + 1) * tokens_dev]
    for distance in hop_list:
        segment = neighbours - distance
        returned = (
            key_flat[segment * tokens_dev : (segment + 1) * tokens_dev],
            value_flat[segment * tokens_dev : (segment + 1) * tokens_dev],
        )
        arrived = shifted((returned[0], returned[1]), "seq", -distance)
        key_total = key_total + arrived[0]
        value_total = value_total + arrived[1]
    key_grad = key_total.astype(jnp.bfloat16)
    value_grad = value_total.astype(jnp.bfloat16)
    query_out = join_heads(query_grad).astype(jnp.bfloat16)
    summed = lax.psum((join_heads(bucket_key), join_heads(bucket_query)), "seq")
    bucket_key_low = summed[0].astype(jnp.bfloat16)
    bucket_query_low = summed[1].astype(jnp.bfloat16)
    rows_dev = rel_emb.shape[1] // seq_count
    rel_columns = lax.dynamic_slice_in_dim(rel_emb, seq_index * rows_dev, rows_dev, 1)
    w_key_grad = contract(rel_columns, bucket_key_low, 0, 0)
    w_query_grad = contract(rel_columns, bucket_query_low, 0, 0)
    rel_partial = contract(bucket_key_low, w_key, 1, 1) + contract(bucket_query_low, w_query, 1, 1)
    rel_emb_grad = lax.psum_scatter(
        rel_partial.astype(jnp.bfloat16), "head", scatter_dimension=1, tiled=True
    ).astype(jnp.float32)
    return (query_out, key_grad, value_grad, rel_emb_grad, w_query_grad, w_key_grad)


def nn(left, right):
    return contract(left, right, 1, 0)


def nt(left, right):
    return contract(left, right, 1, 1)


def grid_of(shape):
    return (
        lax.broadcasted_iota(jnp.int32, shape, 0),
        lax.broadcasted_iota(jnp.int32, shape, 1),
    )


def pack_kernel(q_ref, g_ref, k_ref, v_ref, out_ref, held, pieces, came, left):
    loads = [
        pltpu.make_async_copy(ref, held.at[i], came.at[i])
        for i, ref in enumerate((q_ref, g_ref, k_ref, v_ref))
    ]
    for load in loads:
        load.start()
    for load in loads:
        load.wait()
    stores = []
    for head in range(out_ref.shape[0]):
        cols = slice(head * HD, (head + 1) * HD)
        pieces[head] = jnp.concatenate([held[i, :, cols] for i in range(4)], 1)
        stores.append(pltpu.make_async_copy(pieces.at[head], out_ref.at[head], left.at[head]))
        stores[-1].start()
    for store in stores:
        store.wait()


def table_kernel(pos_ref, table_ref, onehot, pk, pq, both):
    buckets, valid = onehot.shape
    valid0 = valid // 2 + TILE
    for part in range(buckets // TILE):
        ids = lax.broadcasted_iota(jnp.int32, (TILE, valid), 0) + part * TILE
        onehot[pl.ds(part * TILE, TILE), :] = jnp.where(ids == table_ref[...], 1.0, 0.0).astype(BF)
    pos_t = pos_ref[...].astype(F32).T.astype(BF)
    expanded = nn(pos_t, onehot[...]).astype(BF)
    pk[...] = jnp.zeros_like(pk)
    pq[...] = jnp.zeros_like(pq)
    pk[0:HD, valid0 : valid0 + valid] = expanded[:HD]
    pq[0:HD, valid0 : valid0 + valid] = expanded[HD:]
    both[...] = jnp.zeros_like(both)
    both[valid0 : valid0 + valid, :] = expanded.astype(F32).T.astype(BF)


def head_kernel(
    lens_ref, half_ref, own_ref, other_ref, onehot, pk, pq, rows_ref,
    send_ref, keep_ref, bucket_ref, query_ref,
    kvs, acc, acc_pos, g_key, g_query, k_t, k_rev, s_q, st, dp, dtile, pairs, dq_nat, dq_pos,
):
    blocks = own_ref.shape[0]
    tiles = 2 * blocks
    buckets, valid = onehot.shape
    halo = valid // 2 // TILE
    longest = 2 * halo + 1
    scale = 1.0 / math.sqrt(3.0 * HD)
    valid0 = (halo + 1) * TILE
    half = half_ref[0]
    row, col = grid_of((TILE, TILE))
    swap = jnp.where(row + col == TILE - 1, 1.0, 0.0).astype(BF)
    wrap = row + col >= TILE - 1
    wrap_rev = col >= row
    low = col < HD
    acc[...] = jnp.zeros_like(acc)
    acc_pos[...] = jnp.zeros_like(acc_pos)
    g_key[...] = jnp.zeros_like(g_key)
    g_query[...] = jnp.zeros_like(g_query)

    def transpose_tile(b, carry):
        for ref, tile in ((own_ref, 2 * b + half), (other_ref, 2 * b + 1 - half)):
            kv = ref[b, :, 2 * HD : 4 * HD]
            kvs[tile] = kv
            turned = kv.astype(F32).T.astype(BF)
            k_t[tile] = turned[:HD]
            k_rev[tile] = nn(turned[:HD], swap).astype(BF)
        return carry

    lax.fori_loop(0, blocks, transpose_tile, 0)

    def block(b, carry):
        own = 2 * b + half
        token = own * TILE

        def next_end(d, state):
            end, start, stop = state
            stop = jnp.where(end < token + TILE, end + lens_ref[d], stop)
            end = end + lens_ref[d]
            start = jnp.where(end <= token, end, start)
            return (end, start, stop)

        zero = jnp.int32(0)
        _, reach_low, reach_high = lax.fori_loop(
            0, lens_ref.shape[0], next_end, (zero, zero, zero)
        )
        lowest = reach_low // TILE
        count = (reach_high + TILE - 1) // TILE - lowest
        shorter = 0
        for span in SPANS:
            if span < longest:
                pl.when((count > shorter) & (count <= span))(
                    lambda span=span: work(b, own, lowest, span)
                )
                shorter = span
        pl.when(count > shorter)(lambda: work(b, own, lowest, longest))
        return carry

    def work(b, own, lowest, span):
        first = jnp.clip(lowest, 0, tiles - span)
        delta = (own - first) * TILE
        qd = own_ref[b, :, 0 : 2 * HD]
        turned = qd.astype(F32).T
        upper = row < HD
        right = jnp.concatenate(
            [jnp.where(upper, turned, 0.0), jnp.where(upper, 0.0, turned)], 1
        ).astype(BF)
        q_rev = nn(turned[:HD].astype(BF), swap).astype(BF)

        position = own * TILE + lax.broadcasted_iota(jnp.int32, (1, TILE), 1)

        def next_doc(d, state):
            end, start, stop = state
            stop = jnp.where(end <= position, end + lens_ref[d], stop)
            end = end + lens_ref[d]
            start = jnp.where(end <= position, end, start)
            return (end, start, stop)

        nothing = jnp.zeros((1, TILE), jnp.int32)
        _, start, stop = lax.fori_loop(
            0, lens_ref.shape[0], next_doc, (jnp.int32(0), nothing, nothing)
        )
        start = start - first * TILE
        stop = stop - first * TILE

        key_x = pl.multiple_of(halo * 2 * TILE - delta, TILE)
        s_q[:, 0 : (span + 1) * TILE] = nn(qd, pk[:, pl.ds(key_x, (span + 1) * TILE)])
        best = jnp.full((8, TILE), masked_score, F32)
        window_kv = kvs[pl.ds(first, span)].reshape(span * TILE, 2 * HD)
        contents = nn(window_kv, right)
        for t in range(span):
            kv = window_kv[t * TILE : (t + 1) * TILE]
            both = contents[t * TILE : (t + 1) * TILE]
            query_x = pl.multiple_of(2 * halo * TILE + delta - t * TILE, TILE)
            s_k = nn(kv, pq[:, pl.ds(query_x, 2 * TILE)])
            key_term = pltpu.roll(
                jnp.where(wrap, s_k[:, :TILE], s_k[:, TILE:]), 1, 1, stride=1, stride_axis=0
            )
            query_term = pltpu.roll(
                jnp.where(
                    wrap,
                    s_q[:, t * TILE : (t + 1) * TILE],
                    s_q[:, (t + 1) * TILE : (t + 2) * TILE],
                ),
                1,
                1,
                stride=1,
                stride_axis=0,
            )
            score = both[:, :TILE] + key_term + query_term.T
            place = row + t * TILE
            score = jnp.where((place >= start) & (place < stop), score, masked_score)
            st[t] = score
            dp[t] = both[:, TILE:]
            best = jnp.maximum(best, jnp.max(score.reshape(TILE // 8, 8, TILE), 0))
        top = jnp.max(best, 0, keepdims=True)
        total = jnp.zeros((8, TILE), F32)
        dot = jnp.zeros((8, TILE), F32)
        for t in range(span):
            expd = jnp.exp((st[t] - top) * scale)
            st[t] = expd
            total = total + jnp.sum(expd.reshape(TILE // 8, 8, TILE), 0)
            dot = dot + jnp.sum((expd * dp[t]).reshape(TILE // 8, 8, TILE), 0)
        inverse = 1.0 / jnp.sum(total, 0, keepdims=True)
        row_dot = jnp.sum(dot, 0, keepdims=True) * inverse

        lows = jnp.where(low, qd, jnp.zeros_like(qd))
        pair = jnp.concatenate([lows, jnp.where(low, jnp.zeros_like(qd), qd)], 0)
        dq_t = jnp.zeros((HD, TILE), F32)
        before = jnp.zeros((TILE, TILE), F32)
        ahead_part = None
        for t in range(span):
            prob = st[t] * inverse
            dscore = (prob * (dp[t] - row_dot)).astype(BF)
            pairs[t] = jnp.concatenate([dscore, prob.astype(BF)], 1)
            stacked = nn(jnp.concatenate([k_t[first + t], swap], 0), dscore)
            dq_t = dq_t + stacked[:HD]
            query_x = pl.multiple_of(2 * halo * TILE + delta - t * TILE, TILE)
            y = pltpu.roll(stacked[HD:], 0, 1, stride=1, stride_axis=0)
            near = jnp.where(wrap_rev, y, 0.0).astype(BF)
            far = jnp.where(wrap_rev, 0.0, y).astype(BF)
            back = nn(jnp.concatenate([near, far], 1), rows_ref[pl.ds(query_x, 2 * TILE), :])
            acc_pos[first + t] += back[:, HD:]
            turned_keys = k_rev[first + t]
            chunk = pl.ds(query_x + TILE, TILE)
            if ahead_part is None:
                g_query[:, chunk] += nn(turned_keys, far)
            else:
                g_query[:, chunk] += nn(
                    jnp.concatenate([ahead_part[0], turned_keys], 1),
                    jnp.concatenate([ahead_part[1], far], 0),
                )
            ahead_part = (turned_keys, near)
            z = pltpu.roll(nt(swap, dscore), 0, 1, stride=1, stride_axis=0)
            dtile[:, t * TILE : (t + 1) * TILE] = jnp.where(wrap_rev, z, before).astype(BF)
            before = z
        g_query[:, pl.ds(query_x, TILE)] += nn(*ahead_part)
        acc[pl.ds(first, span)] += nn(
            pairs[0:span].reshape(span * TILE, 2 * TILE), pair
        ).reshape(span, TILE, 2 * HD)
        dtile[:, span * TILE : (span + 1) * TILE] = jnp.where(wrap_rev, 0.0, before).astype(BF)
        spread_q = dtile[:, 0 : (span + 1) * TILE]
        window = pl.ds(key_x, (span + 1) * TILE)
        g_key[:, window] += nn(q_rev, spread_q)
        back = nn(spread_q, rows_ref[window, :])[:, :HD]
        high = back.astype(BF)
        dq_pos[b] = jnp.concatenate([high, (back - high.astype(F32)).astype(BF)], 1)
        dq_nat[b] = dq_t

    lax.fori_loop(0, blocks, block, 0)

    parts = []
    for g in (g_key, g_query):
        band = g[:, valid0 : valid0 + valid]
        high = band.astype(BF)
        parts += [high, (band - high.astype(F32)).astype(BF)]
    summed = nt(jnp.concatenate(parts, 0), onehot[...])
    bucket_t = scale * jnp.concatenate(
        [summed[:HD] + summed[HD : 2 * HD], summed[2 * HD : 3 * HD] + summed[3 * HD :]], 0
    )
    bucket = bucket_t.T.astype(BF)
    bucket_ref[...] = bucket
    send_ref[blocks * TILE :, :] = bucket
    factor = jnp.where(low, scale, 1.0)

    def gradients(tile):
        back = acc_pos[tile]
        high = back.astype(BF)
        both = nn(swap, jnp.concatenate([high, (back - high.astype(F32)).astype(BF)], 1))
        extra = both[:, :HD] + both[:, HD:]
        extra = jnp.concatenate([extra, jnp.zeros_like(extra)], 1)
        return (acc[tile] + extra) * factor

    def finish(b, carry):
        keep_ref[b] = gradients(2 * b + half)
        send_ref[pl.ds(b * TILE, TILE), :] = gradients(2 * b + 1 - half).astype(BF)
        both = nn(swap, dq_pos[b])
        extra = both[:, :HD] + both[:, HD:]
        grad = scale * (dq_nat[b].T + extra)
        query_ref[b] = jnp.concatenate([grad[: TILE // 2], grad[TILE // 2 :]], 1).astype(BF)
        return carry

    lax.fori_loop(0, blocks, finish, 0)


def join_kernel(
    half_ref, keep_ref, bucket_ref, query_ref, came_ref, rel_ref, out_ref, rows_ref,
    weight, bucket, pieces, low_rows, sems,
):
    blocks = keep_ref.shape[0]
    tiles = 2 * blocks
    half = half_ref[0]
    w_rows = weight.shape[0] // tiles
    b_rows = bucket.shape[0] // tiles
    base_w = TILE + TILE // 2
    total = bucket_ref[...].astype(F32) + came_ref[blocks * TILE :, :].astype(F32)
    bucket[...] = total
    for b in range(blocks):
        tile = 2 * b + half
        low_rows[b] = bucket[pl.ds(tile * b_rows, b_rows), :].astype(BF)
    first = pltpu.make_async_copy(low_rows, rows_ref, sems.at[0])
    first.start()
    weight[...] = nn(total.T.astype(BF), rel_ref[...]).T
    for b in range(blocks):
        came = came_ref[b * TILE : (b + 1) * TILE, :].astype(F32)
        tile = 2 * b + half
        pieces[b, 0:TILE, :] = (keep_ref[b] + came).astype(BF)
        pieces[b, TILE:base_w, :] = query_ref[b]
        pieces[b, base_w:, :] = weight[pl.ds(tile * w_rows, w_rows), :].astype(BF)
    second = pltpu.make_async_copy(pieces, out_ref, sems.at[1])
    second.start()
    first.wait()
    second.wait()


def rel_kernel(got_ref, wk_ref, wq_ref, rel_ref):
    heads = range(got_ref.shape[0])
    rel = nt(jnp.concatenate([got_ref[h, :, :HD] for h in heads], 1), wk_ref[...]) + nt(
        jnp.concatenate([got_ref[h, :, HD:] for h in heads], 1), wq_ref[...]
    )
    rel_ref[...] = rel.astype(BF)


def unpack_kernel(got_ref, dq_ref, dk_ref, dv_ref, dwq_ref, dwk_ref):
    base_w = TILE + TILE // 2
    for g in range(got_ref.shape[0] // 2):
        cols = slice(2 * g * HD, 2 * (g + 1) * HD)
        two = [got_ref[2 * g], got_ref[2 * g + 1]]
        dq_ref[:, cols] = jnp.concatenate(
            [
                jnp.concatenate([one[TILE:base_w, :HD], one[TILE:base_w, HD:]], 0)
                for one in two
            ],
            1,
        )
        dk_ref[:, cols] = jnp.concatenate([one[:TILE, :HD] for one in two], 1)
        dv_ref[:, cols] = jnp.concatenate([one[:TILE, HD:] for one in two], 1)
        dwk_ref[:, cols] = jnp.concatenate([one[base_w:, :HD] for one in two], 1).astype(F32)
        dwq_ref[:, cols] = jnp.concatenate([one[base_w:, HD:] for one in two], 1).astype(F32)


VMEM = pl.BlockSpec(memory_space=pltpu.VMEM)
SMEM = pl.BlockSpec(memory_space=pltpu.SMEM)
HBM = pl.BlockSpec(memory_space=pltpu.HBM)


def whole_call(kernel, inputs, outputs, scratch=(), scalars=0, source=VMEM, target=VMEM, limit=48):
    return pl.pallas_call(
        kernel,
        out_shape=outputs,
        in_specs=[SMEM] * scalars + [source] * (len(inputs) - scalars),
        out_specs=jax.tree.map(lambda _: target, outputs),
        scratch_shapes=list(scratch),
        compiler_params=pltpu.CompilerParams(vmem_limit_bytes=limit << 20),
    )(*inputs)


def head_body(queries, keys, values, out_grad, rel_emb, w_query, w_key, doc_lengths, bucket_table):
    tokens_dev, width = queries.shape
    heads = width // HD
    seq_count = lax.axis_size("seq")
    seq_index = lax.axis_index("seq")
    buckets, depth = rel_emb.shape
    halo = bucket_table.shape[0] // 2 // TILE
    span = 2 * halo + 1
    mine = seq_index // 2
    half = lax.rem(seq_index, 2).astype(jnp.int32).reshape(1)
    halves = [list(range(0, seq_count, 2)), list(range(1, seq_count, 2))]
    partners = [(i, i ^ 1) for i in range(seq_count)]
    shape = jax.ShapeDtypeStruct
    vm = pltpu.VMEM

    def spread(pieces):
        return lax.all_to_all(pieces, "seq", 0, 0, axis_index_groups=halves, tiled=True)

    packed = whole_call(
        pack_kernel,
        (queries, out_grad, keys, values),
        shape((heads, tokens_dev, 4 * HD), BF),
        [
            vm((4, tokens_dev, width), BF),
            vm((heads, tokens_dev, 4 * HD), BF),
            pltpu.SemaphoreType.DMA((4,)),
            pltpu.SemaphoreType.DMA((heads,)),
        ],
        source=HBM,
        target=HBM,
        limit=64,
    )
    own = spread(packed)
    other = lax.ppermute(own, "seq", partners)
    w_own = jnp.concatenate(
        [
            lax.dynamic_slice_in_dim(w_key, mine * HD, HD, 1),
            lax.dynamic_slice_in_dim(w_query, mine * HD, HD, 1),
        ],
        1,
    )
    pos = nn(rel_emb, w_own).astype(BF)
    table = jnp.flip(bucket_table).reshape(1, -1)
    w_rows, b_rows = depth // seq_count, buckets // seq_count
    rows = TILE + TILE // 2 + w_rows
    line = 2 * span * TILE
    tables = whole_call(
        table_kernel,
        (pos, table),
        [
            shape((buckets, table.shape[1]), BF),
            shape((2 * HD, line), BF),
            shape((2 * HD, line), BF),
            shape((line, 2 * HD), BF),
        ],
    )
    sent, kept, bucket, query = whole_call(
        head_kernel,
        (doc_lengths, half, own, other, *tables),
        [
            shape((heads * TILE + buckets, 2 * HD), BF),
            shape((heads, TILE, 2 * HD), F32),
            shape((buckets, 2 * HD), BF),
            shape((heads, TILE // 2, 2 * HD), BF),
        ],
        [
            vm((seq_count, TILE, 2 * HD), BF),
            vm((seq_count, TILE, 2 * HD), F32),
            vm((seq_count, TILE, HD), F32),
            vm((HD, line), F32),
            vm((HD, line), F32),
            vm((seq_count, HD, TILE), BF),
            vm((seq_count, HD, TILE), BF),
            vm((TILE, (span + 1) * TILE), F32),
            vm((span, TILE, TILE), F32),
            vm((span, TILE, TILE), F32),
            vm((TILE, (span + 1) * TILE), BF),
            vm((span, TILE, 2 * TILE), BF),
            vm((heads, HD, TILE), F32),
            vm((heads, TILE, 2 * HD), BF),
        ],
        scalars=2,
    )
    came = lax.ppermute(sent, "seq", partners)
    joined, bucket_rows = whole_call(
        join_kernel,
        (half, kept, bucket, query, came, rel_emb),
        [shape((heads, rows, 2 * HD), BF), shape((heads, b_rows, 2 * HD), BF)],
        [
            vm((depth, 2 * HD), F32),
            vm((buckets, 2 * HD), F32),
            vm((heads, rows, 2 * HD), BF),
            vm((heads, b_rows, 2 * HD), BF),
            pltpu.SemaphoreType.DMA((2,)),
        ],
        scalars=1,
        target=HBM,
        limit=64,
    )
    rel_rows = whole_call(
        rel_kernel, (spread(bucket_rows), w_key, w_query), shape((b_rows, depth), BF)
    )
    returned = spread(joined)
    tokens = shape((tokens_dev, width), BF)
    weights = shape((w_rows, width), F32)
    head_index = lax.axis_index("head")
    mine_rel = lax.dynamic_slice_in_dim(rel_rows, head_index * width, width, 1)
    far_rel = lax.dynamic_slice_in_dim(rel_rows, (1 - head_index) * width, width, 1)
    far_rel = lax.ppermute(far_rel, "head", [(0, 1), (1, 0)])
    rel_own = (mine_rel.astype(F32) + far_rel.astype(F32)).astype(BF)
    near = spread(jnp.broadcast_to(rel_own[None], (heads, b_rows, width)))
    far = lax.ppermute(near, "seq", partners)
    even = jnp.where(half[0] == 0, near, far)
    odd = jnp.where(half[0] == 0, far, near)
    rel_emb_grad = jnp.stack([even, odd], 1).reshape(buckets, width).astype(F32)
    query_grad, key_grad, value_grad, w_query_grad, w_key_grad = whole_call(
        unpack_kernel, (returned,), [tokens, tokens, tokens, weights, weights]
    )
    return (query_grad, key_grad, value_grad, rel_emb_grad, w_query_grad, w_key_grad)


def fits_heads(mesh, queries, rel_emb, bucket_table):
    seq, head = mesh.shape["seq"], mesh.shape["head"]
    heads = queries.shape[1] // HD // head
    return (
        head == 2
        and seq == 2 * heads
        and heads % 2 == 0
        and queries.shape[0] == seq * TILE
        and bucket_table.shape[0] % (2 * TILE) == 0
        and seq >= bucket_table.shape[0] // TILE + 1
        and rel_emb.shape[0] % (16 * seq) == 0
        and rel_emb.shape[1] % (16 * seq) == 0
        and rel_emb.shape[0] % TILE == 0
    )


def solution(mesh):
    in_specs = (
        P("seq", "head"),
        P("seq", "head"),
        P("seq", "head"),
        P("seq", "head"),
        P(),
        P(None, "head"),
        P(None, "head"),
        P(),
        P(),
    )
    out_specs = (
        P("seq", "head"),
        P("seq", "head"),
        P("seq", "head"),
        P(None, "head"),
        P("seq", "head"),
        P("seq", "head"),
    )

    def run(queries, keys, values, out_grad, rel_emb, w_query, w_key, doc_lengths, bucket_table):
        chosen = head_body if fits_heads(mesh, queries, rel_emb, bucket_table) else body
        return jax.shard_map(
            chosen, mesh=mesh, in_specs=in_specs, out_specs=out_specs, check_vma=False
        )(queries, keys, values, out_grad, rel_emb, w_query, w_key, doc_lengths, bucket_table)

    return run
```

```python
import math

import jax
import jax.numpy as jnp
from jax import lax
from jax.experimental import pallas as pl
from jax.experimental.pallas import tpu as pltpu
from jax.sharding import PartitionSpec as P

HD = 64
SPAN = 4
TILE = 128
SPANS = (2, 3, 4, 5, 6, 7)
BF = jnp.bfloat16
F32 = jnp.float32


masked_score = -1e30


def shifted(block, axis, distance):
    devices = range(lax.axis_size(axis))
    route = [(i - distance, i) for i in devices if i - distance in devices]
    return lax.ppermute(block, axis, route)


def contract(left, right, left_dim, right_dim):
    return lax.dot_general(
        left, right, (((left_dim,), (right_dim,)), ((), ())), preferred_element_type=jnp.float32
    )


def doc_index(position, doc_ends, extent):
    inside = (position >= 0) & (position < extent)
    owner = jnp.sum((doc_ends[None, :] <= position[:, None]).astype(jnp.int32), axis=1)
    return jnp.where(inside, owner, -1)


def same_document(row_pos, col_pos, doc_ends, extent):
    return (
        doc_index(row_pos, doc_ends, extent)[:, None]
        == doc_index(col_pos, doc_ends, extent)[None, :]
    )


def tile_tables(bucket_table, shift, rows, buckets):
    offset_span = bucket_table.shape[0] // 2
    spread = jnp.arange(2 * rows - 1, dtype=jnp.int32) - (rows - 1)
    ahead_index = bucket_table[jnp.clip(shift - spread + offset_span, 0, 2 * offset_span - 1)]
    behind_index = bucket_table[jnp.clip(offset_span - shift - spread, 0, 2 * offset_span - 1)]
    bucket_ids = jnp.arange(buckets, dtype=jnp.int32)[None, :]
    ahead_onehot = (ahead_index[:, None] == bucket_ids).astype(jnp.bfloat16)
    behind_onehot = (behind_index[:, None] == bucket_ids).astype(jnp.bfloat16)
    return (ahead_index, behind_index, ahead_onehot, behind_onehot)


def skew_in(spread, width):
    rows = spread.shape[0]
    line = rows + width - 1
    flat = jnp.pad(spread, ((0, 0), (0, 1))).reshape(-1)
    return flat[rows - 1 : rows - 1 + rows * line].reshape(rows, line)[:, :width]


def skew_out(dense):
    rows, width = dense.shape
    line = rows + width - 1
    padded = jnp.pad(dense, ((0, 0), (0, rows - 1))).reshape(-1)
    flat = jnp.pad(padded, (rows - 1, 1))
    return flat.reshape(rows, line + 1)[:, :line]


def tile_scores(
    query_rows, key_rows, pos_keys, pos_queries, ahead_onehot, behind_onehot, score_scale
):
    content = contract(query_rows, key_rows, 1, 1)
    ahead_band = contract(ahead_onehot, pos_keys, 1, 0).astype(jnp.bfloat16)
    behind_band = contract(behind_onehot, pos_queries, 1, 0).astype(jnp.bfloat16)
    query_term = skew_in(contract(query_rows, ahead_band, 1, 1), key_rows.shape[0])
    key_term = skew_in(contract(key_rows, behind_band, 1, 1), query_rows.shape[0]).T
    return score_scale * (content + query_term + key_term)


def query_side(
    query_rows,
    key_rows,
    value_rows,
    grad_rows,
    pos_keys,
    pos_queries,
    same_doc,
    tables,
    score_scale,
):
    tile_rows = query_rows.shape[0]
    tile_count = key_rows.shape[0] // tile_rows
    pieces = []
    for tile in range(tile_count):
        key_tile = key_rows[tile * tile_rows : (tile + 1) * tile_rows]
        pieces.append(
            tile_scores(
                query_rows,
                key_tile,
                pos_keys,
                pos_queries,
                tables[tile][2],
                tables[tile][3],
                score_scale,
            )
        )
    scores = jnp.where(same_doc, jnp.concatenate(pieces, 1), masked_score)
    row_max = jnp.max(scores, axis=1, keepdims=True)
    expd = jnp.where(same_doc, jnp.exp(scores - row_max), 0.0)
    row_sum = jnp.sum(expd, axis=1, keepdims=True)
    probs = expd / row_sum
    dprobs = contract(grad_rows, value_rows, 1, 1)
    row_dot = jnp.sum(probs * dprobs, axis=1, keepdims=True)
    dscores = probs * (dprobs - row_dot)
    dscores_low = dscores.astype(jnp.bfloat16)
    ahead_grad = jnp.zeros((tile_rows, pos_keys.shape[0]), jnp.float32)
    for tile in range(tile_count):
        band = dscores_low[:, tile * tile_rows : (tile + 1) * tile_rows]
        ahead_grad = ahead_grad + contract(skew_out(band), tables[tile][2], 1, 0)
    ahead_low = ahead_grad.astype(jnp.bfloat16)
    query_grad = score_scale * (
        contract(dscores_low, key_rows, 1, 0) + contract(ahead_low, pos_keys, 1, 0)
    )
    bucket_key = score_scale * contract(ahead_low, query_rows, 0, 0)
    probs_low = probs.astype(jnp.bfloat16)
    behind_parts = []
    for tile in range(tile_count):
        band = dscores_low[:, tile * tile_rows : (tile + 1) * tile_rows]
        behind_parts.append(contract(skew_out(band.T), tables[tile][3], 1, 0).astype(jnp.bfloat16))
    behind_low = jnp.concatenate(behind_parts, 0)
    key_grad = score_scale * (
        contract(dscores_low, query_rows, 0, 0) + contract(behind_low, pos_queries, 1, 0)
    )
    value_grad = contract(probs_low, grad_rows, 0, 0)
    bucket_query = score_scale * contract(behind_low, key_rows, 0, 0)
    return (query_grad, key_grad, value_grad, bucket_key, bucket_query)


def split_heads(matrix):
    return matrix.reshape(matrix.shape[0], matrix.shape[1] // HD, HD).transpose(1, 0, 2)


def join_heads(stacked):
    return stacked.transpose(1, 0, 2).reshape(stacked.shape[1], stacked.shape[0] * HD)


def body(queries, keys, values, out_grad, rel_emb, w_query, w_key, doc_lengths, bucket_table):
    tokens_dev = queries.shape[0]
    seq_count = lax.axis_size("seq")
    neighbours = min(SPAN, seq_count // 4)
    extent = tokens_dev * seq_count
    seq_index = lax.axis_index("seq")
    first_token = seq_index * tokens_dev
    score_scale = 1.0 / math.sqrt(3.0 * HD)
    pos_key = jnp.dot(rel_emb, w_key, preferred_element_type=jnp.float32).astype(jnp.bfloat16)
    pos_query = jnp.dot(rel_emb, w_query, preferred_element_type=jnp.float32).astype(jnp.bfloat16)
    doc_ends = jnp.cumsum(doc_lengths)
    buckets = rel_emb.shape[0]
    tables = [
        tile_tables(bucket_table, (neighbours - tile) * tokens_dev, tokens_dev, buckets)
        for tile in range(2 * neighbours + 1)
    ]
    hop_list = list(range(neighbours, 0, -1)) + list(range(-1, -neighbours - 1, -1))
    fetched = []
    for distance in hop_list:
        fetched.append(shifted((keys, values), "seq", distance))
    lower_side = fetched[:neighbours]
    upper_side = fetched[neighbours:]
    key_window = jnp.concatenate(
        [pair[0] for pair in lower_side] + [keys] + [pair[0] for pair in upper_side], 0
    )
    value_window = jnp.concatenate(
        [pair[1] for pair in lower_side] + [values] + [pair[1] for pair in upper_side], 0
    )
    window = key_window.shape[0]
    query_pos = first_token + jnp.arange(tokens_dev, dtype=jnp.int32)
    window_pos = first_token - neighbours * tokens_dev + jnp.arange(window, dtype=jnp.int32)
    same_doc = same_document(query_pos, window_pos, doc_ends, extent)
    query_heads = split_heads(queries)
    grad_heads = split_heads(out_grad)
    pos_key_heads = split_heads(pos_key)
    pos_query_heads = split_heads(pos_query)

    def every_pair(operands):
        query_rows, key_rows, value_rows, grad_rows, pos_keys, pos_queries = operands
        return query_side(
            query_rows,
            key_rows,
            value_rows,
            grad_rows,
            pos_keys,
            pos_queries,
            same_doc,
            tables,
            score_scale,
        )

    query_grad, key_part, value_part, bucket_key, bucket_query = lax.map(
        every_pair,
        (
            query_heads,
            split_heads(key_window),
            split_heads(value_window),
            grad_heads,
            pos_key_heads,
            pos_query_heads,
        ),
    )
    key_flat = join_heads(key_part)
    value_flat = join_heads(value_part)
    key_total = key_flat[neighbours * tokens_dev : (neighbours + 1) * tokens_dev]
    value_total = value_flat[neighbours * tokens_dev : (neighbours + 1) * tokens_dev]
    for distance in hop_list:
        segment = neighbours - distance
        returned = (
            key_flat[segment * tokens_dev : (segment + 1) * tokens_dev],
            value_flat[segment * tokens_dev : (segment + 1) * tokens_dev],
        )
        arrived = shifted((returned[0], returned[1]), "seq", -distance)
        key_total = key_total + arrived[0]
        value_total = value_total + arrived[1]
    key_grad = key_total.astype(jnp.bfloat16)
    value_grad = value_total.astype(jnp.bfloat16)
    query_out = join_heads(query_grad).astype(jnp.bfloat16)
    summed = lax.psum((join_heads(bucket_key), join_heads(bucket_query)), "seq")
    bucket_key_low = summed[0].astype(jnp.bfloat16)
    bucket_query_low = summed[1].astype(jnp.bfloat16)
    rows_dev = rel_emb.shape[1] // seq_count
    rel_columns = lax.dynamic_slice_in_dim(rel_emb, seq_index * rows_dev, rows_dev, 1)
    w_key_grad = contract(rel_columns, bucket_key_low, 0, 0)
    w_query_grad = contract(rel_columns, bucket_query_low, 0, 0)
    rel_partial = contract(bucket_key_low, w_key, 1, 1) + contract(bucket_query_low, w_query, 1, 1)
    rel_emb_grad = lax.psum_scatter(
        rel_partial.astype(jnp.bfloat16), "head", scatter_dimension=1, tiled=True
    ).astype(jnp.float32)
    return (query_out, key_grad, value_grad, rel_emb_grad, w_query_grad, w_key_grad)


def nn(left, right):
    return contract(left, right, 1, 0)


def nt(left, right):
    return contract(left, right, 1, 1)


def grid_of(shape):
    return (
        lax.broadcasted_iota(jnp.int32, shape, 0),
        lax.broadcasted_iota(jnp.int32, shape, 1),
    )


def pack_kernel(q_ref, g_ref, k_ref, v_ref, out_ref, held, pieces, came, left):
    loads = [
        pltpu.make_async_copy(ref, held.at[i], came.at[i])
        for i, ref in enumerate((q_ref, g_ref, k_ref, v_ref))
    ]
    for load in loads:
        load.start()
    for load in loads:
        load.wait()
    stores = []
    for head in range(out_ref.shape[0]):
        cols = slice(head * HD, (head + 1) * HD)
        pieces[head] = jnp.concatenate([held[i, :, cols] for i in range(4)], 1)
        stores.append(pltpu.make_async_copy(pieces.at[head], out_ref.at[head], left.at[head]))
        stores[-1].start()
    for store in stores:
        store.wait()


def table_kernel(pos_ref, table_ref, onehot, pk, pq, both):
    buckets, valid = onehot.shape
    valid0 = valid // 2 + TILE
    for part in range(buckets // TILE):
        ids = lax.broadcasted_iota(jnp.int32, (TILE, valid), 0) + part * TILE
        onehot[pl.ds(part * TILE, TILE), :] = jnp.where(ids == table_ref[...], 1.0, 0.0).astype(BF)
    pos_t = pos_ref[...].astype(F32).T.astype(BF)
    expanded = nn(pos_t, onehot[...]).astype(BF)
    pk[...] = jnp.zeros_like(pk)
    pq[...] = jnp.zeros_like(pq)
    pk[0:HD, valid0 : valid0 + valid] = expanded[:HD]
    pq[0:HD, valid0 : valid0 + valid] = expanded[HD:]
    both[...] = jnp.zeros_like(both)
    both[valid0 : valid0 + valid, :] = expanded.astype(F32).T.astype(BF)


def head_kernel(
    lens_ref, half_ref, own_ref, other_ref, onehot, pk, pq, rows_ref,
    send_ref, keep_ref, bucket_ref, query_ref,
    kvs, acc, acc_pos, g_key, g_query, k_t, k_rev, s_q, st, dp, dtile, pairs, dq_nat, dq_pos,
):
    blocks = own_ref.shape[0]
    tiles = 2 * blocks
    buckets, valid = onehot.shape
    halo = valid // 2 // TILE
    longest = 2 * halo + 1
    scale = 1.0 / math.sqrt(3.0 * HD)
    valid0 = (halo + 1) * TILE
    half = half_ref[0]
    docs = lens_ref.shape[0]
    row, col = grid_of((TILE, TILE))
    swap = jnp.where(row + col == TILE - 1, 1.0, 0.0).astype(BF)
    wrap = row + col >= TILE - 1
    wrap_rev = col >= row
    low = col < HD
    acc[...] = jnp.zeros_like(acc)
    acc_pos[...] = jnp.zeros_like(acc_pos)
    g_key[...] = jnp.zeros_like(g_key)
    g_query[...] = jnp.zeros_like(g_query)

    def transpose_tile(b, carry):
        for ref, tile in ((own_ref, 2 * b + half), (other_ref, 2 * b + 1 - half)):
            kv = ref[b, :, 2 * HD : 4 * HD]
            kvs[tile] = kv
            turned = kv.astype(F32).T.astype(BF)
            k_t[tile] = turned[:HD]
            k_rev[tile] = nn(turned[:HD], swap).astype(BF)
        return carry

    lax.fori_loop(0, blocks, transpose_tile, 0, unroll=True)

    def block(b, carry):
        own = 2 * b + half
        token = own * TILE

        def next_end(d, state):
            end, start, stop = state
            stop = jnp.where(end < token + TILE, end + lens_ref[d], stop)
            end = end + lens_ref[d]
            start = jnp.where(end <= token, end, start)
            return (end, start, stop)

        zero = jnp.int32(0)
        _, reach_low, reach_high = lax.fori_loop(
            0, docs, next_end, (zero, zero, zero), unroll=docs <= 16
        )
        lowest = reach_low // TILE
        count = (reach_high + TILE - 1) // TILE - lowest
        shorter = 0
        for span in SPANS:
            if span < longest:
                pl.when((count > shorter) & (count <= span))(
                    lambda span=span: work(b, own, lowest, span)
                )
                shorter = span
        pl.when(count > shorter)(lambda: work(b, own, lowest, longest))
        return carry

    def work(b, own, lowest, span):
        first = jnp.clip(lowest, 0, tiles - span)
        delta = (own - first) * TILE
        qd = own_ref[b, :, 0 : 2 * HD]
        turned = qd.astype(F32).T
        upper = row < HD
        right = jnp.concatenate(
            [jnp.where(upper, turned, 0.0), jnp.where(upper, 0.0, turned)], 1
        ).astype(BF)
        q_rev = nn(turned[:HD].astype(BF), swap).astype(BF)

        position = own * TILE + lax.broadcasted_iota(jnp.int32, (1, TILE), 1)

        def next_doc(d, state):
            end, start, stop = state
            stop = jnp.where(end <= position, end + lens_ref[d], stop)
            end = end + lens_ref[d]
            start = jnp.where(end <= position, end, start)
            return (end, start, stop)

        nothing = jnp.zeros((1, TILE), jnp.int32)
        _, start, stop = lax.fori_loop(
            0, docs, next_doc, (jnp.int32(0), nothing, nothing), unroll=docs <= 16
        )
        start = start - first * TILE
        stop = stop - first * TILE

        key_x = pl.multiple_of(halo * 2 * TILE - delta, TILE)
        s_q[:, 0 : (span + 1) * TILE] = nn(qd, pk[:, pl.ds(key_x, (span + 1) * TILE)])
        best = jnp.full((8, TILE), masked_score, F32)
        window_kv = kvs[pl.ds(first, span)].reshape(span * TILE, 2 * HD)
        contents = nn(window_kv, right)
        for t in range(span):
            kv = window_kv[t * TILE : (t + 1) * TILE]
            both = contents[t * TILE : (t + 1) * TILE]
            query_x = pl.multiple_of(2 * halo * TILE + delta - t * TILE, TILE)
            s_k = nn(kv, pq[:, pl.ds(query_x, 2 * TILE)])
            key_term = pltpu.roll(
                jnp.where(wrap, s_k[:, :TILE], s_k[:, TILE:]), 1, 1, stride=1, stride_axis=0
            )
            query_term = pltpu.roll(
                jnp.where(
                    wrap,
                    s_q[:, t * TILE : (t + 1) * TILE],
                    s_q[:, (t + 1) * TILE : (t + 2) * TILE],
                ),
                1,
                1,
                stride=1,
                stride_axis=0,
            )
            score = both[:, :TILE] + key_term + query_term.T
            place = row + t * TILE
            score = jnp.where((place >= start) & (place < stop), score, masked_score)
            st[t] = score
            dp[t] = both[:, TILE:]
            best = jnp.maximum(best, jnp.max(score.reshape(TILE // 8, 8, TILE), 0))
        top = jnp.max(best, 0, keepdims=True)
        total = jnp.zeros((8, TILE), F32)
        dot = jnp.zeros((8, TILE), F32)
        for t in range(span):
            expd = jnp.exp((st[t] - top) * scale)
            st[t] = expd
            total = total + jnp.sum(expd.reshape(TILE // 8, 8, TILE), 0)
            dot = dot + jnp.sum((expd * dp[t]).reshape(TILE // 8, 8, TILE), 0)
        inverse = 1.0 / jnp.sum(total, 0, keepdims=True)
        row_dot = jnp.sum(dot, 0, keepdims=True) * inverse

        lows = jnp.where(low, qd, jnp.zeros_like(qd))
        pair = jnp.concatenate([lows, jnp.where(low, jnp.zeros_like(qd), qd)], 0)
        dq_t = jnp.zeros((HD, TILE), F32)
        before = jnp.zeros((TILE, TILE), F32)
        ahead_part = None
        for t in range(span):
            prob = st[t] * inverse
            dscore = (prob * (dp[t] - row_dot)).astype(BF)
            pairs[t] = jnp.concatenate([dscore, prob.astype(BF)], 1)
            stacked = nn(jnp.concatenate([k_t[first + t], swap], 0), dscore)
            dq_t = dq_t + stacked[:HD]
            query_x = pl.multiple_of(2 * halo * TILE + delta - t * TILE, TILE)
            y = pltpu.roll(stacked[HD:], 0, 1, stride=1, stride_axis=0)
            near = jnp.where(wrap_rev, y, 0.0).astype(BF)
            far = jnp.where(wrap_rev, 0.0, y).astype(BF)
            back = nn(jnp.concatenate([near, far], 1), rows_ref[pl.ds(query_x, 2 * TILE), :])
            acc_pos[first + t] += back[:, HD:]
            turned_keys = k_rev[first + t]
            chunk = pl.ds(query_x + TILE, TILE)
            if ahead_part is None:
                g_query[:, chunk] += nn(turned_keys, far)
            else:
                g_query[:, chunk] += nn(
                    jnp.concatenate([ahead_part[0], turned_keys], 1),
                    jnp.concatenate([ahead_part[1], far], 0),
                )
            ahead_part = (turned_keys, near)
            z = pltpu.roll(nt(swap, dscore), 0, 1, stride=1, stride_axis=0)
            dtile[:, t * TILE : (t + 1) * TILE] = jnp.where(wrap_rev, z, before).astype(BF)
            before = z
        g_query[:, pl.ds(query_x, TILE)] += nn(*ahead_part)
        acc[pl.ds(first, span)] += nn(
            pairs[0:span].reshape(span * TILE, 2 * TILE), pair
        ).reshape(span, TILE, 2 * HD)
        dtile[:, span * TILE : (span + 1) * TILE] = jnp.where(wrap_rev, 0.0, before).astype(BF)
        spread_q = dtile[:, 0 : (span + 1) * TILE]
        window = pl.ds(key_x, (span + 1) * TILE)
        g_key[:, window] += nn(q_rev, spread_q)
        back = nn(spread_q, rows_ref[window, :])[:, :HD]
        high = back.astype(BF)
        dq_pos[b] = jnp.concatenate([high, (back - high.astype(F32)).astype(BF)], 1)
        dq_nat[b] = dq_t

    lax.fori_loop(0, blocks, block, 0)

    parts = []
    for g in (g_key, g_query):
        band = g[:, valid0 : valid0 + valid]
        high = band.astype(BF)
        parts += [high, (band - high.astype(F32)).astype(BF)]
    summed = nt(jnp.concatenate(parts, 0), onehot[...])
    bucket_t = scale * jnp.concatenate(
        [summed[:HD] + summed[HD : 2 * HD], summed[2 * HD : 3 * HD] + summed[3 * HD :]], 0
    )
    bucket = bucket_t.T.astype(BF)
    bucket_ref[...] = bucket
    send_ref[blocks * TILE :, :] = bucket
    factor = jnp.where(low, scale, 1.0)

    def gradients(tile):
        back = acc_pos[tile]
        high = back.astype(BF)
        both = nn(swap, jnp.concatenate([high, (back - high.astype(F32)).astype(BF)], 1))
        extra = both[:, :HD] + both[:, HD:]
        extra = jnp.concatenate([extra, jnp.zeros_like(extra)], 1)
        return (acc[tile] + extra) * factor

    def finish(b, carry):
        keep_ref[b] = gradients(2 * b + half)
        send_ref[pl.ds(b * TILE, TILE), :] = gradients(2 * b + 1 - half).astype(BF)
        both = nn(swap, dq_pos[b])
        extra = both[:, :HD] + both[:, HD:]
        grad = scale * (dq_nat[b].T + extra)
        query_ref[b] = jnp.concatenate([grad[: TILE // 2], grad[TILE // 2 :]], 1).astype(BF)
        return carry

    lax.fori_loop(0, blocks, finish, 0, unroll=True)


def join_kernel(half_ref, keep_ref, bucket_ref, query_ref, came_ref, rel_ref, out_ref, weight, bucket):
    blocks = keep_ref.shape[0]
    tiles = 2 * blocks
    half = half_ref[0]
    w_rows = weight.shape[0] // tiles
    b_rows = bucket.shape[0] // tiles
    base_w = TILE + TILE // 2
    base_b = base_w + w_rows
    total = bucket_ref[...].astype(F32) + came_ref[blocks * TILE :, :].astype(F32)
    bucket[...] = total
    weight[...] = nn(total.T.astype(BF), rel_ref[...]).T
    for b in range(blocks):
        came = came_ref[b * TILE : (b + 1) * TILE, :].astype(F32)
        tile = 2 * b + half
        out_ref[b, 0:TILE, :] = (keep_ref[b] + came).astype(BF)
        out_ref[b, TILE:base_w, :] = query_ref[b]
        out_ref[b, base_w:base_b, :] = weight[pl.ds(tile * w_rows, w_rows), :].astype(BF)
        out_ref[b, base_b:, :] = bucket[pl.ds(tile * b_rows, b_rows), :].astype(BF)


def rel_kernel(got_ref, wk_ref, wq_ref, rel_ref):
    heads = range(got_ref.shape[0])
    base_b = got_ref.shape[1] - rel_ref.shape[0]
    rel = nt(jnp.concatenate([got_ref[h, base_b:, :HD] for h in heads], 1), wk_ref[...]) + nt(
        jnp.concatenate([got_ref[h, base_b:, HD:] for h in heads], 1), wq_ref[...]
    )
    rel_ref[...] = rel.astype(BF)


def unpack_kernel(got_ref, dq_ref, dk_ref, dv_ref, dwq_ref, dwk_ref):
    base_w = TILE + TILE // 2
    base_b = base_w + dwk_ref.shape[0]
    for g in range(got_ref.shape[0] // 2):
        cols = slice(2 * g * HD, 2 * (g + 1) * HD)
        two = [got_ref[2 * g], got_ref[2 * g + 1]]
        dq_ref[:, cols] = jnp.concatenate(
            [
                jnp.concatenate([one[TILE:base_w, :HD], one[TILE:base_w, HD:]], 0)
                for one in two
            ],
            1,
        )
        dk_ref[:, cols] = jnp.concatenate([one[:TILE, :HD] for one in two], 1)
        dv_ref[:, cols] = jnp.concatenate([one[:TILE, HD:] for one in two], 1)
        dwk_ref[:, cols] = jnp.concatenate([one[base_w:base_b, :HD] for one in two], 1).astype(F32)
        dwq_ref[:, cols] = jnp.concatenate([one[base_w:base_b, HD:] for one in two], 1).astype(F32)


VMEM = pl.BlockSpec(memory_space=pltpu.VMEM)
SMEM = pl.BlockSpec(memory_space=pltpu.SMEM)
HBM = pl.BlockSpec(memory_space=pltpu.HBM)


def whole_call(kernel, inputs, outputs, scratch=(), scalars=0, source=VMEM, target=VMEM, limit=48):
    return pl.pallas_call(
        kernel,
        out_shape=outputs,
        in_specs=[SMEM] * scalars + [source] * (len(inputs) - scalars),
        out_specs=jax.tree.map(lambda _: target, outputs),
        scratch_shapes=list(scratch),
        compiler_params=pltpu.CompilerParams(vmem_limit_bytes=limit << 20),
    )(*inputs)


def head_body(queries, keys, values, out_grad, rel_emb, w_query, w_key, doc_lengths, bucket_table):
    tokens_dev, width = queries.shape
    heads = width // HD
    seq_count = lax.axis_size("seq")
    seq_index = lax.axis_index("seq")
    buckets, depth = rel_emb.shape
    halo = bucket_table.shape[0] // 2 // TILE
    span = 2 * halo + 1
    mine = seq_index // 2
    half = lax.rem(seq_index, 2).astype(jnp.int32).reshape(1)
    halves = [list(range(0, seq_count, 2)), list(range(1, seq_count, 2))]
    partners = [(i, i ^ 1) for i in range(seq_count)]
    shape = jax.ShapeDtypeStruct
    vm = pltpu.VMEM

    def spread(pieces):
        return lax.all_to_all(pieces, "seq", 0, 0, axis_index_groups=halves, tiled=True)

    packed = whole_call(
        pack_kernel,
        (queries, out_grad, keys, values),
        shape((heads, tokens_dev, 4 * HD), BF),
        [
            vm((4, tokens_dev, width), BF),
            vm((heads, tokens_dev, 4 * HD), BF),
            pltpu.SemaphoreType.DMA((4,)),
            pltpu.SemaphoreType.DMA((heads,)),
        ],
        source=HBM,
        target=HBM,
        limit=64,
    )
    own = spread(packed)
    other = lax.ppermute(own, "seq", partners)
    w_own = jnp.concatenate(
        [
            lax.dynamic_slice_in_dim(w_key, mine * HD, HD, 1),
            lax.dynamic_slice_in_dim(w_query, mine * HD, HD, 1),
        ],
        1,
    )
    pos = nn(rel_emb, w_own).astype(BF)
    table = jnp.flip(bucket_table).reshape(1, -1)
    w_rows, b_rows = depth // seq_count, buckets // seq_count
    rows = TILE + TILE // 2 + w_rows + b_rows
    line = 2 * span * TILE
    tables = whole_call(
        table_kernel,
        (pos, table),
        [
            shape((buckets, table.shape[1]), BF),
            shape((2 * HD, line), BF),
            shape((2 * HD, line), BF),
            shape((line, 2 * HD), BF),
        ],
    )
    sent, kept, bucket, query = whole_call(
        head_kernel,
        (doc_lengths, half, own, other, *tables),
        [
            shape((heads * TILE + buckets, 2 * HD), BF),
            shape((heads, TILE, 2 * HD), F32),
            shape((buckets, 2 * HD), BF),
            shape((heads, TILE // 2, 2 * HD), BF),
        ],
        [
            vm((seq_count, TILE, 2 * HD), BF),
            vm((seq_count, TILE, 2 * HD), F32),
            vm((seq_count, TILE, HD), F32),
            vm((HD, line), F32),
            vm((HD, line), F32),
            vm((seq_count, HD, TILE), BF),
            vm((seq_count, HD, TILE), BF),
            vm((TILE, (span + 1) * TILE), F32),
            vm((span, TILE, TILE), F32),
            vm((span, TILE, TILE), F32),
            vm((TILE, (span + 1) * TILE), BF),
            vm((span, TILE, 2 * TILE), BF),
            vm((heads, HD, TILE), F32),
            vm((heads, TILE, 2 * HD), BF),
        ],
        scalars=2,
    )
    came = lax.ppermute(sent, "seq", partners)
    joined = whole_call(
        join_kernel,
        (half, kept, bucket, query, came, rel_emb),
        shape((heads, rows, 2 * HD), BF),
        [vm((depth, 2 * HD), F32), vm((buckets, 2 * HD), F32)],
        scalars=1,
    )
    returned = spread(joined)
    rel_rows = whole_call(
        rel_kernel, (returned, w_key, w_query), shape((b_rows, depth), BF)
    )
    tokens = shape((tokens_dev, width), BF)
    weights = shape((w_rows, width), F32)
    head_index = lax.axis_index("head")
    mine_rel = lax.dynamic_slice_in_dim(rel_rows, head_index * width, width, 1)
    far_rel = lax.dynamic_slice_in_dim(rel_rows, (1 - head_index) * width, width, 1)
    far_rel = lax.ppermute(far_rel, "head", [(0, 1), (1, 0)])
    rel_own = (mine_rel.astype(F32) + far_rel.astype(F32)).astype(BF)
    near = spread(jnp.broadcast_to(rel_own[None], (heads, b_rows, width)))
    far = lax.ppermute(near, "seq", partners)
    even = jnp.where(half[0] == 0, near, far)
    odd = jnp.where(half[0] == 0, far, near)
    rel_emb_grad = jnp.stack([even, odd], 1).reshape(buckets, width).astype(F32)
    query_grad, key_grad, value_grad, w_query_grad, w_key_grad = whole_call(
        unpack_kernel, (returned,), [tokens, tokens, tokens, weights, weights]
    )
    return (query_grad, key_grad, value_grad, rel_emb_grad, w_query_grad, w_key_grad)


def fits_heads(mesh, queries, rel_emb, bucket_table):
    seq, head = mesh.shape["seq"], mesh.shape["head"]
    heads = queries.shape[1] // HD // head
    return (
        head == 2
        and seq == 2 * heads
        and heads % 2 == 0
        and queries.shape[0] == seq * TILE
        and bucket_table.shape[0] % (2 * TILE) == 0
        and seq >= bucket_table.shape[0] // TILE + 1
        and rel_emb.shape[0] % (16 * seq) == 0
        and rel_emb.shape[1] % (16 * seq) == 0
        and rel_emb.shape[0] % TILE == 0
    )


def solution(mesh):
    in_specs = (
        P("seq", "head"),
        P("seq", "head"),
        P("seq", "head"),
        P("seq", "head"),
        P(),
        P(None, "head"),
        P(None, "head"),
        P(),
        P(),
    )
    out_specs = (
        P("seq", "head"),
        P("seq", "head"),
        P("seq", "head"),
        P(None, "head"),
        P("seq", "head"),
        P("seq", "head"),
    )

    def run(queries, keys, values, out_grad, rel_emb, w_query, w_key, doc_lengths, bucket_table):
        chosen = head_body if fits_heads(mesh, queries, rel_emb, bucket_table) else body
        return jax.shard_map(
            chosen, mesh=mesh, in_specs=in_specs, out_specs=out_specs, check_vma=False
        )(queries, keys, values, out_grad, rel_emb, w_query, w_key, doc_lengths, bucket_table)

    return run
```

```python
import math

import jax
import jax.numpy as jnp
from jax import lax
from jax.experimental import pallas as pl
from jax.experimental.pallas import tpu as pltpu
from jax.sharding import PartitionSpec as P

HD = 64
SPAN = 4
TILE = 128
SPANS = (2, 3, 4, 5, 6, 7)
BF = jnp.bfloat16
F32 = jnp.float32


masked_score = -1e30


def shifted(block, axis, distance):
    devices = range(lax.axis_size(axis))
    route = [(i - distance, i) for i in devices if i - distance in devices]
    return lax.ppermute(block, axis, route)


def contract(left, right, left_dim, right_dim):
    return lax.dot_general(
        left, right, (((left_dim,), (right_dim,)), ((), ())), preferred_element_type=jnp.float32
    )


def doc_index(position, doc_ends, extent):
    inside = (position >= 0) & (position < extent)
    owner = jnp.sum((doc_ends[None, :] <= position[:, None]).astype(jnp.int32), axis=1)
    return jnp.where(inside, owner, -1)


def same_document(row_pos, col_pos, doc_ends, extent):
    return (
        doc_index(row_pos, doc_ends, extent)[:, None]
        == doc_index(col_pos, doc_ends, extent)[None, :]
    )


def tile_tables(bucket_table, shift, rows, buckets):
    offset_span = bucket_table.shape[0] // 2
    spread = jnp.arange(2 * rows - 1, dtype=jnp.int32) - (rows - 1)
    ahead_index = bucket_table[jnp.clip(shift - spread + offset_span, 0, 2 * offset_span - 1)]
    behind_index = bucket_table[jnp.clip(offset_span - shift - spread, 0, 2 * offset_span - 1)]
    bucket_ids = jnp.arange(buckets, dtype=jnp.int32)[None, :]
    ahead_onehot = (ahead_index[:, None] == bucket_ids).astype(jnp.bfloat16)
    behind_onehot = (behind_index[:, None] == bucket_ids).astype(jnp.bfloat16)
    return (ahead_index, behind_index, ahead_onehot, behind_onehot)


def skew_in(spread, width):
    rows = spread.shape[0]
    line = rows + width - 1
    flat = jnp.pad(spread, ((0, 0), (0, 1))).reshape(-1)
    return flat[rows - 1 : rows - 1 + rows * line].reshape(rows, line)[:, :width]


def skew_out(dense):
    rows, width = dense.shape
    line = rows + width - 1
    padded = jnp.pad(dense, ((0, 0), (0, rows - 1))).reshape(-1)
    flat = jnp.pad(padded, (rows - 1, 1))
    return flat.reshape(rows, line + 1)[:, :line]


def tile_scores(
    query_rows, key_rows, pos_keys, pos_queries, ahead_onehot, behind_onehot, score_scale
):
    content = contract(query_rows, key_rows, 1, 1)
    ahead_band = contract(ahead_onehot, pos_keys, 1, 0).astype(jnp.bfloat16)
    behind_band = contract(behind_onehot, pos_queries, 1, 0).astype(jnp.bfloat16)
    query_term = skew_in(contract(query_rows, ahead_band, 1, 1), key_rows.shape[0])
    key_term = skew_in(contract(key_rows, behind_band, 1, 1), query_rows.shape[0]).T
    return score_scale * (content + query_term + key_term)


def query_side(
    query_rows,
    key_rows,
    value_rows,
    grad_rows,
    pos_keys,
    pos_queries,
    same_doc,
    tables,
    score_scale,
):
    tile_rows = query_rows.shape[0]
    tile_count = key_rows.shape[0] // tile_rows
    pieces = []
    for tile in range(tile_count):
        key_tile = key_rows[tile * tile_rows : (tile + 1) * tile_rows]
        pieces.append(
            tile_scores(
                query_rows,
                key_tile,
                pos_keys,
                pos_queries,
                tables[tile][2],
                tables[tile][3],
                score_scale,
            )
        )
    scores = jnp.where(same_doc, jnp.concatenate(pieces, 1), masked_score)
    row_max = jnp.max(scores, axis=1, keepdims=True)
    expd = jnp.where(same_doc, jnp.exp(scores - row_max), 0.0)
    row_sum = jnp.sum(expd, axis=1, keepdims=True)
    probs = expd / row_sum
    dprobs = contract(grad_rows, value_rows, 1, 1)
    row_dot = jnp.sum(probs * dprobs, axis=1, keepdims=True)
    dscores = probs * (dprobs - row_dot)
    dscores_low = dscores.astype(jnp.bfloat16)
    ahead_grad = jnp.zeros((tile_rows, pos_keys.shape[0]), jnp.float32)
    for tile in range(tile_count):
        band = dscores_low[:, tile * tile_rows : (tile + 1) * tile_rows]
        ahead_grad = ahead_grad + contract(skew_out(band), tables[tile][2], 1, 0)
    ahead_low = ahead_grad.astype(jnp.bfloat16)
    query_grad = score_scale * (
        contract(dscores_low, key_rows, 1, 0) + contract(ahead_low, pos_keys, 1, 0)
    )
    bucket_key = score_scale * contract(ahead_low, query_rows, 0, 0)
    probs_low = probs.astype(jnp.bfloat16)
    behind_parts = []
    for tile in range(tile_count):
        band = dscores_low[:, tile * tile_rows : (tile + 1) * tile_rows]
        behind_parts.append(contract(skew_out(band.T), tables[tile][3], 1, 0).astype(jnp.bfloat16))
    behind_low = jnp.concatenate(behind_parts, 0)
    key_grad = score_scale * (
        contract(dscores_low, query_rows, 0, 0) + contract(behind_low, pos_queries, 1, 0)
    )
    value_grad = contract(probs_low, grad_rows, 0, 0)
    bucket_query = score_scale * contract(behind_low, key_rows, 0, 0)
    return (query_grad, key_grad, value_grad, bucket_key, bucket_query)


def split_heads(matrix):
    return matrix.reshape(matrix.shape[0], matrix.shape[1] // HD, HD).transpose(1, 0, 2)


def join_heads(stacked):
    return stacked.transpose(1, 0, 2).reshape(stacked.shape[1], stacked.shape[0] * HD)


def body(queries, keys, values, out_grad, rel_emb, w_query, w_key, doc_lengths, bucket_table):
    tokens_dev = queries.shape[0]
    seq_count = lax.axis_size("seq")
    neighbours = min(SPAN, seq_count // 4)
    extent = tokens_dev * seq_count
    seq_index = lax.axis_index("seq")
    first_token = seq_index * tokens_dev
    score_scale = 1.0 / math.sqrt(3.0 * HD)
    pos_key = jnp.dot(rel_emb, w_key, preferred_element_type=jnp.float32).astype(jnp.bfloat16)
    pos_query = jnp.dot(rel_emb, w_query, preferred_element_type=jnp.float32).astype(jnp.bfloat16)
    doc_ends = jnp.cumsum(doc_lengths)
    buckets = rel_emb.shape[0]
    tables = [
        tile_tables(bucket_table, (neighbours - tile) * tokens_dev, tokens_dev, buckets)
        for tile in range(2 * neighbours + 1)
    ]
    hop_list = list(range(neighbours, 0, -1)) + list(range(-1, -neighbours - 1, -1))
    fetched = []
    for distance in hop_list:
        fetched.append(shifted((keys, values), "seq", distance))
    lower_side = fetched[:neighbours]
    upper_side = fetched[neighbours:]
    key_window = jnp.concatenate(
        [pair[0] for pair in lower_side] + [keys] + [pair[0] for pair in upper_side], 0
    )
    value_window = jnp.concatenate(
        [pair[1] for pair in lower_side] + [values] + [pair[1] for pair in upper_side], 0
    )
    window = key_window.shape[0]
    query_pos = first_token + jnp.arange(tokens_dev, dtype=jnp.int32)
    window_pos = first_token - neighbours * tokens_dev + jnp.arange(window, dtype=jnp.int32)
    same_doc = same_document(query_pos, window_pos, doc_ends, extent)
    query_heads = split_heads(queries)
    grad_heads = split_heads(out_grad)
    pos_key_heads = split_heads(pos_key)
    pos_query_heads = split_heads(pos_query)

    def every_pair(operands):
        query_rows, key_rows, value_rows, grad_rows, pos_keys, pos_queries = operands
        return query_side(
            query_rows,
            key_rows,
            value_rows,
            grad_rows,
            pos_keys,
            pos_queries,
            same_doc,
            tables,
            score_scale,
        )

    query_grad, key_part, value_part, bucket_key, bucket_query = lax.map(
        every_pair,
        (
            query_heads,
            split_heads(key_window),
            split_heads(value_window),
            grad_heads,
            pos_key_heads,
            pos_query_heads,
        ),
    )
    key_flat = join_heads(key_part)
    value_flat = join_heads(value_part)
    key_total = key_flat[neighbours * tokens_dev : (neighbours + 1) * tokens_dev]
    value_total = value_flat[neighbours * tokens_dev : (neighbours + 1) * tokens_dev]
    for distance in hop_list:
        segment = neighbours - distance
        returned = (
            key_flat[segment * tokens_dev : (segment + 1) * tokens_dev],
            value_flat[segment * tokens_dev : (segment + 1) * tokens_dev],
        )
        arrived = shifted((returned[0], returned[1]), "seq", -distance)
        key_total = key_total + arrived[0]
        value_total = value_total + arrived[1]
    key_grad = key_total.astype(jnp.bfloat16)
    value_grad = value_total.astype(jnp.bfloat16)
    query_out = join_heads(query_grad).astype(jnp.bfloat16)
    summed = lax.psum((join_heads(bucket_key), join_heads(bucket_query)), "seq")
    bucket_key_low = summed[0].astype(jnp.bfloat16)
    bucket_query_low = summed[1].astype(jnp.bfloat16)
    rows_dev = rel_emb.shape[1] // seq_count
    rel_columns = lax.dynamic_slice_in_dim(rel_emb, seq_index * rows_dev, rows_dev, 1)
    w_key_grad = contract(rel_columns, bucket_key_low, 0, 0)
    w_query_grad = contract(rel_columns, bucket_query_low, 0, 0)
    rel_partial = contract(bucket_key_low, w_key, 1, 1) + contract(bucket_query_low, w_query, 1, 1)
    rel_emb_grad = lax.psum_scatter(
        rel_partial.astype(jnp.bfloat16), "head", scatter_dimension=1, tiled=True
    ).astype(jnp.float32)
    return (query_out, key_grad, value_grad, rel_emb_grad, w_query_grad, w_key_grad)


def nn(left, right):
    return contract(left, right, 1, 0)


def nt(left, right):
    return contract(left, right, 1, 1)


def grid_of(shape):
    return (
        lax.broadcasted_iota(jnp.int32, shape, 0),
        lax.broadcasted_iota(jnp.int32, shape, 1),
    )


def pack_kernel(q_ref, g_ref, k_ref, v_ref, out_ref, held, pieces, came, left):
    loads = [
        pltpu.make_async_copy(ref, held.at[i], came.at[i])
        for i, ref in enumerate((q_ref, g_ref, k_ref, v_ref))
    ]
    for load in loads:
        load.start()
    for load in loads:
        load.wait()
    stores = []
    for head in range(out_ref.shape[0]):
        cols = slice(head * HD, (head + 1) * HD)
        pieces[head] = jnp.concatenate([held[i, :, cols] for i in range(4)], 1)
        stores.append(pltpu.make_async_copy(pieces.at[head], out_ref.at[head], left.at[head]))
        stores[-1].start()
    for store in stores:
        store.wait()


def table_kernel(pos_ref, table_ref, onehot, pk, pq, both):
    buckets, valid = onehot.shape
    valid0 = valid // 2 + TILE
    for part in range(buckets // TILE):
        ids = lax.broadcasted_iota(jnp.int32, (TILE, valid), 0) + part * TILE
        onehot[pl.ds(part * TILE, TILE), :] = jnp.where(ids == table_ref[...], 1.0, 0.0).astype(BF)
    pos_t = pos_ref[...].astype(F32).T.astype(BF)
    expanded = nn(pos_t, onehot[...]).astype(BF)
    pk[...] = jnp.zeros_like(pk)
    pq[...] = jnp.zeros_like(pq)
    pk[0:HD, valid0 : valid0 + valid] = expanded[:HD]
    pq[0:HD, valid0 : valid0 + valid] = expanded[HD:]
    both[...] = jnp.zeros_like(both)
    both[valid0 : valid0 + valid, :] = expanded.astype(F32).T.astype(BF)


def cut_kernel(own_ref, onehot, pk, pq, rows_ref, out_ref):
    out_ref[...] = own_ref[:, :, 2 * HD :]


def head_kernel(
    scalars_ref, own_ref, other_ref, onehot, pk, pq, rows_ref,
    send_ref, keep_ref, bucket_ref, query_ref,
    kvs, acc, acc_pos, g_key, g_query, k_t, k_rev, s_q, st, dp, dtile, pairs, dq_nat, dq_pos,
):
    blocks = own_ref.shape[0]
    tiles = 2 * blocks
    buckets, valid = onehot.shape
    halo = valid // 2 // TILE
    longest = 2 * halo + 1
    scale = 1.0 / math.sqrt(3.0 * HD)
    valid0 = (halo + 1) * TILE
    docs = scalars_ref.shape[0] - 1
    half = scalars_ref[docs]
    row, col = grid_of((TILE, TILE))
    swap = jnp.where(row + col == TILE - 1, 1.0, 0.0).astype(BF)
    wrap = row + col >= TILE - 1
    keep = jnp.where(col >= row, 1.0, 0.0).astype(BF)
    low = col < HD
    acc[...] = jnp.zeros_like(acc)
    acc_pos[...] = jnp.zeros_like(acc_pos)
    g_key[...] = jnp.zeros_like(g_key)
    g_query[...] = jnp.zeros_like(g_query)

    def transpose_tile(b, carry):
        for kv, tile in (
            (own_ref[b, :, 2 * HD : 4 * HD], 2 * b + half),
            (other_ref[b], 2 * b + 1 - half),
        ):
            kvs[tile] = kv
            turned = kv.astype(F32).T.astype(BF)
            k_t[tile] = turned[:HD]
            k_rev[tile] = nn(turned[:HD], swap).astype(BF)
        return carry

    lax.fori_loop(0, blocks, transpose_tile, 0, unroll=True)

    def block(b, carry):
        own = 2 * b + half
        token = own * TILE

        def next_end(d, state):
            end, start, stop = state
            stop = jnp.where(end < token + TILE, end + scalars_ref[d], stop)
            end = end + scalars_ref[d]
            start = jnp.where(end <= token, end, start)
            return (end, start, stop)

        zero = jnp.int32(0)
        _, reach_low, reach_high = lax.fori_loop(
            0, docs, next_end, (zero, zero, zero), unroll=docs <= 16
        )
        lowest = reach_low // TILE
        count = (reach_high + TILE - 1) // TILE - lowest
        shorter = 0
        for span in SPANS:
            if span < longest:
                pl.when((count > shorter) & (count <= span))(
                    lambda span=span: work(b, own, lowest, span)
                )
                shorter = span
        pl.when(count > shorter)(lambda: work(b, own, lowest, longest))
        return carry

    def work(b, own, lowest, span):
        first = jnp.clip(lowest, 0, tiles - span)
        delta = (own - first) * TILE
        qd = own_ref[b, :, 0 : 2 * HD]
        turned = qd.astype(F32).T
        upper = row < HD
        right = jnp.concatenate(
            [jnp.where(upper, turned, 0.0), jnp.where(upper, 0.0, turned)], 1
        ).astype(BF)
        q_rev = nn(turned[:HD].astype(BF), swap).astype(BF)

        position = own * TILE + lax.broadcasted_iota(jnp.int32, (1, TILE), 1)

        def next_doc(d, state):
            end, start, stop = state
            stop = jnp.where(end <= position, end + scalars_ref[d], stop)
            end = end + scalars_ref[d]
            start = jnp.where(end <= position, end, start)
            return (end, start, stop)

        nothing = jnp.zeros((1, TILE), jnp.int32)
        _, start, stop = lax.fori_loop(
            0, docs, next_doc, (jnp.int32(0), nothing, nothing), unroll=docs <= 16
        )
        start = start - first * TILE
        stop = stop - first * TILE

        key_x = pl.multiple_of(halo * 2 * TILE - delta, TILE)
        s_q[:, 0 : (span + 1) * TILE] = nn(qd, pk[:, pl.ds(key_x, (span + 1) * TILE)])
        best = jnp.full((8, TILE), masked_score, F32)
        window_kv = kvs[pl.ds(first, span)].reshape(span * TILE, 2 * HD)
        contents = nn(window_kv, right)
        for t in range(span):
            kv = window_kv[t * TILE : (t + 1) * TILE]
            both = contents[t * TILE : (t + 1) * TILE]
            query_x = pl.multiple_of(2 * halo * TILE + delta - t * TILE, TILE)
            s_k = nn(kv, pq[:, pl.ds(query_x, 2 * TILE)])
            key_term = pltpu.roll(
                jnp.where(wrap, s_k[:, :TILE], s_k[:, TILE:]), 1, 1, stride=1, stride_axis=0
            )
            query_term = pltpu.roll(
                jnp.where(
                    wrap,
                    s_q[:, t * TILE : (t + 1) * TILE],
                    s_q[:, (t + 1) * TILE : (t + 2) * TILE],
                ),
                1,
                1,
                stride=1,
                stride_axis=0,
            )
            score = both[:, :TILE] + key_term + query_term.T
            inside = (row >= start - t * TILE) & (row < stop - t * TILE)
            score = jnp.where(inside, score, masked_score)
            st[t] = score
            dp[t] = both[:, TILE:]
            best = jnp.maximum(best, jnp.max(score.reshape(TILE // 8, 8, TILE), 0))
        top = jnp.max(best, 0, keepdims=True)
        total = jnp.zeros((8, TILE), F32)
        dot = jnp.zeros((8, TILE), F32)
        for t in range(span):
            expd = jnp.exp2((st[t] - top) * (scale * math.log2(math.e)))
            st[t] = expd
            total = total + jnp.sum(expd.reshape(TILE // 8, 8, TILE), 0)
            dot = dot + jnp.sum((expd * dp[t]).reshape(TILE // 8, 8, TILE), 0)
        inverse = 1.0 / jnp.sum(total, 0, keepdims=True)
        row_dot = jnp.sum(dot, 0, keepdims=True) * inverse

        lows = jnp.where(low, qd, jnp.zeros_like(qd))
        pair = jnp.concatenate([lows, jnp.where(low, jnp.zeros_like(qd), qd)], 0)
        dq_t = jnp.zeros((HD, TILE), F32)
        before = jnp.zeros((TILE, TILE), BF)
        ahead_part = None
        for t in range(span):
            prob = st[t] * inverse
            dscore = (prob * (dp[t] - row_dot)).astype(BF)
            pairs[t] = jnp.concatenate([dscore, prob.astype(BF)], 1)
            stacked = nn(jnp.concatenate([k_t[first + t], swap], 0), dscore)
            dq_t = dq_t + stacked[:HD]
            query_x = pl.multiple_of(2 * halo * TILE + delta - t * TILE, TILE)
            y = pltpu.roll(stacked[HD:], 0, 1, stride=1, stride_axis=0)
            y = y.astype(BF)
            near = y * keep
            far = y - near
            back = nn(jnp.concatenate([near, far], 1), rows_ref[pl.ds(query_x, 2 * TILE), :])
            acc_pos[first + t] += back[:, HD:]
            turned_keys = k_rev[first + t]
            chunk = pl.ds(query_x + TILE, TILE)
            if ahead_part is None:
                g_query[:, chunk] += nn(turned_keys, far)
            else:
                g_query[:, chunk] += nn(
                    jnp.concatenate([ahead_part[0], turned_keys], 1),
                    jnp.concatenate([ahead_part[1], far], 0),
                )
            ahead_part = (turned_keys, near)
            z = pltpu.roll(nt(swap, dscore), 0, 1, stride=1, stride_axis=0)
            z = z.astype(BF)
            here = z * keep
            dtile[:, t * TILE : (t + 1) * TILE] = here + before
            before = z - here
        g_query[:, pl.ds(query_x, TILE)] += nn(*ahead_part)
        acc[pl.ds(first, span)] += nn(
            pairs[0:span].reshape(span * TILE, 2 * TILE), pair
        ).reshape(span, TILE, 2 * HD)
        dtile[:, span * TILE : (span + 1) * TILE] = before
        spread_q = dtile[:, 0 : (span + 1) * TILE]
        window = pl.ds(key_x, (span + 1) * TILE)
        g_key[:, window] += nn(q_rev, spread_q)
        back = nn(spread_q, rows_ref[window, :])[:, :HD]
        high = back.astype(BF)
        dq_pos[b] = jnp.concatenate([high, (back - high.astype(F32)).astype(BF)], 1)
        dq_nat[b] = dq_t

    lax.fori_loop(0, blocks, block, 0)

    parts = []
    for g in (g_key, g_query):
        band = g[:, valid0 : valid0 + valid]
        high = band.astype(BF)
        parts += [high, (band - high.astype(F32)).astype(BF)]
    summed = nt(jnp.concatenate(parts, 0), onehot[...])
    bucket_t = scale * jnp.concatenate(
        [summed[:HD] + summed[HD : 2 * HD], summed[2 * HD : 3 * HD] + summed[3 * HD :]], 0
    )
    bucket = bucket_t.T.astype(BF)
    bucket_ref[...] = bucket
    send_ref[blocks * TILE :, :] = bucket
    factor = jnp.where(low, scale, 1.0)

    def gradients(tile):
        back = acc_pos[tile]
        high = back.astype(BF)
        both = nn(swap, jnp.concatenate([high, (back - high.astype(F32)).astype(BF)], 1))
        extra = both[:, :HD] + both[:, HD:]
        extra = jnp.concatenate([extra, jnp.zeros_like(extra)], 1)
        return (acc[tile] + extra) * factor

    def finish(b, carry):
        keep_ref[b] = gradients(2 * b + half)
        send_ref[pl.ds(b * TILE, TILE), :] = gradients(2 * b + 1 - half).astype(BF)
        both = nn(swap, dq_pos[b])
        extra = both[:, :HD] + both[:, HD:]
        grad = scale * (dq_nat[b].T + extra)
        query_ref[b] = jnp.concatenate([grad[: TILE // 2], grad[TILE // 2 :]], 1).astype(BF)
        return carry

    lax.fori_loop(0, blocks, finish, 0, unroll=True)


def join_kernel(half_ref, keep_ref, bucket_ref, query_ref, came_ref, rel_ref, out_ref, weight, bucket):
    blocks = keep_ref.shape[0]
    tiles = 2 * blocks
    half = half_ref[0]
    w_rows = weight.shape[0] // tiles
    b_rows = bucket.shape[0] // tiles
    base_w = TILE + TILE // 2
    base_b = base_w + w_rows
    total = bucket_ref[...].astype(F32) + came_ref[blocks * TILE :, :].astype(F32)
    bucket[...] = total
    weight[...] = nn(total.T.astype(BF), rel_ref[...]).T
    for b in range(blocks):
        came = came_ref[b * TILE : (b + 1) * TILE, :].astype(F32)
        tile = 2 * b + half
        out_ref[b, 0:TILE, :] = (keep_ref[b] + came).astype(BF)
        out_ref[b, TILE:base_w, :] = query_ref[b]
        out_ref[b, base_w:base_b, :] = weight[pl.ds(tile * w_rows, w_rows), :].astype(BF)
        out_ref[b, base_b:, :] = bucket[pl.ds(tile * b_rows, b_rows), :].astype(BF)


def weave_kernel(half_ref, near_ref, far_ref, out_ref):
    shards, rows, _ = near_ref.shape
    half = half_ref[0]
    for shard in range(shards):
        for ref, place in ((near_ref, half), (far_ref, 1 - half)):
            start = pl.multiple_of((2 * shard + place) * rows, rows)
            out_ref[pl.ds(start, rows), :] = ref[shard].astype(F32)


def rel_kernel(got_ref, wk_ref, wq_ref, rel_ref):
    heads = range(got_ref.shape[0])
    base_b = got_ref.shape[1] - rel_ref.shape[0]
    rel = nt(jnp.concatenate([got_ref[h, base_b:, :HD] for h in heads], 1), wk_ref[...]) + nt(
        jnp.concatenate([got_ref[h, base_b:, HD:] for h in heads], 1), wq_ref[...]
    )
    rel_ref[...] = rel.astype(BF)


def unpack_kernel(got_ref, dq_ref, dk_ref, dv_ref, dwq_ref, dwk_ref):
    base_w = TILE + TILE // 2
    base_b = base_w + dwk_ref.shape[0]
    for g in range(got_ref.shape[0] // 2):
        cols = slice(2 * g * HD, 2 * (g + 1) * HD)
        two = [got_ref[2 * g], got_ref[2 * g + 1]]
        dq_ref[:, cols] = jnp.concatenate(
            [
                jnp.concatenate([one[TILE:base_w, :HD], one[TILE:base_w, HD:]], 0)
                for one in two
            ],
            1,
        )
        dk_ref[:, cols] = jnp.concatenate([one[:TILE, :HD] for one in two], 1)
        dv_ref[:, cols] = jnp.concatenate([one[:TILE, HD:] for one in two], 1)
        dwk_ref[:, cols] = jnp.concatenate([one[base_w:base_b, :HD] for one in two], 1).astype(F32)
        dwq_ref[:, cols] = jnp.concatenate([one[base_w:base_b, HD:] for one in two], 1).astype(F32)


VMEM = pl.BlockSpec(memory_space=pltpu.VMEM)
SMEM = pl.BlockSpec(memory_space=pltpu.SMEM)
HBM = pl.BlockSpec(memory_space=pltpu.HBM)


def whole_call(kernel, inputs, outputs, scratch=(), scalars=0, source=VMEM, target=VMEM, limit=48):
    return pl.pallas_call(
        kernel,
        out_shape=outputs,
        in_specs=[SMEM] * scalars + [source] * (len(inputs) - scalars),
        out_specs=jax.tree.map(lambda _: target, outputs),
        scratch_shapes=list(scratch),
        compiler_params=pltpu.CompilerParams(vmem_limit_bytes=limit << 20),
    )(*inputs)


def head_body(queries, keys, values, out_grad, rel_emb, w_query, w_key, doc_lengths, bucket_table):
    tokens_dev, width = queries.shape
    heads = width // HD
    seq_count = lax.axis_size("seq")
    seq_index = lax.axis_index("seq")
    buckets, depth = rel_emb.shape
    halo = bucket_table.shape[0] // 2 // TILE
    span = 2 * halo + 1
    mine = seq_index // 2
    half = lax.rem(seq_index, 2).astype(jnp.int32).reshape(1)
    halves = [list(range(0, seq_count, 2)), list(range(1, seq_count, 2))]
    partners = [(i, i ^ 1) for i in range(seq_count)]
    shape = jax.ShapeDtypeStruct
    vm = pltpu.VMEM

    def spread(pieces):
        return lax.all_to_all(pieces, "seq", 0, 0, axis_index_groups=halves, tiled=True)

    packed = whole_call(
        pack_kernel,
        (queries, out_grad, keys, values),
        shape((heads, tokens_dev, 4 * HD), BF),
        [
            vm((4, tokens_dev, width), BF),
            vm((heads, tokens_dev, 4 * HD), BF),
            pltpu.SemaphoreType.DMA((4,)),
            pltpu.SemaphoreType.DMA((heads,)),
        ],
        source=HBM,
        target=HBM,
        limit=64,
    )
    own = spread(packed)
    w_own = jnp.concatenate(
        [
            lax.dynamic_slice_in_dim(w_key, mine * HD, HD, 1),
            lax.dynamic_slice_in_dim(w_query, mine * HD, HD, 1),
        ],
        1,
    )
    pos = nn(rel_emb, w_own).astype(BF)
    table = jnp.flip(bucket_table).reshape(1, -1)
    w_rows, b_rows = depth // seq_count, buckets // seq_count
    rows = TILE + TILE // 2 + w_rows + b_rows
    line = 2 * span * TILE
    tables = whole_call(
        table_kernel,
        (pos, table),
        [
            shape((buckets, table.shape[1]), BF),
            shape((2 * HD, line), BF),
            shape((2 * HD, line), BF),
            shape((line, 2 * HD), BF),
        ],
    )
    other = lax.ppermute(
        whole_call(cut_kernel, (own, *tables), shape((heads, tokens_dev, 2 * HD), BF)),
        "seq",
        partners,
    )
    sent, kept, bucket, query = whole_call(
        head_kernel,
        (jnp.concatenate([doc_lengths, half]), own, other, *tables),
        [
            shape((heads * TILE + buckets, 2 * HD), BF),
            shape((heads, TILE, 2 * HD), F32),
            shape((buckets, 2 * HD), BF),
            shape((heads, TILE // 2, 2 * HD), BF),
        ],
        [
            vm((seq_count, TILE, 2 * HD), BF),
            vm((seq_count, TILE, 2 * HD), F32),
            vm((seq_count, TILE, HD), F32),
            vm((HD, line), F32),
            vm((HD, line), F32),
            vm((seq_count, HD, TILE), BF),
            vm((seq_count, HD, TILE), BF),
            vm((TILE, (span + 1) * TILE), F32),
            vm((span, TILE, TILE), F32),
            vm((span, TILE, TILE), F32),
            vm((TILE, (span + 1) * TILE), BF),
            vm((span, TILE, 2 * TILE), BF),
            vm((heads, HD, TILE), F32),
            vm((heads, TILE, 2 * HD), BF),
        ],
        scalars=1,
    )
    came = lax.ppermute(sent, "seq", partners)
    joined = whole_call(
        join_kernel,
        (half, kept, bucket, query, came, rel_emb),
        shape((heads, rows, 2 * HD), BF),
        [vm((depth, 2 * HD), F32), vm((buckets, 2 * HD), F32)],
        scalars=1,
    )
    returned = spread(joined)
    rel_rows = whole_call(
        rel_kernel, (returned, w_key, w_query), shape((b_rows, depth), BF)
    )
    tokens = shape((tokens_dev, width), BF)
    weights = shape((w_rows, width), F32)
    head_index = lax.axis_index("head")
    mine_rel = lax.dynamic_slice_in_dim(rel_rows, head_index * width, width, 1)
    far_rel = lax.dynamic_slice_in_dim(rel_rows, (1 - head_index) * width, width, 1)
    far_rel = lax.ppermute(far_rel, "head", [(0, 1), (1, 0)])
    rel_own = (mine_rel.astype(F32) + far_rel.astype(F32)).astype(BF)
    near = spread(jnp.broadcast_to(rel_own[None], (heads, b_rows, width)))
    far = lax.ppermute(near, "seq", partners)
    rel_emb_grad = whole_call(
        weave_kernel, (half, near, far), shape((buckets, width), F32), scalars=1
    )
    query_grad, key_grad, value_grad, w_query_grad, w_key_grad = whole_call(
        unpack_kernel, (returned,), [tokens, tokens, tokens, weights, weights]
    )
    return (query_grad, key_grad, value_grad, rel_emb_grad, w_query_grad, w_key_grad)


def fits_heads(mesh, queries, rel_emb, bucket_table):
    seq, head = mesh.shape["seq"], mesh.shape["head"]
    heads = queries.shape[1] // HD // head
    return (
        head == 2
        and seq == 2 * heads
        and heads % 2 == 0
        and queries.shape[0] == seq * TILE
        and bucket_table.shape[0] % (2 * TILE) == 0
        and seq >= bucket_table.shape[0] // TILE + 1
        and rel_emb.shape[0] % (16 * seq) == 0
        and rel_emb.shape[1] % (16 * seq) == 0
        and rel_emb.shape[0] % TILE == 0
    )


def solution(mesh):
    in_specs = (
        P("seq", "head"),
        P("seq", "head"),
        P("seq", "head"),
        P("seq", "head"),
        P(),
        P(None, "head"),
        P(None, "head"),
        P(),
        P(),
    )
    out_specs = (
        P("seq", "head"),
        P("seq", "head"),
        P("seq", "head"),
        P(None, "head"),
        P("seq", "head"),
        P("seq", "head"),
    )

    def run(queries, keys, values, out_grad, rel_emb, w_query, w_key, doc_lengths, bucket_table):
        chosen = head_body if fits_heads(mesh, queries, rel_emb, bucket_table) else body
        return jax.shard_map(
            chosen, mesh=mesh, in_specs=in_specs, out_specs=out_specs, check_vma=False
        )(queries, keys, values, out_grad, rel_emb, w_query, w_key, doc_lengths, bucket_table)

    return run
```

```python
import math

import jax
import jax.numpy as jnp
from jax import lax
from jax.experimental import pallas as pl
from jax.experimental.pallas import tpu as pltpu
from jax.sharding import PartitionSpec as P

HD = 64
SPAN = 4
TILE = 128
SPANS = (2, 3, 4, 5, 6, 7)
BF = jnp.bfloat16
F32 = jnp.float32


masked_score = -1e30


def shifted(block, axis, distance):
    devices = range(lax.axis_size(axis))
    route = [(i - distance, i) for i in devices if i - distance in devices]
    return lax.ppermute(block, axis, route)


def contract(left, right, left_dim, right_dim):
    return lax.dot_general(
        left, right, (((left_dim,), (right_dim,)), ((), ())), preferred_element_type=jnp.float32
    )


def doc_index(position, doc_ends, extent):
    inside = (position >= 0) & (position < extent)
    owner = jnp.sum((doc_ends[None, :] <= position[:, None]).astype(jnp.int32), axis=1)
    return jnp.where(inside, owner, -1)


def same_document(row_pos, col_pos, doc_ends, extent):
    return (
        doc_index(row_pos, doc_ends, extent)[:, None]
        == doc_index(col_pos, doc_ends, extent)[None, :]
    )


def tile_tables(bucket_table, shift, rows, buckets):
    offset_span = bucket_table.shape[0] // 2
    spread = jnp.arange(2 * rows - 1, dtype=jnp.int32) - (rows - 1)
    ahead_index = bucket_table[jnp.clip(shift - spread + offset_span, 0, 2 * offset_span - 1)]
    behind_index = bucket_table[jnp.clip(offset_span - shift - spread, 0, 2 * offset_span - 1)]
    bucket_ids = jnp.arange(buckets, dtype=jnp.int32)[None, :]
    ahead_onehot = (ahead_index[:, None] == bucket_ids).astype(jnp.bfloat16)
    behind_onehot = (behind_index[:, None] == bucket_ids).astype(jnp.bfloat16)
    return (ahead_index, behind_index, ahead_onehot, behind_onehot)


def skew_in(spread, width):
    rows = spread.shape[0]
    line = rows + width - 1
    flat = jnp.pad(spread, ((0, 0), (0, 1))).reshape(-1)
    return flat[rows - 1 : rows - 1 + rows * line].reshape(rows, line)[:, :width]


def skew_out(dense):
    rows, width = dense.shape
    line = rows + width - 1
    padded = jnp.pad(dense, ((0, 0), (0, rows - 1))).reshape(-1)
    flat = jnp.pad(padded, (rows - 1, 1))
    return flat.reshape(rows, line + 1)[:, :line]


def tile_scores(
    query_rows, key_rows, pos_keys, pos_queries, ahead_onehot, behind_onehot, score_scale
):
    content = contract(query_rows, key_rows, 1, 1)
    ahead_band = contract(ahead_onehot, pos_keys, 1, 0).astype(jnp.bfloat16)
    behind_band = contract(behind_onehot, pos_queries, 1, 0).astype(jnp.bfloat16)
    query_term = skew_in(contract(query_rows, ahead_band, 1, 1), key_rows.shape[0])
    key_term = skew_in(contract(key_rows, behind_band, 1, 1), query_rows.shape[0]).T
    return score_scale * (content + query_term + key_term)


def query_side(
    query_rows,
    key_rows,
    value_rows,
    grad_rows,
    pos_keys,
    pos_queries,
    same_doc,
    tables,
    score_scale,
):
    tile_rows = query_rows.shape[0]
    tile_count = key_rows.shape[0] // tile_rows
    pieces = []
    for tile in range(tile_count):
        key_tile = key_rows[tile * tile_rows : (tile + 1) * tile_rows]
        pieces.append(
            tile_scores(
                query_rows,
                key_tile,
                pos_keys,
                pos_queries,
                tables[tile][2],
                tables[tile][3],
                score_scale,
            )
        )
    scores = jnp.where(same_doc, jnp.concatenate(pieces, 1), masked_score)
    row_max = jnp.max(scores, axis=1, keepdims=True)
    expd = jnp.where(same_doc, jnp.exp(scores - row_max), 0.0)
    row_sum = jnp.sum(expd, axis=1, keepdims=True)
    probs = expd / row_sum
    dprobs = contract(grad_rows, value_rows, 1, 1)
    row_dot = jnp.sum(probs * dprobs, axis=1, keepdims=True)
    dscores = probs * (dprobs - row_dot)
    dscores_low = dscores.astype(jnp.bfloat16)
    ahead_grad = jnp.zeros((tile_rows, pos_keys.shape[0]), jnp.float32)
    for tile in range(tile_count):
        band = dscores_low[:, tile * tile_rows : (tile + 1) * tile_rows]
        ahead_grad = ahead_grad + contract(skew_out(band), tables[tile][2], 1, 0)
    ahead_low = ahead_grad.astype(jnp.bfloat16)
    query_grad = score_scale * (
        contract(dscores_low, key_rows, 1, 0) + contract(ahead_low, pos_keys, 1, 0)
    )
    bucket_key = score_scale * contract(ahead_low, query_rows, 0, 0)
    probs_low = probs.astype(jnp.bfloat16)
    behind_parts = []
    for tile in range(tile_count):
        band = dscores_low[:, tile * tile_rows : (tile + 1) * tile_rows]
        behind_parts.append(contract(skew_out(band.T), tables[tile][3], 1, 0).astype(jnp.bfloat16))
    behind_low = jnp.concatenate(behind_parts, 0)
    key_grad = score_scale * (
        contract(dscores_low, query_rows, 0, 0) + contract(behind_low, pos_queries, 1, 0)
    )
    value_grad = contract(probs_low, grad_rows, 0, 0)
    bucket_query = score_scale * contract(behind_low, key_rows, 0, 0)
    return (query_grad, key_grad, value_grad, bucket_key, bucket_query)


def split_heads(matrix):
    return matrix.reshape(matrix.shape[0], matrix.shape[1] // HD, HD).transpose(1, 0, 2)


def join_heads(stacked):
    return stacked.transpose(1, 0, 2).reshape(stacked.shape[1], stacked.shape[0] * HD)


def body(queries, keys, values, out_grad, rel_emb, w_query, w_key, doc_lengths, bucket_table):
    tokens_dev = queries.shape[0]
    seq_count = lax.axis_size("seq")
    neighbours = min(SPAN, seq_count // 4)
    extent = tokens_dev * seq_count
    seq_index = lax.axis_index("seq")
    first_token = seq_index * tokens_dev
    score_scale = 1.0 / math.sqrt(3.0 * HD)
    pos_key = jnp.dot(rel_emb, w_key, preferred_element_type=jnp.float32).astype(jnp.bfloat16)
    pos_query = jnp.dot(rel_emb, w_query, preferred_element_type=jnp.float32).astype(jnp.bfloat16)
    doc_ends = jnp.cumsum(doc_lengths)
    buckets = rel_emb.shape[0]
    tables = [
        tile_tables(bucket_table, (neighbours - tile) * tokens_dev, tokens_dev, buckets)
        for tile in range(2 * neighbours + 1)
    ]
    hop_list = list(range(neighbours, 0, -1)) + list(range(-1, -neighbours - 1, -1))
    fetched = []
    for distance in hop_list:
        fetched.append(shifted((keys, values), "seq", distance))
    lower_side = fetched[:neighbours]
    upper_side = fetched[neighbours:]
    key_window = jnp.concatenate(
        [pair[0] for pair in lower_side] + [keys] + [pair[0] for pair in upper_side], 0
    )
    value_window = jnp.concatenate(
        [pair[1] for pair in lower_side] + [values] + [pair[1] for pair in upper_side], 0
    )
    window = key_window.shape[0]
    query_pos = first_token + jnp.arange(tokens_dev, dtype=jnp.int32)
    window_pos = first_token - neighbours * tokens_dev + jnp.arange(window, dtype=jnp.int32)
    same_doc = same_document(query_pos, window_pos, doc_ends, extent)
    query_heads = split_heads(queries)
    grad_heads = split_heads(out_grad)
    pos_key_heads = split_heads(pos_key)
    pos_query_heads = split_heads(pos_query)

    def every_pair(operands):
        query_rows, key_rows, value_rows, grad_rows, pos_keys, pos_queries = operands
        return query_side(
            query_rows,
            key_rows,
            value_rows,
            grad_rows,
            pos_keys,
            pos_queries,
            same_doc,
            tables,
            score_scale,
        )

    query_grad, key_part, value_part, bucket_key, bucket_query = lax.map(
        every_pair,
        (
            query_heads,
            split_heads(key_window),
            split_heads(value_window),
            grad_heads,
            pos_key_heads,
            pos_query_heads,
        ),
    )
    key_flat = join_heads(key_part)
    value_flat = join_heads(value_part)
    key_total = key_flat[neighbours * tokens_dev : (neighbours + 1) * tokens_dev]
    value_total = value_flat[neighbours * tokens_dev : (neighbours + 1) * tokens_dev]
    for distance in hop_list:
        segment = neighbours - distance
        returned = (
            key_flat[segment * tokens_dev : (segment + 1) * tokens_dev],
            value_flat[segment * tokens_dev : (segment + 1) * tokens_dev],
        )
        arrived = shifted((returned[0], returned[1]), "seq", -distance)
        key_total = key_total + arrived[0]
        value_total = value_total + arrived[1]
    key_grad = key_total.astype(jnp.bfloat16)
    value_grad = value_total.astype(jnp.bfloat16)
    query_out = join_heads(query_grad).astype(jnp.bfloat16)
    summed = lax.psum((join_heads(bucket_key), join_heads(bucket_query)), "seq")
    bucket_key_low = summed[0].astype(jnp.bfloat16)
    bucket_query_low = summed[1].astype(jnp.bfloat16)
    rows_dev = rel_emb.shape[1] // seq_count
    rel_columns = lax.dynamic_slice_in_dim(rel_emb, seq_index * rows_dev, rows_dev, 1)
    w_key_grad = contract(rel_columns, bucket_key_low, 0, 0)
    w_query_grad = contract(rel_columns, bucket_query_low, 0, 0)
    rel_partial = contract(bucket_key_low, w_key, 1, 1) + contract(bucket_query_low, w_query, 1, 1)
    rel_emb_grad = lax.psum_scatter(
        rel_partial.astype(jnp.bfloat16), "head", scatter_dimension=1, tiled=True
    ).astype(jnp.float32)
    return (query_out, key_grad, value_grad, rel_emb_grad, w_query_grad, w_key_grad)


def nn(left, right):
    return contract(left, right, 1, 0)


def nt(left, right):
    return contract(left, right, 1, 1)


def grid_of(shape):
    return (
        lax.broadcasted_iota(jnp.int32, shape, 0),
        lax.broadcasted_iota(jnp.int32, shape, 1),
    )


def pack_kernel(q_ref, g_ref, k_ref, v_ref, out_ref, held, pieces, came, left):
    loads = [
        pltpu.make_async_copy(ref, held.at[i], came.at[i])
        for i, ref in enumerate((q_ref, g_ref, k_ref, v_ref))
    ]
    for load in loads:
        load.start()
    for load in loads:
        load.wait()
    stores = []
    for head in range(out_ref.shape[0]):
        cols = slice(head * HD, (head + 1) * HD)
        pieces[head] = jnp.concatenate([held[i, :, cols] for i in range(4)], 1)
        stores.append(pltpu.make_async_copy(pieces.at[head], out_ref.at[head], left.at[head]))
        stores[-1].start()
    for store in stores:
        store.wait()


def table_kernel(scalars_ref, pos_ref, table_ref, onehot, expanded):
    buckets, valid = onehot.shape
    for part in range(buckets // TILE):
        ids = lax.broadcasted_iota(jnp.int32, (TILE, valid), 0) + part * TILE
        onehot[pl.ds(part * TILE, TILE), :] = jnp.where(ids == table_ref[...], 1.0, 0.0).astype(BF)
    pos_t = pos_ref[...].astype(F32).T.astype(BF)
    expanded[...] = nn(pos_t, onehot[...]).astype(BF)


def cut_kernel(own_ref, expanded, out_ref):
    out_ref[...] = own_ref[:, :, 2 * HD :]


def head_kernel(
    scalars_ref, own_ref, other_ref, onehot, expanded,
    send_ref, keep_ref, bucket_ref, query_ref,
    pk, pq, rows_ref, kvs, acc, acc_pos, g_key, g_query, k_t, k_rev, s_q, st, dp, dtile, pairs, dq_nat, dq_pos,
):
    blocks = own_ref.shape[0]
    tiles = 2 * blocks
    buckets, valid = onehot.shape
    halo = valid // 2 // TILE
    longest = 2 * halo + 1
    scale = 1.0 / math.sqrt(3.0 * HD)
    valid0 = (halo + 1) * TILE
    docs = scalars_ref.shape[0] - 1
    half = scalars_ref[docs]
    row, col = grid_of((TILE, TILE))
    swap = jnp.where(row + col == TILE - 1, 1.0, 0.0).astype(BF)
    wrap = row + col >= TILE - 1
    keep = jnp.where(col >= row, 1.0, 0.0).astype(BF)
    low = col < HD
    for table in (pk, pq, rows_ref):
        table[...] = jnp.zeros_like(table)
    pk[0:HD, valid0 : valid0 + valid] = expanded[:HD]
    pq[0:HD, valid0 : valid0 + valid] = expanded[HD:]
    rows_ref[valid0 : valid0 + valid, :] = expanded[...].astype(F32).T.astype(BF)
    acc[...] = jnp.zeros_like(acc)
    acc_pos[...] = jnp.zeros_like(acc_pos)
    g_key[...] = jnp.zeros_like(g_key)
    g_query[...] = jnp.zeros_like(g_query)

    def transpose_tile(b, carry):
        for kv, tile in (
            (own_ref[b, :, 2 * HD : 4 * HD], 2 * b + half),
            (other_ref[b], 2 * b + 1 - half),
        ):
            kvs[tile] = kv
            turned = kv.astype(F32).T.astype(BF)
            k_t[tile] = turned[:HD]
            k_rev[tile] = nn(turned[:HD], swap).astype(BF)
        return carry

    lax.fori_loop(0, blocks, transpose_tile, 0, unroll=True)

    def block(b, carry):
        own = 2 * b + half
        token = own * TILE

        def next_end(d, state):
            end, start, stop = state
            stop = jnp.where(end < token + TILE, end + scalars_ref[d], stop)
            end = end + scalars_ref[d]
            start = jnp.where(end <= token, end, start)
            return (end, start, stop)

        zero = jnp.int32(0)
        _, reach_low, reach_high = lax.fori_loop(
            0, docs, next_end, (zero, zero, zero), unroll=docs <= 16
        )
        lowest = reach_low // TILE
        count = (reach_high + TILE - 1) // TILE - lowest
        shorter = 0
        for span in SPANS:
            if span < longest:
                pl.when((count > shorter) & (count <= span))(
                    lambda span=span: work(b, own, lowest, span)
                )
                shorter = span
        pl.when(count > shorter)(lambda: work(b, own, lowest, longest))
        return carry

    def work(b, own, lowest, span):
        first = jnp.clip(lowest, 0, tiles - span)
        delta = (own - first) * TILE
        qd = own_ref[b, :, 0 : 2 * HD]
        turned = qd.astype(F32).T
        upper = row < HD
        right = jnp.concatenate(
            [jnp.where(upper, turned, 0.0), jnp.where(upper, 0.0, turned)], 1
        ).astype(BF)
        q_rev = nn(turned[:HD].astype(BF), swap).astype(BF)

        position = own * TILE + lax.broadcasted_iota(jnp.int32, (1, TILE), 1)

        def next_doc(d, state):
            end, start, stop = state
            stop = jnp.where(end <= position, end + scalars_ref[d], stop)
            end = end + scalars_ref[d]
            start = jnp.where(end <= position, end, start)
            return (end, start, stop)

        nothing = jnp.zeros((1, TILE), jnp.int32)
        _, start, stop = lax.fori_loop(
            0, docs, next_doc, (jnp.int32(0), nothing, nothing), unroll=docs <= 16
        )
        start = start - first * TILE
        stop = stop - first * TILE

        key_x = pl.multiple_of(halo * 2 * TILE - delta, TILE)
        s_q[:, 0 : (span + 1) * TILE] = nn(qd, pk[:, pl.ds(key_x, (span + 1) * TILE)])
        best = jnp.full((8, TILE), masked_score, F32)
        window_kv = kvs[pl.ds(first, span)].reshape(span * TILE, 2 * HD)
        contents = nn(window_kv, right)
        for t in range(span):
            kv = window_kv[t * TILE : (t + 1) * TILE]
            both = contents[t * TILE : (t + 1) * TILE]
            query_x = pl.multiple_of(2 * halo * TILE + delta - t * TILE, TILE)
            s_k = nn(kv, pq[:, pl.ds(query_x, 2 * TILE)])
            key_term = pltpu.roll(
                jnp.where(wrap, s_k[:, :TILE], s_k[:, TILE:]), 1, 1, stride=1, stride_axis=0
            )
            query_term = pltpu.roll(
                jnp.where(
                    wrap,
                    s_q[:, t * TILE : (t + 1) * TILE],
                    s_q[:, (t + 1) * TILE : (t + 2) * TILE],
                ),
                1,
                1,
                stride=1,
                stride_axis=0,
            )
            score = both[:, :TILE] + key_term + query_term.T
            inside = (row >= start - t * TILE) & (row < stop - t * TILE)
            score = jnp.where(inside, score, masked_score)
            st[t] = score
            dp[t] = both[:, TILE:]
            best = jnp.maximum(best, jnp.max(score.reshape(TILE // 8, 8, TILE), 0))
        top = jnp.max(best, 0, keepdims=True)
        total = jnp.zeros((8, TILE), F32)
        dot = jnp.zeros((8, TILE), F32)
        for t in range(span):
            expd = jnp.exp2((st[t] - top) * (scale * math.log2(math.e)))
            st[t] = expd
            total = total + jnp.sum(expd.reshape(TILE // 8, 8, TILE), 0)
            dot = dot + jnp.sum((expd * dp[t]).reshape(TILE // 8, 8, TILE), 0)
        inverse = 1.0 / jnp.sum(total, 0, keepdims=True)
        row_dot = jnp.sum(dot, 0, keepdims=True) * inverse

        lows = jnp.where(low, qd, jnp.zeros_like(qd))
        pair = jnp.concatenate([lows, jnp.where(low, jnp.zeros_like(qd), qd)], 0)
        dq_t = jnp.zeros((HD, TILE), F32)
        before = jnp.zeros((TILE, TILE), BF)
        ahead_part = None
        for t in range(span):
            prob = st[t] * inverse
            dscore = (prob * (dp[t] - row_dot)).astype(BF)
            pairs[t] = jnp.concatenate([dscore, prob.astype(BF)], 1)
            stacked = nn(jnp.concatenate([k_t[first + t], swap], 0), dscore)
            dq_t = dq_t + stacked[:HD]
            query_x = pl.multiple_of(2 * halo * TILE + delta - t * TILE, TILE)
            y = pltpu.roll(stacked[HD:], 0, 1, stride=1, stride_axis=0)
            y = y.astype(BF)
            near = y * keep
            far = y - near
            back = nn(jnp.concatenate([near, far], 1), rows_ref[pl.ds(query_x, 2 * TILE), :])
            acc_pos[first + t] += back[:, HD:]
            turned_keys = k_rev[first + t]
            chunk = pl.ds(query_x + TILE, TILE)
            if ahead_part is None:
                g_query[:, chunk] += nn(turned_keys, far)
            else:
                g_query[:, chunk] += nn(
                    jnp.concatenate([ahead_part[0], turned_keys], 1),
                    jnp.concatenate([ahead_part[1], far], 0),
                )
            ahead_part = (turned_keys, near)
            z = pltpu.roll(nt(swap, dscore), 0, 1, stride=1, stride_axis=0)
            z = z.astype(BF)
            here = z * keep
            dtile[:, t * TILE : (t + 1) * TILE] = here + before
            before = z - here
        g_query[:, pl.ds(query_x, TILE)] += nn(*ahead_part)
        acc[pl.ds(first, span)] += nn(
            pairs[0:span].reshape(span * TILE, 2 * TILE), pair
        ).reshape(span, TILE, 2 * HD)
        dtile[:, span * TILE : (span + 1) * TILE] = before
        spread_q = dtile[:, 0 : (span + 1) * TILE]
        window = pl.ds(key_x, (span + 1) * TILE)
        g_key[:, window] += nn(q_rev, spread_q)
        back = nn(spread_q, rows_ref[window, :])[:, :HD]
        high = back.astype(BF)
        dq_pos[b] = jnp.concatenate([high, (back - high.astype(F32)).astype(BF)], 1)
        dq_nat[b] = dq_t

    lax.fori_loop(0, blocks, block, 0)

    parts = []
    for g in (g_key, g_query):
        band = g[:, valid0 : valid0 + valid]
        high = band.astype(BF)
        parts += [high, (band - high.astype(F32)).astype(BF)]
    summed = nt(jnp.concatenate(parts, 0), onehot[...])
    bucket_t = scale * jnp.concatenate(
        [summed[:HD] + summed[HD : 2 * HD], summed[2 * HD : 3 * HD] + summed[3 * HD :]], 0
    )
    bucket = bucket_t.T.astype(BF)
    bucket_ref[...] = bucket
    send_ref[blocks * TILE :, :] = bucket
    factor = jnp.where(low, scale, 1.0)

    def gradients(tile):
        back = acc_pos[tile]
        high = back.astype(BF)
        both = nn(swap, jnp.concatenate([high, (back - high.astype(F32)).astype(BF)], 1))
        extra = both[:, :HD] + both[:, HD:]
        extra = jnp.concatenate([extra, jnp.zeros_like(extra)], 1)
        return (acc[tile] + extra) * factor

    def finish(b, carry):
        keep_ref[b] = gradients(2 * b + half)
        send_ref[pl.ds(b * TILE, TILE), :] = gradients(2 * b + 1 - half).astype(BF)
        both = nn(swap, dq_pos[b])
        extra = both[:, :HD] + both[:, HD:]
        grad = scale * (dq_nat[b].T + extra)
        query_ref[b] = jnp.concatenate([grad[: TILE // 2], grad[TILE // 2 :]], 1).astype(BF)
        return carry

    lax.fori_loop(0, blocks, finish, 0, unroll=True)


def join_kernel(half_ref, keep_ref, bucket_ref, query_ref, came_ref, rel_ref, out_ref, weight, bucket):
    blocks = keep_ref.shape[0]
    tiles = 2 * blocks
    half = half_ref[0]
    w_rows = weight.shape[0] // tiles
    b_rows = bucket.shape[0] // tiles
    base_w = TILE + TILE // 2
    base_b = base_w + w_rows
    total = bucket_ref[...].astype(F32) + came_ref[blocks * TILE :, :].astype(F32)
    bucket[...] = total
    weight[...] = nn(total.T.astype(BF), rel_ref[...]).T
    for b in range(blocks):
        came = came_ref[b * TILE : (b + 1) * TILE, :].astype(F32)
        tile = 2 * b + half
        out_ref[b, 0:TILE, :] = (keep_ref[b] + came).astype(BF)
        out_ref[b, TILE:base_w, :] = query_ref[b]
        out_ref[b, base_w:base_b, :] = weight[pl.ds(tile * w_rows, w_rows), :].astype(BF)
        out_ref[b, base_b:, :] = bucket[pl.ds(tile * b_rows, b_rows), :].astype(BF)


def weave_kernel(half_ref, near_ref, far_ref, out_ref):
    shards, rows, _ = near_ref.shape
    half = half_ref[0]
    for shard in range(shards):
        for ref, place in ((near_ref, half), (far_ref, 1 - half)):
            start = pl.multiple_of((2 * shard + place) * rows, rows)
            out_ref[pl.ds(start, rows), :] = ref[shard].astype(F32)


def rel_kernel(got_ref, wk_ref, wq_ref, rel_ref):
    heads = range(got_ref.shape[0])
    base_b = got_ref.shape[1] - rel_ref.shape[0]
    rel = nt(jnp.concatenate([got_ref[h, base_b:, :HD] for h in heads], 1), wk_ref[...]) + nt(
        jnp.concatenate([got_ref[h, base_b:, HD:] for h in heads], 1), wq_ref[...]
    )
    rel_ref[...] = rel.astype(BF)


def unpack_kernel(got_ref, dq_ref, dk_ref, dv_ref, dwq_ref, dwk_ref):
    base_w = TILE + TILE // 2
    base_b = base_w + dwk_ref.shape[0]
    for g in range(got_ref.shape[0] // 2):
        cols = slice(2 * g * HD, 2 * (g + 1) * HD)
        two = [got_ref[2 * g], got_ref[2 * g + 1]]
        dq_ref[:, cols] = jnp.concatenate(
            [
                jnp.concatenate([one[TILE:base_w, :HD], one[TILE:base_w, HD:]], 0)
                for one in two
            ],
            1,
        )
        dk_ref[:, cols] = jnp.concatenate([one[:TILE, :HD] for one in two], 1)
        dv_ref[:, cols] = jnp.concatenate([one[:TILE, HD:] for one in two], 1)
        dwk_ref[:, cols] = jnp.concatenate([one[base_w:base_b, :HD] for one in two], 1).astype(F32)
        dwq_ref[:, cols] = jnp.concatenate([one[base_w:base_b, HD:] for one in two], 1).astype(F32)


VMEM = pl.BlockSpec(memory_space=pltpu.VMEM)
SMEM = pl.BlockSpec(memory_space=pltpu.SMEM)
HBM = pl.BlockSpec(memory_space=pltpu.HBM)


def whole_call(kernel, inputs, outputs, scratch=(), scalars=0, source=VMEM, target=VMEM, limit=48):
    return pl.pallas_call(
        kernel,
        out_shape=outputs,
        in_specs=[SMEM] * scalars + [source] * (len(inputs) - scalars),
        out_specs=jax.tree.map(lambda _: target, outputs),
        scratch_shapes=list(scratch),
        compiler_params=pltpu.CompilerParams(vmem_limit_bytes=limit << 20),
    )(*inputs)


def head_body(queries, keys, values, out_grad, rel_emb, w_query, w_key, doc_lengths, bucket_table):
    tokens_dev, width = queries.shape
    heads = width // HD
    seq_count = lax.axis_size("seq")
    seq_index = lax.axis_index("seq")
    buckets, depth = rel_emb.shape
    halo = bucket_table.shape[0] // 2 // TILE
    span = 2 * halo + 1
    mine = seq_index // 2
    half = lax.rem(seq_index, 2).astype(jnp.int32).reshape(1)
    halves = [list(range(0, seq_count, 2)), list(range(1, seq_count, 2))]
    partners = [(i, i ^ 1) for i in range(seq_count)]
    shape = jax.ShapeDtypeStruct
    vm = pltpu.VMEM

    def spread(pieces):
        return lax.all_to_all(pieces, "seq", 0, 0, axis_index_groups=halves, tiled=True)

    packed = whole_call(
        pack_kernel,
        (queries, out_grad, keys, values),
        shape((heads, tokens_dev, 4 * HD), BF),
        [
            vm((4, tokens_dev, width), BF),
            vm((heads, tokens_dev, 4 * HD), BF),
            pltpu.SemaphoreType.DMA((4,)),
            pltpu.SemaphoreType.DMA((heads,)),
        ],
        source=HBM,
        target=HBM,
        limit=64,
    )
    own = spread(packed)
    w_own = jnp.concatenate(
        [
            lax.dynamic_slice_in_dim(w_key, mine * HD, HD, 1),
            lax.dynamic_slice_in_dim(w_query, mine * HD, HD, 1),
        ],
        1,
    )
    pos = nn(rel_emb, w_own).astype(BF)
    table = jnp.flip(bucket_table).reshape(1, -1)
    w_rows, b_rows = depth // seq_count, buckets // seq_count
    rows = TILE + TILE // 2 + w_rows + b_rows
    line = 2 * span * TILE
    scalars = jnp.concatenate([doc_lengths, half])
    onehot, expanded = whole_call(
        table_kernel,
        (scalars, pos, table),
        [shape((buckets, table.shape[1]), BF), shape((2 * HD, table.shape[1]), BF)],
        scalars=1,
    )
    other = lax.ppermute(
        whole_call(cut_kernel, (own, expanded), shape((heads, tokens_dev, 2 * HD), BF)),
        "seq",
        partners,
    )
    sent, kept, bucket, query = whole_call(
        head_kernel,
        (scalars, own, other, onehot, expanded),
        [
            shape((heads * TILE + buckets, 2 * HD), BF),
            shape((heads, TILE, 2 * HD), F32),
            shape((buckets, 2 * HD), BF),
            shape((heads, TILE // 2, 2 * HD), BF),
        ],
        [
            vm((2 * HD, line), BF),
            vm((2 * HD, line), BF),
            vm((line, 2 * HD), BF),
            vm((seq_count, TILE, 2 * HD), BF),
            vm((seq_count, TILE, 2 * HD), F32),
            vm((seq_count, TILE, HD), F32),
            vm((HD, line), F32),
            vm((HD, line), F32),
            vm((seq_count, HD, TILE), BF),
            vm((seq_count, HD, TILE), BF),
            vm((TILE, (span + 1) * TILE), F32),
            vm((span, TILE, TILE), F32),
            vm((span, TILE, TILE), F32),
            vm((TILE, (span + 1) * TILE), BF),
            vm((span, TILE, 2 * TILE), BF),
            vm((heads, HD, TILE), F32),
            vm((heads, TILE, 2 * HD), BF),
        ],
        scalars=1,
    )
    came = lax.ppermute(sent, "seq", partners)
    joined = whole_call(
        join_kernel,
        (half, kept, bucket, query, came, rel_emb),
        shape((heads, rows, 2 * HD), BF),
        [vm((depth, 2 * HD), F32), vm((buckets, 2 * HD), F32)],
        scalars=1,
    )
    returned = spread(joined)
    rel_rows = whole_call(
        rel_kernel, (returned, w_key, w_query), shape((b_rows, depth), BF)
    )
    tokens = shape((tokens_dev, width), BF)
    weights = shape((w_rows, width), F32)
    head_index = lax.axis_index("head")
    mine_rel = lax.dynamic_slice_in_dim(rel_rows, head_index * width, width, 1)
    far_rel = lax.dynamic_slice_in_dim(rel_rows, (1 - head_index) * width, width, 1)
    far_rel = lax.ppermute(far_rel, "head", [(0, 1), (1, 0)])
    rel_own = (mine_rel.astype(F32) + far_rel.astype(F32)).astype(BF)
    near = spread(jnp.broadcast_to(rel_own[None], (heads, b_rows, width)))
    far = lax.ppermute(near, "seq", partners)
    rel_emb_grad = whole_call(
        weave_kernel, (half, near, far), shape((buckets, width), F32), scalars=1
    )
    query_grad, key_grad, value_grad, w_query_grad, w_key_grad = whole_call(
        unpack_kernel, (returned,), [tokens, tokens, tokens, weights, weights]
    )
    return (query_grad, key_grad, value_grad, rel_emb_grad, w_query_grad, w_key_grad)


def fits_heads(mesh, queries, rel_emb, bucket_table):
    seq, head = mesh.shape["seq"], mesh.shape["head"]
    heads = queries.shape[1] // HD // head
    return (
        head == 2
        and seq == 2 * heads
        and heads % 2 == 0
        and queries.shape[0] == seq * TILE
        and bucket_table.shape[0] % (2 * TILE) == 0
        and seq >= bucket_table.shape[0] // TILE + 1
        and rel_emb.shape[0] % (16 * seq) == 0
        and rel_emb.shape[1] % (16 * seq) == 0
        and rel_emb.shape[0] % TILE == 0
    )


def solution(mesh):
    in_specs = (
        P("seq", "head"),
        P("seq", "head"),
        P("seq", "head"),
        P("seq", "head"),
        P(),
        P(None, "head"),
        P(None, "head"),
        P(),
        P(),
    )
    out_specs = (
        P("seq", "head"),
        P("seq", "head"),
        P("seq", "head"),
        P(None, "head"),
        P("seq", "head"),
        P("seq", "head"),
    )

    def run(queries, keys, values, out_grad, rel_emb, w_query, w_key, doc_lengths, bucket_table):
        chosen = head_body if fits_heads(mesh, queries, rel_emb, bucket_table) else body
        return jax.shard_map(
            chosen, mesh=mesh, in_specs=in_specs, out_specs=out_specs, check_vma=False
        )(queries, keys, values, out_grad, rel_emb, w_query, w_key, doc_lengths, bucket_table)

    return run
```

```python
import math

import jax
import jax.numpy as jnp
from jax import lax
from jax.experimental import pallas as pl
from jax.experimental.pallas import tpu as pltpu
from jax.sharding import PartitionSpec as P

HD = 64
SPAN = 4
TILE = 128
SPANS = (2, 3, 4, 5, 6, 7)
BF = jnp.bfloat16
F32 = jnp.float32


masked_score = -1e30


def shifted(block, axis, distance):
    devices = range(lax.axis_size(axis))
    route = [(i - distance, i) for i in devices if i - distance in devices]
    return lax.ppermute(block, axis, route)


def contract(left, right, left_dim, right_dim):
    return lax.dot_general(
        left, right, (((left_dim,), (right_dim,)), ((), ())), preferred_element_type=jnp.float32
    )


def doc_index(position, doc_ends, extent):
    inside = (position >= 0) & (position < extent)
    owner = jnp.sum((doc_ends[None, :] <= position[:, None]).astype(jnp.int32), axis=1)
    return jnp.where(inside, owner, -1)


def same_document(row_pos, col_pos, doc_ends, extent):
    return (
        doc_index(row_pos, doc_ends, extent)[:, None]
        == doc_index(col_pos, doc_ends, extent)[None, :]
    )


def tile_tables(bucket_table, shift, rows, buckets):
    offset_span = bucket_table.shape[0] // 2
    spread = jnp.arange(2 * rows - 1, dtype=jnp.int32) - (rows - 1)
    ahead_index = bucket_table[jnp.clip(shift - spread + offset_span, 0, 2 * offset_span - 1)]
    behind_index = bucket_table[jnp.clip(offset_span - shift - spread, 0, 2 * offset_span - 1)]
    bucket_ids = jnp.arange(buckets, dtype=jnp.int32)[None, :]
    ahead_onehot = (ahead_index[:, None] == bucket_ids).astype(jnp.bfloat16)
    behind_onehot = (behind_index[:, None] == bucket_ids).astype(jnp.bfloat16)
    return (ahead_index, behind_index, ahead_onehot, behind_onehot)


def skew_in(spread, width):
    rows = spread.shape[0]
    line = rows + width - 1
    flat = jnp.pad(spread, ((0, 0), (0, 1))).reshape(-1)
    return flat[rows - 1 : rows - 1 + rows * line].reshape(rows, line)[:, :width]


def skew_out(dense):
    rows, width = dense.shape
    line = rows + width - 1
    padded = jnp.pad(dense, ((0, 0), (0, rows - 1))).reshape(-1)
    flat = jnp.pad(padded, (rows - 1, 1))
    return flat.reshape(rows, line + 1)[:, :line]


def tile_scores(
    query_rows, key_rows, pos_keys, pos_queries, ahead_onehot, behind_onehot, score_scale
):
    content = contract(query_rows, key_rows, 1, 1)
    ahead_band = contract(ahead_onehot, pos_keys, 1, 0).astype(jnp.bfloat16)
    behind_band = contract(behind_onehot, pos_queries, 1, 0).astype(jnp.bfloat16)
    query_term = skew_in(contract(query_rows, ahead_band, 1, 1), key_rows.shape[0])
    key_term = skew_in(contract(key_rows, behind_band, 1, 1), query_rows.shape[0]).T
    return score_scale * (content + query_term + key_term)


def query_side(
    query_rows,
    key_rows,
    value_rows,
    grad_rows,
    pos_keys,
    pos_queries,
    same_doc,
    tables,
    score_scale,
):
    tile_rows = query_rows.shape[0]
    tile_count = key_rows.shape[0] // tile_rows
    pieces = []
    for tile in range(tile_count):
        key_tile = key_rows[tile * tile_rows : (tile + 1) * tile_rows]
        pieces.append(
            tile_scores(
                query_rows,
                key_tile,
                pos_keys,
                pos_queries,
                tables[tile][2],
                tables[tile][3],
                score_scale,
            )
        )
    scores = jnp.where(same_doc, jnp.concatenate(pieces, 1), masked_score)
    row_max = jnp.max(scores, axis=1, keepdims=True)
    expd = jnp.where(same_doc, jnp.exp(scores - row_max), 0.0)
    row_sum = jnp.sum(expd, axis=1, keepdims=True)
    probs = expd / row_sum
    dprobs = contract(grad_rows, value_rows, 1, 1)
    row_dot = jnp.sum(probs * dprobs, axis=1, keepdims=True)
    dscores = probs * (dprobs - row_dot)
    dscores_low = dscores.astype(jnp.bfloat16)
    ahead_grad = jnp.zeros((tile_rows, pos_keys.shape[0]), jnp.float32)
    for tile in range(tile_count):
        band = dscores_low[:, tile * tile_rows : (tile + 1) * tile_rows]
        ahead_grad = ahead_grad + contract(skew_out(band), tables[tile][2], 1, 0)
    ahead_low = ahead_grad.astype(jnp.bfloat16)
    query_grad = score_scale * (
        contract(dscores_low, key_rows, 1, 0) + contract(ahead_low, pos_keys, 1, 0)
    )
    bucket_key = score_scale * contract(ahead_low, query_rows, 0, 0)
    probs_low = probs.astype(jnp.bfloat16)
    behind_parts = []
    for tile in range(tile_count):
        band = dscores_low[:, tile * tile_rows : (tile + 1) * tile_rows]
        behind_parts.append(contract(skew_out(band.T), tables[tile][3], 1, 0).astype(jnp.bfloat16))
    behind_low = jnp.concatenate(behind_parts, 0)
    key_grad = score_scale * (
        contract(dscores_low, query_rows, 0, 0) + contract(behind_low, pos_queries, 1, 0)
    )
    value_grad = contract(probs_low, grad_rows, 0, 0)
    bucket_query = score_scale * contract(behind_low, key_rows, 0, 0)
    return (query_grad, key_grad, value_grad, bucket_key, bucket_query)


def split_heads(matrix):
    return matrix.reshape(matrix.shape[0], matrix.shape[1] // HD, HD).transpose(1, 0, 2)


def join_heads(stacked):
    return stacked.transpose(1, 0, 2).reshape(stacked.shape[1], stacked.shape[0] * HD)


def body(queries, keys, values, out_grad, rel_emb, w_query, w_key, doc_lengths, bucket_table):
    tokens_dev = queries.shape[0]
    seq_count = lax.axis_size("seq")
    neighbours = min(SPAN, seq_count // 4)
    extent = tokens_dev * seq_count
    seq_index = lax.axis_index("seq")
    first_token = seq_index * tokens_dev
    score_scale = 1.0 / math.sqrt(3.0 * HD)
    pos_key = jnp.dot(rel_emb, w_key, preferred_element_type=jnp.float32).astype(jnp.bfloat16)
    pos_query = jnp.dot(rel_emb, w_query, preferred_element_type=jnp.float32).astype(jnp.bfloat16)
    doc_ends = jnp.cumsum(doc_lengths)
    buckets = rel_emb.shape[0]
    tables = [
        tile_tables(bucket_table, (neighbours - tile) * tokens_dev, tokens_dev, buckets)
        for tile in range(2 * neighbours + 1)
    ]
    hop_list = list(range(neighbours, 0, -1)) + list(range(-1, -neighbours - 1, -1))
    fetched = []
    for distance in hop_list:
        fetched.append(shifted((keys, values), "seq", distance))
    lower_side = fetched[:neighbours]
    upper_side = fetched[neighbours:]
    key_window = jnp.concatenate(
        [pair[0] for pair in lower_side] + [keys] + [pair[0] for pair in upper_side], 0
    )
    value_window = jnp.concatenate(
        [pair[1] for pair in lower_side] + [values] + [pair[1] for pair in upper_side], 0
    )
    window = key_window.shape[0]
    query_pos = first_token + jnp.arange(tokens_dev, dtype=jnp.int32)
    window_pos = first_token - neighbours * tokens_dev + jnp.arange(window, dtype=jnp.int32)
    same_doc = same_document(query_pos, window_pos, doc_ends, extent)
    query_heads = split_heads(queries)
    grad_heads = split_heads(out_grad)
    pos_key_heads = split_heads(pos_key)
    pos_query_heads = split_heads(pos_query)

    def every_pair(operands):
        query_rows, key_rows, value_rows, grad_rows, pos_keys, pos_queries = operands
        return query_side(
            query_rows,
            key_rows,
            value_rows,
            grad_rows,
            pos_keys,
            pos_queries,
            same_doc,
            tables,
            score_scale,
        )

    query_grad, key_part, value_part, bucket_key, bucket_query = lax.map(
        every_pair,
        (
            query_heads,
            split_heads(key_window),
            split_heads(value_window),
            grad_heads,
            pos_key_heads,
            pos_query_heads,
        ),
    )
    key_flat = join_heads(key_part)
    value_flat = join_heads(value_part)
    key_total = key_flat[neighbours * tokens_dev : (neighbours + 1) * tokens_dev]
    value_total = value_flat[neighbours * tokens_dev : (neighbours + 1) * tokens_dev]
    for distance in hop_list:
        segment = neighbours - distance
        returned = (
            key_flat[segment * tokens_dev : (segment + 1) * tokens_dev],
            value_flat[segment * tokens_dev : (segment + 1) * tokens_dev],
        )
        arrived = shifted((returned[0], returned[1]), "seq", -distance)
        key_total = key_total + arrived[0]
        value_total = value_total + arrived[1]
    key_grad = key_total.astype(jnp.bfloat16)
    value_grad = value_total.astype(jnp.bfloat16)
    query_out = join_heads(query_grad).astype(jnp.bfloat16)
    summed = lax.psum((join_heads(bucket_key), join_heads(bucket_query)), "seq")
    bucket_key_low = summed[0].astype(jnp.bfloat16)
    bucket_query_low = summed[1].astype(jnp.bfloat16)
    rows_dev = rel_emb.shape[1] // seq_count
    rel_columns = lax.dynamic_slice_in_dim(rel_emb, seq_index * rows_dev, rows_dev, 1)
    w_key_grad = contract(rel_columns, bucket_key_low, 0, 0)
    w_query_grad = contract(rel_columns, bucket_query_low, 0, 0)
    rel_partial = contract(bucket_key_low, w_key, 1, 1) + contract(bucket_query_low, w_query, 1, 1)
    rel_emb_grad = lax.psum_scatter(
        rel_partial.astype(jnp.bfloat16), "head", scatter_dimension=1, tiled=True
    ).astype(jnp.float32)
    return (query_out, key_grad, value_grad, rel_emb_grad, w_query_grad, w_key_grad)


def nn(left, right):
    return contract(left, right, 1, 0)


def nt(left, right):
    return contract(left, right, 1, 1)


def grid_of(shape):
    return (
        lax.broadcasted_iota(jnp.int32, shape, 0),
        lax.broadcasted_iota(jnp.int32, shape, 1),
    )


def pack_kernel(q_ref, g_ref, k_ref, v_ref, out_ref, held, pieces, came, left):
    loads = [
        pltpu.make_async_copy(ref, held.at[i], came.at[i])
        for i, ref in enumerate((q_ref, g_ref, k_ref, v_ref))
    ]
    for load in loads:
        load.start()
    for load in loads:
        load.wait()
    stores = []
    for head in range(out_ref.shape[0]):
        cols = slice(head * HD, (head + 1) * HD)
        pieces[head] = jnp.concatenate([held[i, :, cols] for i in range(4)], 1)
        stores.append(pltpu.make_async_copy(pieces.at[head], out_ref.at[head], left.at[head]))
        stores[-1].start()
    for store in stores:
        store.wait()


def table_kernel(scalars_ref, pos_ref, table_ref, onehot, expanded):
    buckets, valid = onehot.shape
    for part in range(buckets // TILE):
        ids = lax.broadcasted_iota(jnp.int32, (TILE, valid), 0) + part * TILE
        onehot[pl.ds(part * TILE, TILE), :] = jnp.where(ids == table_ref[...], 1.0, 0.0).astype(BF)
    pos_t = pos_ref[...].astype(F32).T.astype(BF)
    expanded[...] = nn(pos_t, onehot[...]).astype(BF)


def cut_kernel(own_ref, expanded, out_ref):
    out_ref[...] = own_ref[:, :, 2 * HD :]


def head_kernel(
    scalars_ref, own_ref, other_ref, onehot, expanded,
    send_ref, keep_ref, bucket_ref, query_ref,
    pk, pq, kvs, acc, acc_pos, g_key, g_query, k_t, k_rev, s_q, st, dp, dtile, pairs, dq_nat, dq_pos,
):
    blocks = own_ref.shape[0]
    tiles = 2 * blocks
    buckets, valid = onehot.shape
    halo = valid // 2 // TILE
    longest = 2 * halo + 1
    scale = 1.0 / math.sqrt(3.0 * HD)
    valid0 = (halo + 1) * TILE
    docs = scalars_ref.shape[0] - 1
    half = scalars_ref[docs]
    row, col = grid_of((TILE, TILE))
    swap = jnp.where(row + col == TILE - 1, 1.0, 0.0).astype(BF)
    wrap = row + col >= TILE - 1
    keep = jnp.where(col >= row, 1.0, 0.0).astype(BF)
    low = col < HD
    for table, part in ((pk, expanded[:HD]), (pq, expanded[HD:])):
        table[...] = jnp.zeros_like(table)
        table[:, valid0 : valid0 + valid] = part
    acc[...] = jnp.zeros_like(acc)
    acc_pos[...] = jnp.zeros_like(acc_pos)
    g_key[...] = jnp.zeros_like(g_key)
    g_query[...] = jnp.zeros_like(g_query)

    def transpose_tile(b, carry):
        for kv, tile in (
            (own_ref[b, :, 2 * HD : 4 * HD], 2 * b + half),
            (other_ref[b], 2 * b + 1 - half),
        ):
            kvs[tile] = kv
            turned = kv.astype(F32).T.astype(BF)
            k_t[tile] = turned[:HD]
            k_rev[tile] = nn(turned[:HD], swap).astype(BF)
        return carry

    lax.fori_loop(0, blocks, transpose_tile, 0, unroll=True)

    def block(b, carry):
        own = 2 * b + half
        token = own * TILE

        def next_end(d, state):
            end, start, stop = state
            stop = jnp.where(end < token + TILE, end + scalars_ref[d], stop)
            end = end + scalars_ref[d]
            start = jnp.where(end <= token, end, start)
            return (end, start, stop)

        zero = jnp.int32(0)
        _, reach_low, reach_high = lax.fori_loop(
            0, docs, next_end, (zero, zero, zero), unroll=docs <= 16
        )
        lowest = reach_low // TILE
        count = (reach_high + TILE - 1) // TILE - lowest
        shorter = 0
        for span in SPANS:
            if span < longest:
                pl.when((count > shorter) & (count <= span))(
                    lambda span=span: work(b, own, lowest, span)
                )
                shorter = span
        pl.when(count > shorter)(lambda: work(b, own, lowest, longest))
        return carry

    def work(b, own, lowest, span):
        first = jnp.clip(lowest, 0, tiles - span)
        delta = (own - first) * TILE
        qd = own_ref[b, :, 0 : 2 * HD]
        turned = qd.astype(F32).T
        upper = row < HD
        right = jnp.concatenate(
            [jnp.where(upper, turned, 0.0), jnp.where(upper, 0.0, turned)], 1
        ).astype(BF)
        q_rev = nn(turned[:HD].astype(BF), swap).astype(BF)

        position = own * TILE + lax.broadcasted_iota(jnp.int32, (1, TILE), 1)

        def next_doc(d, state):
            end, start, stop = state
            stop = jnp.where(end <= position, end + scalars_ref[d], stop)
            end = end + scalars_ref[d]
            start = jnp.where(end <= position, end, start)
            return (end, start, stop)

        nothing = jnp.zeros((1, TILE), jnp.int32)
        _, start, stop = lax.fori_loop(
            0, docs, next_doc, (jnp.int32(0), nothing, nothing), unroll=docs <= 16
        )
        start = start - first * TILE
        stop = stop - first * TILE

        key_x = pl.multiple_of(halo * 2 * TILE - delta, TILE)
        s_q[:, 0 : (span + 1) * TILE] = nn(qd[:, :HD], pk[:, pl.ds(key_x, (span + 1) * TILE)])
        best = jnp.full((8, TILE), masked_score, F32)
        window_kv = kvs[pl.ds(first, span)].reshape(span * TILE, 2 * HD)
        contents = nn(window_kv, right)
        for t in range(span):
            kv = window_kv[t * TILE : (t + 1) * TILE]
            both = contents[t * TILE : (t + 1) * TILE]
            query_x = pl.multiple_of(2 * halo * TILE + delta - t * TILE, TILE)
            s_k = nn(kv[:, :HD], pq[:, pl.ds(query_x, 2 * TILE)])
            key_term = pltpu.roll(
                jnp.where(wrap, s_k[:, :TILE], s_k[:, TILE:]), 1, 1, stride=1, stride_axis=0
            )
            query_term = pltpu.roll(
                jnp.where(
                    wrap,
                    s_q[:, t * TILE : (t + 1) * TILE],
                    s_q[:, (t + 1) * TILE : (t + 2) * TILE],
                ),
                1,
                1,
                stride=1,
                stride_axis=0,
            )
            score = both[:, :TILE] + key_term + query_term.T
            inside = (row >= start - t * TILE) & (row < stop - t * TILE)
            score = jnp.where(inside, score, masked_score)
            st[t] = score
            dp[t] = both[:, TILE:]
            best = jnp.maximum(best, jnp.max(score.reshape(TILE // 8, 8, TILE), 0))
        top = jnp.max(best, 0, keepdims=True)
        total = jnp.zeros((8, TILE), F32)
        dot = jnp.zeros((8, TILE), F32)
        for t in range(span):
            expd = jnp.exp2((st[t] - top) * (scale * math.log2(math.e)))
            st[t] = expd
            total = total + jnp.sum(expd.reshape(TILE // 8, 8, TILE), 0)
            dot = dot + jnp.sum((expd * dp[t]).reshape(TILE // 8, 8, TILE), 0)
        inverse = 1.0 / jnp.sum(total, 0, keepdims=True)
        row_dot = jnp.sum(dot, 0, keepdims=True) * inverse

        lows = jnp.where(low, qd, jnp.zeros_like(qd))
        pair = jnp.concatenate([lows, jnp.where(low, jnp.zeros_like(qd), qd)], 0)
        dq_t = jnp.zeros((HD, TILE), F32)
        before = jnp.zeros((TILE, TILE), BF)
        near = held = None
        for t in range(span):
            prob = st[t] * inverse
            dscore = (prob * (dp[t] - row_dot)).astype(BF)
            pairs[t] = jnp.concatenate([dscore, prob.astype(BF)], 1)
            stacked = nn(
                jnp.concatenate([k_t[first + t], swap], 0),
                jnp.concatenate([dscore, dscore.T], 1),
            )
            dq_t = dq_t + stacked[:HD, :TILE]
            query_x = pl.multiple_of(2 * halo * TILE + delta - t * TILE, TILE)
            y = pltpu.roll(stacked[HD:, :TILE], 0, 1, stride=1, stride_axis=0).astype(BF)
            last = near
            near = y * keep
            far = y - near
            g_query[:, pl.ds(query_x, 2 * TILE)] += nn(
                k_rev[first + t], jnp.concatenate([near, far], 1)
            )
            chunk = pq[:, pl.ds(query_x + TILE, TILE)]
            if t == 0:
                held = nt(chunk, far)
            else:
                back = nt(chunk, jnp.concatenate([last, far], 0))
                acc_pos[first + t - 1] += held + back[:, :TILE]
                held = back[:, TILE:]
            z = pltpu.roll(stacked[HD:, TILE:], 0, 1, stride=1, stride_axis=0).astype(BF)
            here = z * keep
            dtile[:, t * TILE : (t + 1) * TILE] = here + before
            before = z - here
        acc_pos[first + span - 1] += held + nt(pq[:, pl.ds(query_x, TILE)], near)
        acc[pl.ds(first, span)] += nn(
            pairs[0:span].reshape(span * TILE, 2 * TILE), pair
        ).reshape(span, TILE, 2 * HD)
        dtile[:, span * TILE : (span + 1) * TILE] = before
        spread_q = dtile[:, 0 : (span + 1) * TILE]
        window = pl.ds(key_x, (span + 1) * TILE)
        g_key[:, window] += nn(q_rev, spread_q)
        dq_pos[b] = nt(pk[:, window], spread_q)
        dq_nat[b] = dq_t

    lax.fori_loop(0, blocks, block, 0)

    parts = []
    for g in (g_key, g_query):
        band = g[:, valid0 : valid0 + valid]
        high = band.astype(BF)
        parts += [high, (band - high.astype(F32)).astype(BF)]
    summed = nt(jnp.concatenate(parts, 0), onehot[...])
    bucket_t = scale * jnp.concatenate(
        [summed[:HD] + summed[HD : 2 * HD], summed[2 * HD : 3 * HD] + summed[3 * HD :]], 0
    )
    bucket = bucket_t.T.astype(BF)
    bucket_ref[...] = bucket
    send_ref[blocks * TILE :, :] = bucket
    factor = jnp.where(low, scale, 1.0)

    def unreversed(part):
        high = part.astype(BF)
        both = nn(jnp.concatenate([high, (part - high.astype(F32)).astype(BF)], 0), swap)
        return both[:HD] + both[HD:]

    def gradients(tile):
        extra = unreversed(acc_pos[tile]).T
        extra = jnp.concatenate([extra, jnp.zeros_like(extra)], 1)
        return (acc[tile] + extra) * factor

    def finish(b, carry):
        keep_ref[b] = gradients(2 * b + half)
        send_ref[pl.ds(b * TILE, TILE), :] = gradients(2 * b + 1 - half).astype(BF)
        grad = scale * (dq_nat[b] + unreversed(dq_pos[b])).T
        query_ref[b] = jnp.concatenate([grad[: TILE // 2], grad[TILE // 2 :]], 1).astype(BF)
        return carry

    lax.fori_loop(0, blocks, finish, 0, unroll=True)


def join_kernel(half_ref, keep_ref, bucket_ref, query_ref, came_ref, rel_ref, out_ref, weight, bucket):
    blocks = keep_ref.shape[0]
    tiles = 2 * blocks
    half = half_ref[0]
    w_rows = weight.shape[0] // tiles
    b_rows = bucket.shape[0] // tiles
    base_w = TILE + TILE // 2
    base_b = base_w + w_rows
    total = bucket_ref[...].astype(F32) + came_ref[blocks * TILE :, :].astype(F32)
    bucket[...] = total
    weight[...] = nn(total.T.astype(BF), rel_ref[...]).T
    for b in range(blocks):
        came = came_ref[b * TILE : (b + 1) * TILE, :].astype(F32)
        tile = 2 * b + half
        out_ref[b, 0:TILE, :] = (keep_ref[b] + came).astype(BF)
        out_ref[b, TILE:base_w, :] = query_ref[b]
        out_ref[b, base_w:base_b, :] = weight[pl.ds(tile * w_rows, w_rows), :].astype(BF)
        out_ref[b, base_b:, :] = bucket[pl.ds(tile * b_rows, b_rows), :].astype(BF)


def weave_kernel(half_ref, near_ref, far_ref, out_ref):
    shards, rows, _ = near_ref.shape
    half = half_ref[0]
    for shard in range(shards):
        for ref, place in ((near_ref, half), (far_ref, 1 - half)):
            start = pl.multiple_of((2 * shard + place) * rows, rows)
            out_ref[pl.ds(start, rows), :] = ref[shard].astype(F32)


def rel_kernel(got_ref, wk_ref, wq_ref, rel_ref):
    heads = range(got_ref.shape[0])
    base_b = got_ref.shape[1] - rel_ref.shape[0]
    rel = nt(jnp.concatenate([got_ref[h, base_b:, :HD] for h in heads], 1), wk_ref[...]) + nt(
        jnp.concatenate([got_ref[h, base_b:, HD:] for h in heads], 1), wq_ref[...]
    )
    rel_ref[...] = rel.astype(BF)


def unpack_kernel(got_ref, dq_ref, dk_ref, dv_ref, dwq_ref, dwk_ref):
    base_w = TILE + TILE // 2
    base_b = base_w + dwk_ref.shape[0]
    for g in range(got_ref.shape[0] // 2):
        cols = slice(2 * g * HD, 2 * (g + 1) * HD)
        two = [got_ref[2 * g], got_ref[2 * g + 1]]
        dq_ref[:, cols] = jnp.concatenate(
            [
                jnp.concatenate([one[TILE:base_w, :HD], one[TILE:base_w, HD:]], 0)
                for one in two
            ],
            1,
        )
        dk_ref[:, cols] = jnp.concatenate([one[:TILE, :HD] for one in two], 1)
        dv_ref[:, cols] = jnp.concatenate([one[:TILE, HD:] for one in two], 1)
        dwk_ref[:, cols] = jnp.concatenate([one[base_w:base_b, :HD] for one in two], 1).astype(F32)
        dwq_ref[:, cols] = jnp.concatenate([one[base_w:base_b, HD:] for one in two], 1).astype(F32)


VMEM = pl.BlockSpec(memory_space=pltpu.VMEM)
SMEM = pl.BlockSpec(memory_space=pltpu.SMEM)
HBM = pl.BlockSpec(memory_space=pltpu.HBM)


def whole_call(kernel, inputs, outputs, scratch=(), scalars=0, source=VMEM, target=VMEM, limit=48):
    return pl.pallas_call(
        kernel,
        out_shape=outputs,
        in_specs=[SMEM] * scalars + [source] * (len(inputs) - scalars),
        out_specs=jax.tree.map(lambda _: target, outputs),
        scratch_shapes=list(scratch),
        compiler_params=pltpu.CompilerParams(vmem_limit_bytes=limit << 20),
    )(*inputs)


def head_body(queries, keys, values, out_grad, rel_emb, w_query, w_key, doc_lengths, bucket_table):
    tokens_dev, width = queries.shape
    heads = width // HD
    seq_count = lax.axis_size("seq")
    seq_index = lax.axis_index("seq")
    buckets, depth = rel_emb.shape
    halo = bucket_table.shape[0] // 2 // TILE
    span = 2 * halo + 1
    mine = seq_index // 2
    half = lax.rem(seq_index, 2).astype(jnp.int32).reshape(1)
    halves = [list(range(0, seq_count, 2)), list(range(1, seq_count, 2))]
    partners = [(i, i ^ 1) for i in range(seq_count)]
    shape = jax.ShapeDtypeStruct
    vm = pltpu.VMEM

    def spread(pieces):
        return lax.all_to_all(pieces, "seq", 0, 0, axis_index_groups=halves, tiled=True)

    packed = whole_call(
        pack_kernel,
        (queries, out_grad, keys, values),
        shape((heads, tokens_dev, 4 * HD), BF),
        [
            vm((4, tokens_dev, width), BF),
            vm((heads, tokens_dev, 4 * HD), BF),
            pltpu.SemaphoreType.DMA((4,)),
            pltpu.SemaphoreType.DMA((heads,)),
        ],
        source=HBM,
        target=HBM,
        limit=64,
    )
    own = spread(packed)
    w_own = jnp.concatenate(
        [
            lax.dynamic_slice_in_dim(w_key, mine * HD, HD, 1),
            lax.dynamic_slice_in_dim(w_query, mine * HD, HD, 1),
        ],
        1,
    )
    pos = nn(rel_emb, w_own).astype(BF)
    table = jnp.flip(bucket_table).reshape(1, -1)
    w_rows, b_rows = depth // seq_count, buckets // seq_count
    rows = TILE + TILE // 2 + w_rows + b_rows
    line = 2 * span * TILE
    scalars = jnp.concatenate([doc_lengths, half])
    onehot, expanded = whole_call(
        table_kernel,
        (scalars, pos, table),
        [shape((buckets, table.shape[1]), BF), shape((2 * HD, table.shape[1]), BF)],
        scalars=1,
    )
    other = lax.ppermute(
        whole_call(cut_kernel, (own, expanded), shape((heads, tokens_dev, 2 * HD), BF)),
        "seq",
        partners,
    )
    sent, kept, bucket, query = whole_call(
        head_kernel,
        (scalars, own, other, onehot, expanded),
        [
            shape((heads * TILE + buckets, 2 * HD), BF),
            shape((heads, TILE, 2 * HD), F32),
            shape((buckets, 2 * HD), BF),
            shape((heads, TILE // 2, 2 * HD), BF),
        ],
        [
            vm((HD, line), BF),
            vm((HD, line), BF),
            vm((seq_count, TILE, 2 * HD), BF),
            vm((seq_count, TILE, 2 * HD), F32),
            vm((seq_count, HD, TILE), F32),
            vm((HD, line), F32),
            vm((HD, line), F32),
            vm((seq_count, HD, TILE), BF),
            vm((seq_count, HD, TILE), BF),
            vm((TILE, (span + 1) * TILE), F32),
            vm((span, TILE, TILE), F32),
            vm((span, TILE, TILE), F32),
            vm((TILE, (span + 1) * TILE), BF),
            vm((span, TILE, 2 * TILE), BF),
            vm((heads, HD, TILE), F32),
            vm((heads, HD, TILE), F32),
        ],
        scalars=1,
    )
    came = lax.ppermute(sent, "seq", partners)
    joined = whole_call(
        join_kernel,
        (half, kept, bucket, query, came, rel_emb),
        shape((heads, rows, 2 * HD), BF),
        [vm((depth, 2 * HD), F32), vm((buckets, 2 * HD), F32)],
        scalars=1,
    )
    returned = spread(joined)
    rel_rows = whole_call(
        rel_kernel, (returned, w_key, w_query), shape((b_rows, depth), BF)
    )
    tokens = shape((tokens_dev, width), BF)
    weights = shape((w_rows, width), F32)
    head_index = lax.axis_index("head")
    mine_rel = lax.dynamic_slice_in_dim(rel_rows, head_index * width, width, 1)
    far_rel = lax.dynamic_slice_in_dim(rel_rows, (1 - head_index) * width, width, 1)
    far_rel = lax.ppermute(far_rel, "head", [(0, 1), (1, 0)])
    rel_own = (mine_rel.astype(F32) + far_rel.astype(F32)).astype(BF)
    near = spread(jnp.broadcast_to(rel_own[None], (heads, b_rows, width)))
    far = lax.ppermute(near, "seq", partners)
    rel_emb_grad = whole_call(
        weave_kernel, (half, near, far), shape((buckets, width), F32), scalars=1
    )
    query_grad, key_grad, value_grad, w_query_grad, w_key_grad = whole_call(
        unpack_kernel, (returned,), [tokens, tokens, tokens, weights, weights]
    )
    return (query_grad, key_grad, value_grad, rel_emb_grad, w_query_grad, w_key_grad)


def fits_heads(mesh, queries, rel_emb, bucket_table):
    seq, head = mesh.shape["seq"], mesh.shape["head"]
    heads = queries.shape[1] // HD // head
    return (
        head == 2
        and seq == 2 * heads
        and heads % 2 == 0
        and queries.shape[0] == seq * TILE
        and bucket_table.shape[0] % (2 * TILE) == 0
        and seq >= bucket_table.shape[0] // TILE + 1
        and rel_emb.shape[0] % (16 * seq) == 0
        and rel_emb.shape[1] % (16 * seq) == 0
        and rel_emb.shape[0] % TILE == 0
    )


def solution(mesh):
    in_specs = (
        P("seq", "head"),
        P("seq", "head"),
        P("seq", "head"),
        P("seq", "head"),
        P(),
        P(None, "head"),
        P(None, "head"),
        P(),
        P(),
    )
    out_specs = (
        P("seq", "head"),
        P("seq", "head"),
        P("seq", "head"),
        P(None, "head"),
        P("seq", "head"),
        P("seq", "head"),
    )

    def run(queries, keys, values, out_grad, rel_emb, w_query, w_key, doc_lengths, bucket_table):
        chosen = head_body if fits_heads(mesh, queries, rel_emb, bucket_table) else body
        return jax.shard_map(
            chosen, mesh=mesh, in_specs=in_specs, out_specs=out_specs, check_vma=False
        )(queries, keys, values, out_grad, rel_emb, w_query, w_key, doc_lengths, bucket_table)

    return run
```

```python
import math

import jax
import jax.numpy as jnp
from jax import lax
from jax.experimental import pallas as pl
from jax.experimental.pallas import tpu as pltpu
from jax.sharding import PartitionSpec as P

HD = 64
SPAN = 4
TILE = 128
SPANS = (2, 3, 4, 5, 6, 7)
BF = jnp.bfloat16
F32 = jnp.float32


masked_score = -1e30


def shifted(block, axis, distance):
    devices = range(lax.axis_size(axis))
    route = [(i - distance, i) for i in devices if i - distance in devices]
    return lax.ppermute(block, axis, route)


def contract(left, right, left_dim, right_dim):
    return lax.dot_general(
        left, right, (((left_dim,), (right_dim,)), ((), ())), preferred_element_type=jnp.float32
    )


def doc_index(position, doc_ends, extent):
    inside = (position >= 0) & (position < extent)
    owner = jnp.sum((doc_ends[None, :] <= position[:, None]).astype(jnp.int32), axis=1)
    return jnp.where(inside, owner, -1)


def same_document(row_pos, col_pos, doc_ends, extent):
    return (
        doc_index(row_pos, doc_ends, extent)[:, None]
        == doc_index(col_pos, doc_ends, extent)[None, :]
    )


def tile_tables(bucket_table, shift, rows, buckets):
    offset_span = bucket_table.shape[0] // 2
    spread = jnp.arange(2 * rows - 1, dtype=jnp.int32) - (rows - 1)
    ahead_index = bucket_table[jnp.clip(shift - spread + offset_span, 0, 2 * offset_span - 1)]
    behind_index = bucket_table[jnp.clip(offset_span - shift - spread, 0, 2 * offset_span - 1)]
    bucket_ids = jnp.arange(buckets, dtype=jnp.int32)[None, :]
    ahead_onehot = (ahead_index[:, None] == bucket_ids).astype(jnp.bfloat16)
    behind_onehot = (behind_index[:, None] == bucket_ids).astype(jnp.bfloat16)
    return (ahead_index, behind_index, ahead_onehot, behind_onehot)


def skew_in(spread, width):
    rows = spread.shape[0]
    line = rows + width - 1
    flat = jnp.pad(spread, ((0, 0), (0, 1))).reshape(-1)
    return flat[rows - 1 : rows - 1 + rows * line].reshape(rows, line)[:, :width]


def skew_out(dense):
    rows, width = dense.shape
    line = rows + width - 1
    padded = jnp.pad(dense, ((0, 0), (0, rows - 1))).reshape(-1)
    flat = jnp.pad(padded, (rows - 1, 1))
    return flat.reshape(rows, line + 1)[:, :line]


def tile_scores(
    query_rows, key_rows, pos_keys, pos_queries, ahead_onehot, behind_onehot, score_scale
):
    content = contract(query_rows, key_rows, 1, 1)
    ahead_band = contract(ahead_onehot, pos_keys, 1, 0).astype(jnp.bfloat16)
    behind_band = contract(behind_onehot, pos_queries, 1, 0).astype(jnp.bfloat16)
    query_term = skew_in(contract(query_rows, ahead_band, 1, 1), key_rows.shape[0])
    key_term = skew_in(contract(key_rows, behind_band, 1, 1), query_rows.shape[0]).T
    return score_scale * (content + query_term + key_term)


def query_side(
    query_rows,
    key_rows,
    value_rows,
    grad_rows,
    pos_keys,
    pos_queries,
    same_doc,
    tables,
    score_scale,
):
    tile_rows = query_rows.shape[0]
    tile_count = key_rows.shape[0] // tile_rows
    pieces = []
    for tile in range(tile_count):
        key_tile = key_rows[tile * tile_rows : (tile + 1) * tile_rows]
        pieces.append(
            tile_scores(
                query_rows,
                key_tile,
                pos_keys,
                pos_queries,
                tables[tile][2],
                tables[tile][3],
                score_scale,
            )
        )
    scores = jnp.where(same_doc, jnp.concatenate(pieces, 1), masked_score)
    row_max = jnp.max(scores, axis=1, keepdims=True)
    expd = jnp.where(same_doc, jnp.exp(scores - row_max), 0.0)
    row_sum = jnp.sum(expd, axis=1, keepdims=True)
    probs = expd / row_sum
    dprobs = contract(grad_rows, value_rows, 1, 1)
    row_dot = jnp.sum(probs * dprobs, axis=1, keepdims=True)
    dscores = probs * (dprobs - row_dot)
    dscores_low = dscores.astype(jnp.bfloat16)
    ahead_grad = jnp.zeros((tile_rows, pos_keys.shape[0]), jnp.float32)
    for tile in range(tile_count):
        band = dscores_low[:, tile * tile_rows : (tile + 1) * tile_rows]
        ahead_grad = ahead_grad + contract(skew_out(band), tables[tile][2], 1, 0)
    ahead_low = ahead_grad.astype(jnp.bfloat16)
    query_grad = score_scale * (
        contract(dscores_low, key_rows, 1, 0) + contract(ahead_low, pos_keys, 1, 0)
    )
    bucket_key = score_scale * contract(ahead_low, query_rows, 0, 0)
    probs_low = probs.astype(jnp.bfloat16)
    behind_parts = []
    for tile in range(tile_count):
        band = dscores_low[:, tile * tile_rows : (tile + 1) * tile_rows]
        behind_parts.append(contract(skew_out(band.T), tables[tile][3], 1, 0).astype(jnp.bfloat16))
    behind_low = jnp.concatenate(behind_parts, 0)
    key_grad = score_scale * (
        contract(dscores_low, query_rows, 0, 0) + contract(behind_low, pos_queries, 1, 0)
    )
    value_grad = contract(probs_low, grad_rows, 0, 0)
    bucket_query = score_scale * contract(behind_low, key_rows, 0, 0)
    return (query_grad, key_grad, value_grad, bucket_key, bucket_query)


def split_heads(matrix):
    return matrix.reshape(matrix.shape[0], matrix.shape[1] // HD, HD).transpose(1, 0, 2)


def join_heads(stacked):
    return stacked.transpose(1, 0, 2).reshape(stacked.shape[1], stacked.shape[0] * HD)


def body(queries, keys, values, out_grad, rel_emb, w_query, w_key, doc_lengths, bucket_table):
    tokens_dev = queries.shape[0]
    seq_count = lax.axis_size("seq")
    neighbours = min(SPAN, seq_count // 4)
    extent = tokens_dev * seq_count
    seq_index = lax.axis_index("seq")
    first_token = seq_index * tokens_dev
    score_scale = 1.0 / math.sqrt(3.0 * HD)
    pos_key = jnp.dot(rel_emb, w_key, preferred_element_type=jnp.float32).astype(jnp.bfloat16)
    pos_query = jnp.dot(rel_emb, w_query, preferred_element_type=jnp.float32).astype(jnp.bfloat16)
    doc_ends = jnp.cumsum(doc_lengths)
    buckets = rel_emb.shape[0]
    tables = [
        tile_tables(bucket_table, (neighbours - tile) * tokens_dev, tokens_dev, buckets)
        for tile in range(2 * neighbours + 1)
    ]
    hop_list = list(range(neighbours, 0, -1)) + list(range(-1, -neighbours - 1, -1))
    fetched = []
    for distance in hop_list:
        fetched.append(shifted((keys, values), "seq", distance))
    lower_side = fetched[:neighbours]
    upper_side = fetched[neighbours:]
    key_window = jnp.concatenate(
        [pair[0] for pair in lower_side] + [keys] + [pair[0] for pair in upper_side], 0
    )
    value_window = jnp.concatenate(
        [pair[1] for pair in lower_side] + [values] + [pair[1] for pair in upper_side], 0
    )
    window = key_window.shape[0]
    query_pos = first_token + jnp.arange(tokens_dev, dtype=jnp.int32)
    window_pos = first_token - neighbours * tokens_dev + jnp.arange(window, dtype=jnp.int32)
    same_doc = same_document(query_pos, window_pos, doc_ends, extent)
    query_heads = split_heads(queries)
    grad_heads = split_heads(out_grad)
    pos_key_heads = split_heads(pos_key)
    pos_query_heads = split_heads(pos_query)

    def every_pair(operands):
        query_rows, key_rows, value_rows, grad_rows, pos_keys, pos_queries = operands
        return query_side(
            query_rows,
            key_rows,
            value_rows,
            grad_rows,
            pos_keys,
            pos_queries,
            same_doc,
            tables,
            score_scale,
        )

    query_grad, key_part, value_part, bucket_key, bucket_query = lax.map(
        every_pair,
        (
            query_heads,
            split_heads(key_window),
            split_heads(value_window),
            grad_heads,
            pos_key_heads,
            pos_query_heads,
        ),
    )
    key_flat = join_heads(key_part)
    value_flat = join_heads(value_part)
    key_total = key_flat[neighbours * tokens_dev : (neighbours + 1) * tokens_dev]
    value_total = value_flat[neighbours * tokens_dev : (neighbours + 1) * tokens_dev]
    for distance in hop_list:
        segment = neighbours - distance
        returned = (
            key_flat[segment * tokens_dev : (segment + 1) * tokens_dev],
            value_flat[segment * tokens_dev : (segment + 1) * tokens_dev],
        )
        arrived = shifted((returned[0], returned[1]), "seq", -distance)
        key_total = key_total + arrived[0]
        value_total = value_total + arrived[1]
    key_grad = key_total.astype(jnp.bfloat16)
    value_grad = value_total.astype(jnp.bfloat16)
    query_out = join_heads(query_grad).astype(jnp.bfloat16)
    summed = lax.psum((join_heads(bucket_key), join_heads(bucket_query)), "seq")
    bucket_key_low = summed[0].astype(jnp.bfloat16)
    bucket_query_low = summed[1].astype(jnp.bfloat16)
    rows_dev = rel_emb.shape[1] // seq_count
    rel_columns = lax.dynamic_slice_in_dim(rel_emb, seq_index * rows_dev, rows_dev, 1)
    w_key_grad = contract(rel_columns, bucket_key_low, 0, 0)
    w_query_grad = contract(rel_columns, bucket_query_low, 0, 0)
    rel_partial = contract(bucket_key_low, w_key, 1, 1) + contract(bucket_query_low, w_query, 1, 1)
    rel_emb_grad = lax.psum_scatter(
        rel_partial.astype(jnp.bfloat16), "head", scatter_dimension=1, tiled=True
    ).astype(jnp.float32)
    return (query_out, key_grad, value_grad, rel_emb_grad, w_query_grad, w_key_grad)


def nn(left, right):
    return contract(left, right, 1, 0)


def nt(left, right):
    return contract(left, right, 1, 1)


def grid_of(shape):
    return (
        lax.broadcasted_iota(jnp.int32, shape, 0),
        lax.broadcasted_iota(jnp.int32, shape, 1),
    )


def pack_kernel(q_ref, g_ref, k_ref, v_ref, out_ref, held, pieces, came, left):
    heads = out_ref.shape[0]
    wide = 2 * HD
    loads = []
    for g in range(heads // 2):
        cols = pl.ds(g * wide, wide)
        loads.append(
            [
                pltpu.make_async_copy(ref.at[:, cols], held.at[i, :, cols], came.at[g, i])
                for i, ref in enumerate((q_ref, g_ref, k_ref, v_ref))
            ]
        )
        for load in loads[g]:
            load.start()
    stores = []
    for g in range(heads // 2):
        for load in loads[g]:
            load.wait()
        for head in (2 * g, 2 * g + 1):
            cols = slice(head * HD, (head + 1) * HD)
            pieces[head] = jnp.concatenate([held[i, :, cols] for i in range(4)], 1)
        two = pl.ds(2 * g, 2)
        stores.append(pltpu.make_async_copy(pieces.at[two], out_ref.at[two], left.at[g]))
        stores[g].start()
    for store in stores:
        store.wait()


def table_kernel(scalars_ref, pos_ref, table_ref, onehot, expanded):
    buckets, valid = onehot.shape
    for part in range(buckets // TILE):
        ids = lax.broadcasted_iota(jnp.int32, (TILE, valid), 0) + part * TILE
        onehot[pl.ds(part * TILE, TILE), :] = jnp.where(ids == table_ref[...], 1.0, 0.0).astype(BF)
    pos_t = pos_ref[...].astype(F32).T.astype(BF)
    expanded[...] = nn(pos_t, onehot[...]).astype(BF)


def cut_kernel(own_ref, expanded, out_ref):
    out_ref[...] = own_ref[:, :, 2 * HD :]


def head_kernel(
    scalars_ref, own_ref, other_ref, onehot, expanded,
    send_ref, keep_ref, bucket_ref, query_ref,
    pk, pq, kvs, acc, acc_pos, g_key, g_query, k_t, k_rev, s_q, st, dp, dtile, pairs, dq_nat, dq_pos,
):
    blocks = own_ref.shape[0]
    tiles = 2 * blocks
    buckets, valid = onehot.shape
    halo = valid // 2 // TILE
    longest = 2 * halo + 1
    scale = 1.0 / math.sqrt(3.0 * HD)
    valid0 = (halo + 1) * TILE
    docs = scalars_ref.shape[0] - 1
    half = scalars_ref[docs]
    row, col = grid_of((TILE, TILE))
    swap = jnp.where(row + col == TILE - 1, 1.0, 0.0).astype(BF)
    wrap = row + col >= TILE - 1
    keep = jnp.where(col >= row, 1.0, 0.0).astype(BF)
    low = col < HD
    for table, part in ((pk, expanded[:HD]), (pq, expanded[HD:])):
        table[...] = jnp.zeros_like(table)
        table[:, valid0 : valid0 + valid] = part
    acc[...] = jnp.zeros_like(acc)
    acc_pos[...] = jnp.zeros_like(acc_pos)
    g_key[...] = jnp.zeros_like(g_key)
    g_query[...] = jnp.zeros_like(g_query)

    for b in range(blocks):
        for kv, tile in (
            (own_ref[b, :, 2 * HD : 4 * HD], 2 * b + half),
            (other_ref[b], 2 * b + 1 - half),
        ):
            kvs[tile] = kv
            k_t[tile] = kv.astype(F32).T[:HD].astype(BF)
    k_rev[...] = (
        nn(k_t[...].reshape(tiles * HD, TILE), swap).astype(BF).reshape(tiles, HD, TILE)
    )

    def block(b, carry):
        own = 2 * b + half
        token = own * TILE

        def next_end(d, state):
            end, start, stop = state
            stop = jnp.where(end < token + TILE, end + scalars_ref[d], stop)
            end = end + scalars_ref[d]
            start = jnp.where(end <= token, end, start)
            return (end, start, stop)

        zero = jnp.int32(0)
        _, reach_low, reach_high = lax.fori_loop(
            0, docs, next_end, (zero, zero, zero), unroll=docs <= 16
        )
        lowest = reach_low // TILE
        count = (reach_high + TILE - 1) // TILE - lowest
        shorter = 0
        for span in SPANS:
            if span < longest:
                pl.when((count > shorter) & (count <= span))(
                    lambda span=span: work(b, own, lowest, span)
                )
                shorter = span
        pl.when(count > shorter)(lambda: work(b, own, lowest, longest))
        return carry

    def work(b, own, lowest, span):
        first = jnp.clip(lowest, 0, tiles - span)
        delta = (own - first) * TILE
        qd = own_ref[b, :, 0 : 2 * HD]
        turned = qd.astype(F32).T
        upper = row < HD
        right = jnp.concatenate(
            [jnp.where(upper, turned, 0.0), jnp.where(upper, 0.0, turned)], 1
        ).astype(BF)
        q_rev = nn(turned[:HD].astype(BF), swap).astype(BF)

        position = own * TILE + lax.broadcasted_iota(jnp.int32, (1, TILE), 1)

        def next_doc(d, state):
            end, start, stop = state
            stop = jnp.where(end <= position, end + scalars_ref[d], stop)
            end = end + scalars_ref[d]
            start = jnp.where(end <= position, end, start)
            return (end, start, stop)

        nothing = jnp.zeros((1, TILE), jnp.int32)
        _, start, stop = lax.fori_loop(
            0, docs, next_doc, (jnp.int32(0), nothing, nothing), unroll=docs <= 16
        )
        start = start - first * TILE
        stop = stop - first * TILE

        key_x = pl.multiple_of(halo * 2 * TILE - delta, TILE)
        s_q[:, 0 : (span + 1) * TILE] = nn(qd[:, :HD], pk[:, pl.ds(key_x, (span + 1) * TILE)])
        best = jnp.full((8, TILE), masked_score, F32)
        window_kv = kvs[pl.ds(first, span)].reshape(span * TILE, 2 * HD)
        contents = nn(window_kv, right)
        for t in range(span):
            kv = window_kv[t * TILE : (t + 1) * TILE]
            both = contents[t * TILE : (t + 1) * TILE]
            query_x = pl.multiple_of(2 * halo * TILE + delta - t * TILE, TILE)
            s_k = nn(kv[:, :HD], pq[:, pl.ds(query_x, 2 * TILE)])
            key_term = pltpu.roll(
                jnp.where(wrap, s_k[:, :TILE], s_k[:, TILE:]), 1, 1, stride=1, stride_axis=0
            )
            query_term = pltpu.roll(
                jnp.where(
                    wrap,
                    s_q[:, t * TILE : (t + 1) * TILE],
                    s_q[:, (t + 1) * TILE : (t + 2) * TILE],
                ),
                1,
                1,
                stride=1,
                stride_axis=0,
            )
            score = both[:, :TILE] + key_term + query_term.T
            inside = (row >= start - t * TILE) & (row < stop - t * TILE)
            score = jnp.where(inside, score, masked_score)
            st[t] = score
            dp[t] = both[:, TILE:]
            best = jnp.maximum(best, jnp.max(score.reshape(TILE // 8, 8, TILE), 0))
        top = jnp.max(best, 0, keepdims=True)
        total = jnp.zeros((8, TILE), F32)
        dot = jnp.zeros((8, TILE), F32)
        for t in range(span):
            expd = jnp.exp2((st[t] - top) * (scale * math.log2(math.e)))
            st[t] = expd
            total = total + jnp.sum(expd.reshape(TILE // 8, 8, TILE), 0)
            dot = dot + jnp.sum((expd * dp[t]).reshape(TILE // 8, 8, TILE), 0)
        inverse = 1.0 / jnp.sum(total, 0, keepdims=True)
        row_dot = jnp.sum(dot, 0, keepdims=True) * inverse

        lows = jnp.where(low, qd, jnp.zeros_like(qd))
        pair = jnp.concatenate([lows, jnp.where(low, jnp.zeros_like(qd), qd)], 0)
        dq_t = jnp.zeros((HD, TILE), F32)
        before = jnp.zeros((TILE, TILE), BF)
        near = held = None
        for t in range(span):
            prob = st[t] * inverse
            dscore = (prob * (dp[t] - row_dot)).astype(BF)
            pairs[t] = jnp.concatenate([dscore, prob.astype(BF)], 1)
            stacked = nn(
                jnp.concatenate([k_t[first + t], swap], 0),
                jnp.concatenate([dscore, dscore.T], 1),
            )
            dq_t = dq_t + stacked[:HD, :TILE]
            query_x = pl.multiple_of(2 * halo * TILE + delta - t * TILE, TILE)
            y = pltpu.roll(stacked[HD:, :TILE], 0, 1, stride=1, stride_axis=0).astype(BF)
            last = near
            near = y * keep
            far = y - near
            g_query[:, pl.ds(query_x, 2 * TILE)] += nn(
                k_rev[first + t], jnp.concatenate([near, far], 1)
            )
            chunk = pq[:, pl.ds(query_x + TILE, TILE)]
            if t == 0:
                held = nt(chunk, far)
            else:
                back = nt(chunk, jnp.concatenate([last, far], 0))
                acc_pos[first + t - 1] += held + back[:, :TILE]
                held = back[:, TILE:]
            z = pltpu.roll(stacked[HD:, TILE:], 0, 1, stride=1, stride_axis=0).astype(BF)
            here = z * keep
            dtile[:, t * TILE : (t + 1) * TILE] = here + before
            before = z - here
        acc_pos[first + span - 1] += held + nt(pq[:, pl.ds(query_x, TILE)], near)
        acc[pl.ds(first, span)] += nn(
            pairs[0:span].reshape(span * TILE, 2 * TILE), pair
        ).reshape(span, TILE, 2 * HD)
        dtile[:, span * TILE : (span + 1) * TILE] = before
        spread_q = dtile[:, 0 : (span + 1) * TILE]
        window = pl.ds(key_x, (span + 1) * TILE)
        g_key[:, window] += nn(q_rev, spread_q)
        dq_pos[b] = nt(pk[:, window], spread_q)
        dq_nat[b] = dq_t

    lax.fori_loop(0, blocks, block, 0)

    parts = []
    for g in (g_key, g_query):
        band = g[:, valid0 : valid0 + valid]
        high = band.astype(BF)
        parts += [high, (band - high.astype(F32)).astype(BF)]
    summed = nt(jnp.concatenate(parts, 0), onehot[...])
    bucket_t = scale * jnp.concatenate(
        [summed[:HD] + summed[HD : 2 * HD], summed[2 * HD : 3 * HD] + summed[3 * HD :]], 0
    )
    bucket = bucket_t.T.astype(BF)
    bucket_ref[...] = bucket
    send_ref[blocks * TILE :, :] = bucket
    factor = jnp.where(low, scale, 1.0)

    def unreverse(ref):
        part = ref[...].reshape(ref.shape[0] * HD, TILE)
        high = part.astype(BF)
        low_part = (part - high.astype(F32)).astype(BF)
        ref[...] = (nn(high, swap) + nn(low_part, swap)).reshape(ref.shape)

    unreverse(acc_pos)
    unreverse(dq_pos)

    def gradients(tile):
        extra = acc_pos[tile].T
        extra = jnp.concatenate([extra, jnp.zeros_like(extra)], 1)
        return (acc[tile] + extra) * factor

    for b in range(blocks):
        keep_ref[b] = gradients(2 * b + half)
        send_ref[b * TILE : (b + 1) * TILE, :] = gradients(2 * b + 1 - half).astype(BF)
        grad = scale * (dq_nat[b] + dq_pos[b]).T
        query_ref[b] = jnp.concatenate([grad[: TILE // 2], grad[TILE // 2 :]], 1).astype(BF)


def join_kernel(half_ref, keep_ref, bucket_ref, query_ref, came_ref, rel_ref, out_ref, weight, bucket):
    blocks = keep_ref.shape[0]
    tiles = 2 * blocks
    half = half_ref[0]
    w_rows = weight.shape[0] // tiles
    b_rows = bucket.shape[0] // tiles
    base_w = TILE + TILE // 2
    base_b = base_w + w_rows
    total = bucket_ref[...].astype(F32) + came_ref[blocks * TILE :, :].astype(F32)
    bucket[...] = total
    weight[...] = nn(total.T.astype(BF), rel_ref[...]).T
    for b in range(blocks):
        came = came_ref[b * TILE : (b + 1) * TILE, :].astype(F32)
        tile = 2 * b + half
        out_ref[b, 0:TILE, :] = (keep_ref[b] + came).astype(BF)
        out_ref[b, TILE:base_w, :] = query_ref[b]
        out_ref[b, base_w:base_b, :] = weight[pl.ds(tile * w_rows, w_rows), :].astype(BF)
        out_ref[b, base_b:, :] = bucket[pl.ds(tile * b_rows, b_rows), :].astype(BF)


def weave_kernel(half_ref, near_ref, far_ref, out_ref):
    shards, rows, _ = near_ref.shape
    half = half_ref[0]
    for shard in range(shards):
        for ref, place in ((near_ref, half), (far_ref, 1 - half)):
            start = pl.multiple_of((2 * shard + place) * rows, rows)
            out_ref[pl.ds(start, rows), :] = ref[shard].astype(F32)


def rel_kernel(side_ref, got_ref, wk_ref, wq_ref, kept_ref, away_ref):
    heads = range(got_ref.shape[0])
    rows, width = kept_ref.shape
    base_b = got_ref.shape[1] - rows
    rel = nt(jnp.concatenate([got_ref[h, base_b:, :HD] for h in heads], 1), wk_ref[...]) + nt(
        jnp.concatenate([got_ref[h, base_b:, HD:] for h in heads], 1), wq_ref[...]
    )
    left, right = rel[:, :width], rel[:, width:]
    first = jnp.full(left.shape, side_ref[0], jnp.int32) == 0
    kept_ref[...] = jnp.where(first, left, right).astype(BF)
    away_ref[...] = jnp.where(first, right, left).astype(BF)


def total_kernel(kept_ref, came_ref, after_ref, out_ref):
    total = (kept_ref[...].astype(F32) + came_ref[...].astype(F32)).astype(BF)
    for shard in range(out_ref.shape[0]):
        out_ref[shard] = total


def unpack_kernel(got_ref, dq_ref, dk_ref, dv_ref, dwq_ref, dwk_ref, done_ref):
    done_ref[...] = jnp.zeros_like(done_ref)
    base_w = TILE + TILE // 2
    base_b = base_w + dwk_ref.shape[0]
    for g in range(got_ref.shape[0] // 2):
        cols = slice(2 * g * HD, 2 * (g + 1) * HD)
        two = [got_ref[2 * g], got_ref[2 * g + 1]]
        dq_ref[:, cols] = jnp.concatenate(
            [
                jnp.concatenate([one[TILE:base_w, :HD], one[TILE:base_w, HD:]], 0)
                for one in two
            ],
            1,
        )
        dk_ref[:, cols] = jnp.concatenate([one[:TILE, :HD] for one in two], 1)
        dv_ref[:, cols] = jnp.concatenate([one[:TILE, HD:] for one in two], 1)
        dwk_ref[:, cols] = jnp.concatenate([one[base_w:base_b, :HD] for one in two], 1).astype(F32)
        dwq_ref[:, cols] = jnp.concatenate([one[base_w:base_b, HD:] for one in two], 1).astype(F32)


VMEM = pl.BlockSpec(memory_space=pltpu.VMEM)
SMEM = pl.BlockSpec(memory_space=pltpu.SMEM)
HBM = pl.BlockSpec(memory_space=pltpu.HBM)


def whole_call(kernel, inputs, outputs, scratch=(), scalars=0, source=VMEM, target=VMEM, limit=48):
    return pl.pallas_call(
        kernel,
        out_shape=outputs,
        in_specs=[SMEM] * scalars + [source] * (len(inputs) - scalars),
        out_specs=jax.tree.map(lambda _: target, outputs),
        scratch_shapes=list(scratch),
        compiler_params=pltpu.CompilerParams(vmem_limit_bytes=limit << 20),
    )(*inputs)


def head_body(queries, keys, values, out_grad, rel_emb, w_query, w_key, doc_lengths, bucket_table):
    tokens_dev, width = queries.shape
    heads = width // HD
    seq_count = lax.axis_size("seq")
    seq_index = lax.axis_index("seq")
    buckets, depth = rel_emb.shape
    halo = bucket_table.shape[0] // 2 // TILE
    span = 2 * halo + 1
    mine = seq_index // 2
    half = lax.rem(seq_index, 2).astype(jnp.int32).reshape(1)
    halves = [list(range(0, seq_count, 2)), list(range(1, seq_count, 2))]
    partners = [(i, i ^ 1) for i in range(seq_count)]
    shape = jax.ShapeDtypeStruct
    vm = pltpu.VMEM

    def spread(pieces):
        return lax.all_to_all(pieces, "seq", 0, 0, axis_index_groups=halves, tiled=True)

    packed = whole_call(
        pack_kernel,
        (queries, out_grad, keys, values),
        shape((heads, tokens_dev, 4 * HD), BF),
        [
            vm((4, tokens_dev, width), BF),
            vm((heads, tokens_dev, 4 * HD), BF),
            pltpu.SemaphoreType.DMA((heads // 2, 4)),
            pltpu.SemaphoreType.DMA((heads // 2,)),
        ],
        source=HBM,
        target=HBM,
        limit=64,
    )
    own = spread(packed)
    w_own = jnp.concatenate(
        [
            lax.dynamic_slice_in_dim(w_key, mine * HD, HD, 1),
            lax.dynamic_slice_in_dim(w_query, mine * HD, HD, 1),
        ],
        1,
    )
    pos = nn(rel_emb, w_own).astype(BF)
    table = jnp.flip(bucket_table).reshape(1, -1)
    w_rows, b_rows = depth // seq_count, buckets // seq_count
    rows = TILE + TILE // 2 + w_rows + b_rows
    line = 2 * span * TILE
    scalars = jnp.concatenate([doc_lengths, half])
    onehot, expanded = whole_call(
        table_kernel,
        (scalars, pos, table),
        [shape((buckets, table.shape[1]), BF), shape((2 * HD, table.shape[1]), BF)],
        scalars=1,
    )
    other = lax.ppermute(
        whole_call(cut_kernel, (own, expanded), shape((heads, tokens_dev, 2 * HD), BF)),
        "seq",
        partners,
    )
    sent, kept, bucket, query = whole_call(
        head_kernel,
        (scalars, own, other, onehot, expanded),
        [
            shape((heads * TILE + buckets, 2 * HD), BF),
            shape((heads, TILE, 2 * HD), F32),
            shape((buckets, 2 * HD), BF),
            shape((heads, TILE // 2, 2 * HD), BF),
        ],
        [
            vm((HD, line), BF),
            vm((HD, line), BF),
            vm((seq_count, TILE, 2 * HD), BF),
            vm((seq_count, TILE, 2 * HD), F32),
            vm((seq_count, HD, TILE), F32),
            vm((HD, line), F32),
            vm((HD, line), F32),
            vm((seq_count, HD, TILE), BF),
            vm((seq_count, HD, TILE), BF),
            vm((TILE, (span + 1) * TILE), F32),
            vm((span, TILE, TILE), F32),
            vm((span, TILE, TILE), F32),
            vm((TILE, (span + 1) * TILE), BF),
            vm((span, TILE, 2 * TILE), BF),
            vm((heads, HD, TILE), F32),
            vm((heads, HD, TILE), F32),
        ],
        scalars=1,
    )
    came = lax.ppermute(sent, "seq", partners)
    joined = whole_call(
        join_kernel,
        (half, kept, bucket, query, came, rel_emb),
        shape((heads, rows, 2 * HD), BF),
        [vm((depth, 2 * HD), F32), vm((buckets, 2 * HD), F32)],
        scalars=1,
    )
    returned = spread(joined)
    side = lax.axis_index("head").astype(jnp.int32).reshape(1)
    rel_half = shape((b_rows, width), BF)
    kept_rel, away_rel = whole_call(
        rel_kernel, (side, returned, w_key, w_query), [rel_half, rel_half], scalars=1
    )
    came_rel = lax.ppermute(away_rel, "head", [(0, 1), (1, 0)])
    tokens = shape((tokens_dev, width), BF)
    weights = shape((w_rows, width), F32)
    query_grad, key_grad, value_grad, w_query_grad, w_key_grad, done = whole_call(
        unpack_kernel,
        (returned,),
        [tokens, tokens, tokens, weights, weights, shape((8, TILE), F32)],
    )
    totals = whole_call(
        total_kernel, (kept_rel, came_rel, done), shape((heads, b_rows, width), BF)
    )
    near = spread(totals)
    far = lax.ppermute(near, "seq", partners)
    rel_emb_grad = whole_call(
        weave_kernel, (half, near, far), shape((buckets, width), F32), scalars=1
    )
    return (query_grad, key_grad, value_grad, rel_emb_grad, w_query_grad, w_key_grad)


def fits_heads(mesh, queries, rel_emb, bucket_table):
    seq, head = mesh.shape["seq"], mesh.shape["head"]
    heads = queries.shape[1] // HD // head
    return (
        head == 2
        and seq == 2 * heads
        and heads % 2 == 0
        and queries.shape[0] == seq * TILE
        and bucket_table.shape[0] % (2 * TILE) == 0
        and seq >= bucket_table.shape[0] // TILE + 1
        and rel_emb.shape[0] % (16 * seq) == 0
        and rel_emb.shape[1] % (16 * seq) == 0
        and rel_emb.shape[0] % TILE == 0
    )


def solution(mesh):
    in_specs = (
        P("seq", "head"),
        P("seq", "head"),
        P("seq", "head"),
        P("seq", "head"),
        P(),
        P(None, "head"),
        P(None, "head"),
        P(),
        P(),
    )
    out_specs = (
        P("seq", "head"),
        P("seq", "head"),
        P("seq", "head"),
        P(None, "head"),
        P("seq", "head"),
        P("seq", "head"),
    )

    def run(queries, keys, values, out_grad, rel_emb, w_query, w_key, doc_lengths, bucket_table):
        chosen = head_body if fits_heads(mesh, queries, rel_emb, bucket_table) else body
        return jax.shard_map(
            chosen, mesh=mesh, in_specs=in_specs, out_specs=out_specs, check_vma=False
        )(queries, keys, values, out_grad, rel_emb, w_query, w_key, doc_lengths, bucket_table)

    return run
```

```python
import math

import jax
import jax.numpy as jnp
from jax import lax
from jax.experimental import pallas as pl
from jax.experimental.pallas import tpu as pltpu
from jax.sharding import PartitionSpec as P

HD = 64
SPAN = 4
TILE = 128
SPANS = (2, 3, 4, 5, 6, 7)
BF = jnp.bfloat16
F32 = jnp.float32


masked_score = -1e30


def shifted(block, axis, distance):
    devices = range(lax.axis_size(axis))
    route = [(i - distance, i) for i in devices if i - distance in devices]
    return lax.ppermute(block, axis, route)


def contract(left, right, left_dim, right_dim):
    return lax.dot_general(
        left, right, (((left_dim,), (right_dim,)), ((), ())), preferred_element_type=jnp.float32
    )


def doc_index(position, doc_ends, extent):
    inside = (position >= 0) & (position < extent)
    owner = jnp.sum((doc_ends[None, :] <= position[:, None]).astype(jnp.int32), axis=1)
    return jnp.where(inside, owner, -1)


def same_document(row_pos, col_pos, doc_ends, extent):
    return (
        doc_index(row_pos, doc_ends, extent)[:, None]
        == doc_index(col_pos, doc_ends, extent)[None, :]
    )


def tile_tables(bucket_table, shift, rows, buckets):
    offset_span = bucket_table.shape[0] // 2
    spread = jnp.arange(2 * rows - 1, dtype=jnp.int32) - (rows - 1)
    ahead_index = bucket_table[jnp.clip(shift - spread + offset_span, 0, 2 * offset_span - 1)]
    behind_index = bucket_table[jnp.clip(offset_span - shift - spread, 0, 2 * offset_span - 1)]
    bucket_ids = jnp.arange(buckets, dtype=jnp.int32)[None, :]
    ahead_onehot = (ahead_index[:, None] == bucket_ids).astype(jnp.bfloat16)
    behind_onehot = (behind_index[:, None] == bucket_ids).astype(jnp.bfloat16)
    return (ahead_index, behind_index, ahead_onehot, behind_onehot)


def skew_in(spread, width):
    rows = spread.shape[0]
    line = rows + width - 1
    flat = jnp.pad(spread, ((0, 0), (0, 1))).reshape(-1)
    return flat[rows - 1 : rows - 1 + rows * line].reshape(rows, line)[:, :width]


def skew_out(dense):
    rows, width = dense.shape
    line = rows + width - 1
    padded = jnp.pad(dense, ((0, 0), (0, rows - 1))).reshape(-1)
    flat = jnp.pad(padded, (rows - 1, 1))
    return flat.reshape(rows, line + 1)[:, :line]


def tile_scores(
    query_rows, key_rows, pos_keys, pos_queries, ahead_onehot, behind_onehot, score_scale
):
    content = contract(query_rows, key_rows, 1, 1)
    ahead_band = contract(ahead_onehot, pos_keys, 1, 0).astype(jnp.bfloat16)
    behind_band = contract(behind_onehot, pos_queries, 1, 0).astype(jnp.bfloat16)
    query_term = skew_in(contract(query_rows, ahead_band, 1, 1), key_rows.shape[0])
    key_term = skew_in(contract(key_rows, behind_band, 1, 1), query_rows.shape[0]).T
    return score_scale * (content + query_term + key_term)


def query_side(
    query_rows,
    key_rows,
    value_rows,
    grad_rows,
    pos_keys,
    pos_queries,
    same_doc,
    tables,
    score_scale,
):
    tile_rows = query_rows.shape[0]
    tile_count = key_rows.shape[0] // tile_rows
    pieces = []
    for tile in range(tile_count):
        key_tile = key_rows[tile * tile_rows : (tile + 1) * tile_rows]
        pieces.append(
            tile_scores(
                query_rows,
                key_tile,
                pos_keys,
                pos_queries,
                tables[tile][2],
                tables[tile][3],
                score_scale,
            )
        )
    scores = jnp.where(same_doc, jnp.concatenate(pieces, 1), masked_score)
    row_max = jnp.max(scores, axis=1, keepdims=True)
    expd = jnp.where(same_doc, jnp.exp(scores - row_max), 0.0)
    row_sum = jnp.sum(expd, axis=1, keepdims=True)
    probs = expd / row_sum
    dprobs = contract(grad_rows, value_rows, 1, 1)
    row_dot = jnp.sum(probs * dprobs, axis=1, keepdims=True)
    dscores = probs * (dprobs - row_dot)
    dscores_low = dscores.astype(jnp.bfloat16)
    ahead_grad = jnp.zeros((tile_rows, pos_keys.shape[0]), jnp.float32)
    for tile in range(tile_count):
        band = dscores_low[:, tile * tile_rows : (tile + 1) * tile_rows]
        ahead_grad = ahead_grad + contract(skew_out(band), tables[tile][2], 1, 0)
    ahead_low = ahead_grad.astype(jnp.bfloat16)
    query_grad = score_scale * (
        contract(dscores_low, key_rows, 1, 0) + contract(ahead_low, pos_keys, 1, 0)
    )
    bucket_key = score_scale * contract(ahead_low, query_rows, 0, 0)
    probs_low = probs.astype(jnp.bfloat16)
    behind_parts = []
    for tile in range(tile_count):
        band = dscores_low[:, tile * tile_rows : (tile + 1) * tile_rows]
        behind_parts.append(contract(skew_out(band.T), tables[tile][3], 1, 0).astype(jnp.bfloat16))
    behind_low = jnp.concatenate(behind_parts, 0)
    key_grad = score_scale * (
        contract(dscores_low, query_rows, 0, 0) + contract(behind_low, pos_queries, 1, 0)
    )
    value_grad = contract(probs_low, grad_rows, 0, 0)
    bucket_query = score_scale * contract(behind_low, key_rows, 0, 0)
    return (query_grad, key_grad, value_grad, bucket_key, bucket_query)


def split_heads(matrix):
    return matrix.reshape(matrix.shape[0], matrix.shape[1] // HD, HD).transpose(1, 0, 2)


def join_heads(stacked):
    return stacked.transpose(1, 0, 2).reshape(stacked.shape[1], stacked.shape[0] * HD)


def body(queries, keys, values, out_grad, rel_emb, w_query, w_key, doc_lengths, bucket_table):
    tokens_dev = queries.shape[0]
    seq_count = lax.axis_size("seq")
    neighbours = min(SPAN, seq_count // 4)
    extent = tokens_dev * seq_count
    seq_index = lax.axis_index("seq")
    first_token = seq_index * tokens_dev
    score_scale = 1.0 / math.sqrt(3.0 * HD)
    pos_key = jnp.dot(rel_emb, w_key, preferred_element_type=jnp.float32).astype(jnp.bfloat16)
    pos_query = jnp.dot(rel_emb, w_query, preferred_element_type=jnp.float32).astype(jnp.bfloat16)
    doc_ends = jnp.cumsum(doc_lengths)
    buckets = rel_emb.shape[0]
    tables = [
        tile_tables(bucket_table, (neighbours - tile) * tokens_dev, tokens_dev, buckets)
        for tile in range(2 * neighbours + 1)
    ]
    hop_list = list(range(neighbours, 0, -1)) + list(range(-1, -neighbours - 1, -1))
    fetched = []
    for distance in hop_list:
        fetched.append(shifted((keys, values), "seq", distance))
    lower_side = fetched[:neighbours]
    upper_side = fetched[neighbours:]
    key_window = jnp.concatenate(
        [pair[0] for pair in lower_side] + [keys] + [pair[0] for pair in upper_side], 0
    )
    value_window = jnp.concatenate(
        [pair[1] for pair in lower_side] + [values] + [pair[1] for pair in upper_side], 0
    )
    window = key_window.shape[0]
    query_pos = first_token + jnp.arange(tokens_dev, dtype=jnp.int32)
    window_pos = first_token - neighbours * tokens_dev + jnp.arange(window, dtype=jnp.int32)
    same_doc = same_document(query_pos, window_pos, doc_ends, extent)
    query_heads = split_heads(queries)
    grad_heads = split_heads(out_grad)
    pos_key_heads = split_heads(pos_key)
    pos_query_heads = split_heads(pos_query)

    def every_pair(operands):
        query_rows, key_rows, value_rows, grad_rows, pos_keys, pos_queries = operands
        return query_side(
            query_rows,
            key_rows,
            value_rows,
            grad_rows,
            pos_keys,
            pos_queries,
            same_doc,
            tables,
            score_scale,
        )

    query_grad, key_part, value_part, bucket_key, bucket_query = lax.map(
        every_pair,
        (
            query_heads,
            split_heads(key_window),
            split_heads(value_window),
            grad_heads,
            pos_key_heads,
            pos_query_heads,
        ),
    )
    key_flat = join_heads(key_part)
    value_flat = join_heads(value_part)
    key_total = key_flat[neighbours * tokens_dev : (neighbours + 1) * tokens_dev]
    value_total = value_flat[neighbours * tokens_dev : (neighbours + 1) * tokens_dev]
    for distance in hop_list:
        segment = neighbours - distance
        returned = (
            key_flat[segment * tokens_dev : (segment + 1) * tokens_dev],
            value_flat[segment * tokens_dev : (segment + 1) * tokens_dev],
        )
        arrived = shifted((returned[0], returned[1]), "seq", -distance)
        key_total = key_total + arrived[0]
        value_total = value_total + arrived[1]
    key_grad = key_total.astype(jnp.bfloat16)
    value_grad = value_total.astype(jnp.bfloat16)
    query_out = join_heads(query_grad).astype(jnp.bfloat16)
    summed = lax.psum((join_heads(bucket_key), join_heads(bucket_query)), "seq")
    bucket_key_low = summed[0].astype(jnp.bfloat16)
    bucket_query_low = summed[1].astype(jnp.bfloat16)
    rows_dev = rel_emb.shape[1] // seq_count
    rel_columns = lax.dynamic_slice_in_dim(rel_emb, seq_index * rows_dev, rows_dev, 1)
    w_key_grad = contract(rel_columns, bucket_key_low, 0, 0)
    w_query_grad = contract(rel_columns, bucket_query_low, 0, 0)
    rel_partial = contract(bucket_key_low, w_key, 1, 1) + contract(bucket_query_low, w_query, 1, 1)
    rel_emb_grad = lax.psum_scatter(
        rel_partial.astype(jnp.bfloat16), "head", scatter_dimension=1, tiled=True
    ).astype(jnp.float32)
    return (query_out, key_grad, value_grad, rel_emb_grad, w_query_grad, w_key_grad)


def nn(left, right):
    return contract(left, right, 1, 0)


def nt(left, right):
    return contract(left, right, 1, 1)


def grid_of(shape):
    return (
        lax.broadcasted_iota(jnp.int32, shape, 0),
        lax.broadcasted_iota(jnp.int32, shape, 1),
    )


def pack_kernel(q_ref, g_ref, k_ref, v_ref, out_ref, held, pieces, came, left):
    heads = out_ref.shape[0]
    wide = 2 * HD
    loads = []
    for g in range(heads // 2):
        cols = pl.ds(g * wide, wide)
        loads.append(
            [
                pltpu.make_async_copy(ref.at[:, cols], held.at[i, :, cols], came.at[g, i])
                for i, ref in enumerate((q_ref, g_ref, k_ref, v_ref))
            ]
        )
        for load in loads[g]:
            load.start()
    stores = []
    for g in range(heads // 2):
        for load in loads[g]:
            load.wait()
        for head in (2 * g, 2 * g + 1):
            cols = slice(head * HD, (head + 1) * HD)
            pieces[head] = jnp.concatenate([held[i, :, cols] for i in range(4)], 1)
        two = pl.ds(2 * g, 2)
        stores.append(pltpu.make_async_copy(pieces.at[two], out_ref.at[two], left.at[g]))
        stores[g].start()
    for store in stores:
        store.wait()


def table_kernel(scalars_ref, pos_ref, table_ref, onehot, expanded):
    buckets, valid = onehot.shape
    for part in range(buckets // TILE):
        ids = lax.broadcasted_iota(jnp.int32, (TILE, valid), 0) + part * TILE
        onehot[pl.ds(part * TILE, TILE), :] = jnp.where(ids == table_ref[...], 1.0, 0.0).astype(BF)
    pos_t = pos_ref[...].astype(F32).T.astype(BF)
    expanded[...] = nn(pos_t, onehot[...]).astype(BF)


def cut_kernel(own_ref, expanded, out_ref):
    out_ref[...] = own_ref[:, :, 2 * HD :]


def head_kernel(
    scalars_ref, own_ref, other_ref, onehot, expanded,
    send_ref, keep_ref, bucket_ref, query_ref,
    pk, pq, kvs, acc, acc_pos, g_key, g_query, k_t, k_rev, s_q, st, both, turns, dtile, pairs, moves, spreads, dq_nat, dq_pos,
):
    blocks = own_ref.shape[0]
    tiles = 2 * blocks
    buckets, valid = onehot.shape
    halo = valid // 2 // TILE
    longest = 2 * halo + 1
    scale = 1.0 / math.sqrt(3.0 * HD)
    valid0 = (halo + 1) * TILE
    docs = scalars_ref.shape[0] - 1
    half = scalars_ref[docs]
    row, col = grid_of((TILE, TILE))
    swap = jnp.where(row + col == TILE - 1, 1.0, 0.0).astype(BF)
    wrap = row + col >= TILE - 1
    keep = jnp.where(col >= row, 1.0, 0.0).astype(BF)
    low = col < HD
    for table, part in ((pk, expanded[:HD]), (pq, expanded[HD:])):
        table[...] = jnp.zeros_like(table)
        table[:, valid0 : valid0 + valid] = part
    acc[...] = jnp.zeros_like(acc)
    acc_pos[...] = jnp.zeros_like(acc_pos)
    g_key[...] = jnp.zeros_like(g_key)
    g_query[...] = jnp.zeros_like(g_query)

    for b in range(blocks):
        for kv, tile in (
            (own_ref[b, :, 2 * HD : 4 * HD], 2 * b + half),
            (other_ref[b], 2 * b + 1 - half),
        ):
            kvs[tile] = kv
            k_t[tile] = kv.astype(F32).T[:HD].astype(BF)
    k_rev[...] = (
        nn(k_t[...].reshape(tiles * HD, TILE), swap).astype(BF).reshape(tiles, HD, TILE)
    )

    def block(b, carry):
        own = 2 * b + half
        token = own * TILE

        def next_end(d, state):
            end, start, stop = state
            stop = jnp.where(end < token + TILE, end + scalars_ref[d], stop)
            end = end + scalars_ref[d]
            start = jnp.where(end <= token, end, start)
            return (end, start, stop)

        zero = jnp.int32(0)
        _, reach_low, reach_high = lax.fori_loop(
            0, docs, next_end, (zero, zero, zero), unroll=docs <= 16
        )
        lowest = reach_low // TILE
        count = (reach_high + TILE - 1) // TILE - lowest
        shorter = 0
        for span in SPANS:
            if span < longest:
                pl.when((count > shorter) & (count <= span))(
                    lambda span=span: work(b, own, lowest, span)
                )
                shorter = span
        pl.when(count > shorter)(lambda: work(b, own, lowest, longest))
        return carry

    def work(b, own, lowest, span):
        first = jnp.clip(lowest, 0, tiles - span)
        delta = (own - first) * TILE
        qd = own_ref[b, :, 0 : 2 * HD]
        turned = qd.astype(F32).T
        upper = row < HD
        right = jnp.concatenate(
            [jnp.where(upper, turned, 0.0), jnp.where(upper, 0.0, turned)], 1
        ).astype(BF)
        q_rev = nn(turned[:HD].astype(BF), swap).astype(BF)

        position = own * TILE + lax.broadcasted_iota(jnp.int32, (1, TILE), 1)

        def next_doc(d, state):
            end, start, stop = state
            stop = jnp.where(end <= position, end + scalars_ref[d], stop)
            end = end + scalars_ref[d]
            start = jnp.where(end <= position, end, start)
            return (end, start, stop)

        nothing = jnp.zeros((1, TILE), jnp.int32)
        _, start, stop = lax.fori_loop(
            0, docs, next_doc, (jnp.int32(0), nothing, nothing), unroll=docs <= 16
        )
        start = start - first * TILE
        stop = stop - first * TILE

        key_x = pl.multiple_of(halo * 2 * TILE - delta, TILE)
        s_q[:, 0 : (span + 1) * TILE] = nn(qd[:, :HD], pk[:, pl.ds(key_x, (span + 1) * TILE)])
        best = jnp.full((8, TILE), masked_score, F32)
        window_kv = kvs[pl.ds(first, span)].reshape(span * TILE, 2 * HD)
        both[0 : span * TILE, :] = nn(window_kv, right)

        def query_window(t):
            return pl.multiple_of(2 * halo * TILE + delta - t * TILE, TILE)

        for t in range(span):
            s_k = nn(
                window_kv[t * TILE : (t + 1) * TILE, :HD], pq[:, pl.ds(query_window(t), 2 * TILE)]
            )
            st[t] = jnp.where(wrap, s_k[:, :TILE], s_k[:, TILE:])
        for t in range(span):
            turns[t] = pltpu.roll(
                jnp.where(
                    wrap,
                    s_q[:, t * TILE : (t + 1) * TILE],
                    s_q[:, (t + 1) * TILE : (t + 2) * TILE],
                ),
                1,
                1,
                stride=1,
                stride_axis=0,
            )
        for t in range(span):
            key_term = pltpu.roll(st[t], 1, 1, stride=1, stride_axis=0)
            score = both[t * TILE : (t + 1) * TILE, :TILE] + key_term + turns[t].T
            inside = (row >= start - t * TILE) & (row < stop - t * TILE)
            score = jnp.where(inside, score, masked_score)
            st[t] = score
            best = jnp.maximum(best, jnp.max(score.reshape(TILE // 8, 8, TILE), 0))
        top = jnp.max(best, 0, keepdims=True)
        total = jnp.zeros((8, TILE), F32)
        dot = jnp.zeros((8, TILE), F32)
        for t in range(span):
            expd = jnp.exp2((st[t] - top) * (scale * math.log2(math.e)))
            st[t] = expd
            total = total + jnp.sum(expd.reshape(TILE // 8, 8, TILE), 0)
            dot = dot + jnp.sum((expd * both[t * TILE : (t + 1) * TILE, TILE:]).reshape(TILE // 8, 8, TILE), 0)
        inverse = 1.0 / jnp.sum(total, 0, keepdims=True)
        row_dot = jnp.sum(dot, 0, keepdims=True) * inverse

        lows = jnp.where(low, qd, jnp.zeros_like(qd))
        pair = jnp.concatenate([lows, jnp.where(low, jnp.zeros_like(qd), qd)], 0)
        for t in range(span):
            prob = st[t] * inverse
            dscore = (prob * (both[t * TILE : (t + 1) * TILE, TILE:] - row_dot)).astype(BF)
            pairs[t] = jnp.concatenate([dscore, prob.astype(BF)], 1)
            moves[t] = jnp.concatenate([dscore, dscore.T], 1)
        dq_t = jnp.zeros((HD, TILE), F32)
        for t in range(span):
            stacked = nn(jnp.concatenate([k_t[first + t], swap], 0), moves[t])
            dq_t = dq_t + stacked[:HD, :TILE]
            st[t] = stacked[HD:, :TILE]
            turns[t] = stacked[HD:, TILE:]
        before = jnp.zeros((TILE, TILE), BF)
        for t in range(span):
            y = pltpu.roll(st[t], 0, 1, stride=1, stride_axis=0).astype(BF)
            near = y * keep
            spreads[t] = jnp.concatenate([near, y - near], 1)
            z = pltpu.roll(turns[t], 0, 1, stride=1, stride_axis=0).astype(BF)
            here = z * keep
            dtile[:, t * TILE : (t + 1) * TILE] = here + before
            before = z - here
        held = None
        for t in range(span):
            query_x = query_window(t)
            g_query[:, pl.ds(query_x, 2 * TILE)] += nn(k_rev[first + t], spreads[t])
            chunk = pq[:, pl.ds(query_x + TILE, TILE)]
            if t == 0:
                held = nt(chunk, spreads[t, :, TILE:])
            else:
                back = nt(
                    chunk, jnp.concatenate([spreads[t - 1, :, :TILE], spreads[t, :, TILE:]], 0)
                )
                acc_pos[first + t - 1] += held + back[:, :TILE]
                held = back[:, TILE:]
        acc_pos[first + span - 1] += held + nt(
            pq[:, pl.ds(query_window(span - 1), TILE)], spreads[span - 1, :, :TILE]
        )
        acc[pl.ds(first, span)] += nn(
            pairs[0:span].reshape(span * TILE, 2 * TILE), pair
        ).reshape(span, TILE, 2 * HD)
        dtile[:, span * TILE : (span + 1) * TILE] = before
        spread_q = dtile[:, 0 : (span + 1) * TILE]
        window = pl.ds(key_x, (span + 1) * TILE)
        g_key[:, window] += nn(q_rev, spread_q)
        dq_pos[b] = nt(pk[:, window], spread_q)
        dq_nat[b] = dq_t

    lax.fori_loop(0, blocks, block, 0)

    parts = []
    for g in (g_key, g_query):
        band = g[:, valid0 : valid0 + valid]
        high = band.astype(BF)
        parts += [high, (band - high.astype(F32)).astype(BF)]
    summed = nt(jnp.concatenate(parts, 0), onehot[...])
    bucket_t = scale * jnp.concatenate(
        [summed[:HD] + summed[HD : 2 * HD], summed[2 * HD : 3 * HD] + summed[3 * HD :]], 0
    )
    bucket = bucket_t.T.astype(BF)
    bucket_ref[...] = bucket
    send_ref[blocks * TILE :, :] = bucket
    factor = jnp.where(low, scale, 1.0)

    def unreverse(ref):
        part = ref[...].reshape(ref.shape[0] * HD, TILE)
        high = part.astype(BF)
        low_part = (part - high.astype(F32)).astype(BF)
        ref[...] = (nn(high, swap) + nn(low_part, swap)).reshape(ref.shape)

    unreverse(acc_pos)
    unreverse(dq_pos)

    def gradients(tile):
        extra = acc_pos[tile].T
        extra = jnp.concatenate([extra, jnp.zeros_like(extra)], 1)
        return (acc[tile] + extra) * factor

    for b in range(blocks):
        keep_ref[b] = gradients(2 * b + half)
        send_ref[b * TILE : (b + 1) * TILE, :] = gradients(2 * b + 1 - half).astype(BF)
        grad = scale * (dq_nat[b] + dq_pos[b]).T
        query_ref[b] = jnp.concatenate([grad[: TILE // 2], grad[TILE // 2 :]], 1).astype(BF)


def join_kernel(half_ref, keep_ref, bucket_ref, query_ref, came_ref, rel_ref, out_ref, weight, bucket):
    blocks = keep_ref.shape[0]
    tiles = 2 * blocks
    half = half_ref[0]
    w_rows = weight.shape[0] // tiles
    b_rows = bucket.shape[0] // tiles
    base_w = TILE + TILE // 2
    base_b = base_w + w_rows
    total = bucket_ref[...].astype(F32) + came_ref[blocks * TILE :, :].astype(F32)
    bucket[...] = total
    weight[...] = nn(total.T.astype(BF), rel_ref[...]).T
    for b in range(blocks):
        came = came_ref[b * TILE : (b + 1) * TILE, :].astype(F32)
        tile = 2 * b + half
        out_ref[b, 0:TILE, :] = (keep_ref[b] + came).astype(BF)
        out_ref[b, TILE:base_w, :] = query_ref[b]
        out_ref[b, base_w:base_b, :] = weight[pl.ds(tile * w_rows, w_rows), :].astype(BF)
        out_ref[b, base_b:, :] = bucket[pl.ds(tile * b_rows, b_rows), :].astype(BF)


def weave_kernel(half_ref, near_ref, far_ref, out_ref):
    shards, rows, _ = near_ref.shape
    half = half_ref[0]
    for shard in range(shards):
        for ref, place in ((near_ref, half), (far_ref, 1 - half)):
            start = pl.multiple_of((2 * shard + place) * rows, rows)
            out_ref[pl.ds(start, rows), :] = ref[shard].astype(F32)


def rel_kernel(side_ref, got_ref, wk_ref, wq_ref, kept_ref, away_ref):
    heads = range(got_ref.shape[0])
    rows, width = kept_ref.shape
    base_b = got_ref.shape[1] - rows
    rel = nt(jnp.concatenate([got_ref[h, base_b:, :HD] for h in heads], 1), wk_ref[...]) + nt(
        jnp.concatenate([got_ref[h, base_b:, HD:] for h in heads], 1), wq_ref[...]
    )
    left, right = rel[:, :width], rel[:, width:]
    first = jnp.full(left.shape, side_ref[0], jnp.int32) == 0
    kept_ref[...] = jnp.where(first, left, right).astype(BF)
    away_ref[...] = jnp.where(first, right, left).astype(BF)


def total_kernel(kept_ref, came_ref, after_ref, out_ref):
    total = (kept_ref[...].astype(F32) + came_ref[...].astype(F32)).astype(BF)
    for shard in range(out_ref.shape[0]):
        out_ref[shard] = total


def unpack_kernel(got_ref, dq_ref, dk_ref, dv_ref, dwq_ref, dwk_ref, done_ref):
    done_ref[...] = jnp.zeros_like(done_ref)
    base_w = TILE + TILE // 2
    base_b = base_w + dwk_ref.shape[0]
    for g in range(got_ref.shape[0] // 2):
        cols = slice(2 * g * HD, 2 * (g + 1) * HD)
        two = [got_ref[2 * g], got_ref[2 * g + 1]]
        dq_ref[:, cols] = jnp.concatenate(
            [
                jnp.concatenate([one[TILE:base_w, :HD], one[TILE:base_w, HD:]], 0)
                for one in two
            ],
            1,
        )
        dk_ref[:, cols] = jnp.concatenate([one[:TILE, :HD] for one in two], 1)
        dv_ref[:, cols] = jnp.concatenate([one[:TILE, HD:] for one in two], 1)
        dwk_ref[:, cols] = jnp.concatenate([one[base_w:base_b, :HD] for one in two], 1).astype(F32)
        dwq_ref[:, cols] = jnp.concatenate([one[base_w:base_b, HD:] for one in two], 1).astype(F32)


VMEM = pl.BlockSpec(memory_space=pltpu.VMEM)
SMEM = pl.BlockSpec(memory_space=pltpu.SMEM)
HBM = pl.BlockSpec(memory_space=pltpu.HBM)


def whole_call(kernel, inputs, outputs, scratch=(), scalars=0, source=VMEM, target=VMEM, limit=48):
    return pl.pallas_call(
        kernel,
        out_shape=outputs,
        in_specs=[SMEM] * scalars + [source] * (len(inputs) - scalars),
        out_specs=jax.tree.map(lambda _: target, outputs),
        scratch_shapes=list(scratch),
        compiler_params=pltpu.CompilerParams(vmem_limit_bytes=limit << 20),
    )(*inputs)


def head_body(queries, keys, values, out_grad, rel_emb, w_query, w_key, doc_lengths, bucket_table):
    tokens_dev, width = queries.shape
    heads = width // HD
    seq_count = lax.axis_size("seq")
    seq_index = lax.axis_index("seq")
    buckets, depth = rel_emb.shape
    halo = bucket_table.shape[0] // 2 // TILE
    span = 2 * halo + 1
    mine = seq_index // 2
    half = lax.rem(seq_index, 2).astype(jnp.int32).reshape(1)
    halves = [list(range(0, seq_count, 2)), list(range(1, seq_count, 2))]
    partners = [(i, i ^ 1) for i in range(seq_count)]
    shape = jax.ShapeDtypeStruct
    vm = pltpu.VMEM

    def spread(pieces):
        return lax.all_to_all(pieces, "seq", 0, 0, axis_index_groups=halves, tiled=True)

    packed = whole_call(
        pack_kernel,
        (queries, out_grad, keys, values),
        shape((heads, tokens_dev, 4 * HD), BF),
        [
            vm((4, tokens_dev, width), BF),
            vm((heads, tokens_dev, 4 * HD), BF),
            pltpu.SemaphoreType.DMA((heads // 2, 4)),
            pltpu.SemaphoreType.DMA((heads // 2,)),
        ],
        source=HBM,
        target=HBM,
        limit=64,
    )
    own = spread(packed)
    w_own = jnp.concatenate(
        [
            lax.dynamic_slice_in_dim(w_key, mine * HD, HD, 1),
            lax.dynamic_slice_in_dim(w_query, mine * HD, HD, 1),
        ],
        1,
    )
    pos = nn(rel_emb, w_own).astype(BF)
    table = jnp.flip(bucket_table).reshape(1, -1)
    w_rows, b_rows = depth // seq_count, buckets // seq_count
    rows = TILE + TILE // 2 + w_rows + b_rows
    line = 2 * span * TILE
    scalars = jnp.concatenate([doc_lengths, half])
    onehot, expanded = whole_call(
        table_kernel,
        (scalars, pos, table),
        [shape((buckets, table.shape[1]), BF), shape((2 * HD, table.shape[1]), BF)],
        scalars=1,
    )
    other = lax.ppermute(
        whole_call(cut_kernel, (own, expanded), shape((heads, tokens_dev, 2 * HD), BF)),
        "seq",
        partners,
    )
    sent, kept, bucket, query = whole_call(
        head_kernel,
        (scalars, own, other, onehot, expanded),
        [
            shape((heads * TILE + buckets, 2 * HD), BF),
            shape((heads, TILE, 2 * HD), F32),
            shape((buckets, 2 * HD), BF),
            shape((heads, TILE // 2, 2 * HD), BF),
        ],
        [
            vm((HD, line), BF),
            vm((HD, line), BF),
            vm((seq_count, TILE, 2 * HD), BF),
            vm((seq_count, TILE, 2 * HD), F32),
            vm((seq_count, HD, TILE), F32),
            vm((HD, line), F32),
            vm((HD, line), F32),
            vm((seq_count, HD, TILE), BF),
            vm((seq_count, HD, TILE), BF),
            vm((TILE, (span + 1) * TILE), F32),
            vm((span, TILE, TILE), F32),
            vm((span * TILE, 2 * TILE), F32),
            vm((span, TILE, TILE), F32),
            vm((TILE, (span + 1) * TILE), BF),
            vm((span, TILE, 2 * TILE), BF),
            vm((span, TILE, 2 * TILE), BF),
            vm((span, TILE, 2 * TILE), BF),
            vm((heads, HD, TILE), F32),
            vm((heads, HD, TILE), F32),
        ],
        scalars=1,
    )
    came = lax.ppermute(sent, "seq", partners)
    joined = whole_call(
        join_kernel,
        (half, kept, bucket, query, came, rel_emb),
        shape((heads, rows, 2 * HD), BF),
        [vm((depth, 2 * HD), F32), vm((buckets, 2 * HD), F32)],
        scalars=1,
    )
    returned = spread(joined)
    side = lax.axis_index("head").astype(jnp.int32).reshape(1)
    rel_half = shape((b_rows, width), BF)
    kept_rel, away_rel = whole_call(
        rel_kernel, (side, returned, w_key, w_query), [rel_half, rel_half], scalars=1
    )
    came_rel = lax.ppermute(away_rel, "head", [(0, 1), (1, 0)])
    tokens = shape((tokens_dev, width), BF)
    weights = shape((w_rows, width), F32)
    query_grad, key_grad, value_grad, w_query_grad, w_key_grad, done = whole_call(
        unpack_kernel,
        (returned,),
        [tokens, tokens, tokens, weights, weights, shape((8, TILE), F32)],
    )
    totals = whole_call(
        total_kernel, (kept_rel, came_rel, done), shape((heads, b_rows, width), BF)
    )
    near = spread(totals)
    far = lax.ppermute(near, "seq", partners)
    rel_emb_grad = whole_call(
        weave_kernel, (half, near, far), shape((buckets, width), F32), scalars=1
    )
    return (query_grad, key_grad, value_grad, rel_emb_grad, w_query_grad, w_key_grad)


def fits_heads(mesh, queries, rel_emb, bucket_table):
    seq, head = mesh.shape["seq"], mesh.shape["head"]
    heads = queries.shape[1] // HD // head
    return (
        head == 2
        and seq == 2 * heads
        and heads % 2 == 0
        and queries.shape[0] == seq * TILE
        and bucket_table.shape[0] % (2 * TILE) == 0
        and seq >= bucket_table.shape[0] // TILE + 1
        and rel_emb.shape[0] % (16 * seq) == 0
        and rel_emb.shape[1] % (16 * seq) == 0
        and rel_emb.shape[0] % TILE == 0
    )


def solution(mesh):
    in_specs = (
        P("seq", "head"),
        P("seq", "head"),
        P("seq", "head"),
        P("seq", "head"),
        P(),
        P(None, "head"),
        P(None, "head"),
        P(),
        P(),
    )
    out_specs = (
        P("seq", "head"),
        P("seq", "head"),
        P("seq", "head"),
        P(None, "head"),
        P("seq", "head"),
        P("seq", "head"),
    )

    def run(queries, keys, values, out_grad, rel_emb, w_query, w_key, doc_lengths, bucket_table):
        chosen = head_body if fits_heads(mesh, queries, rel_emb, bucket_table) else body
        return jax.shard_map(
            chosen, mesh=mesh, in_specs=in_specs, out_specs=out_specs, check_vma=False
        )(queries, keys, values, out_grad, rel_emb, w_query, w_key, doc_lengths, bucket_table)

    return run
```

```python
import math

import jax
import jax.numpy as jnp
from jax import lax
from jax.experimental import pallas as pl
from jax.experimental.pallas import tpu as pltpu
from jax.sharding import PartitionSpec as P

HD = 64
SPAN = 4
TILE = 128
SPANS = (2, 3, 4, 5, 6, 7)
BF = jnp.bfloat16
F32 = jnp.float32


masked_score = -1e30


def shifted(block, axis, distance):
    devices = range(lax.axis_size(axis))
    route = [(i - distance, i) for i in devices if i - distance in devices]
    return lax.ppermute(block, axis, route)


def contract(left, right, left_dim, right_dim):
    return lax.dot_general(
        left, right, (((left_dim,), (right_dim,)), ((), ())), preferred_element_type=jnp.float32
    )


def doc_index(position, doc_ends, extent):
    inside = (position >= 0) & (position < extent)
    owner = jnp.sum((doc_ends[None, :] <= position[:, None]).astype(jnp.int32), axis=1)
    return jnp.where(inside, owner, -1)


def same_document(row_pos, col_pos, doc_ends, extent):
    return (
        doc_index(row_pos, doc_ends, extent)[:, None]
        == doc_index(col_pos, doc_ends, extent)[None, :]
    )


def tile_tables(bucket_table, shift, rows, buckets):
    offset_span = bucket_table.shape[0] // 2
    spread = jnp.arange(2 * rows - 1, dtype=jnp.int32) - (rows - 1)
    ahead_index = bucket_table[jnp.clip(shift - spread + offset_span, 0, 2 * offset_span - 1)]
    behind_index = bucket_table[jnp.clip(offset_span - shift - spread, 0, 2 * offset_span - 1)]
    bucket_ids = jnp.arange(buckets, dtype=jnp.int32)[None, :]
    ahead_onehot = (ahead_index[:, None] == bucket_ids).astype(jnp.bfloat16)
    behind_onehot = (behind_index[:, None] == bucket_ids).astype(jnp.bfloat16)
    return (ahead_index, behind_index, ahead_onehot, behind_onehot)


def skew_in(spread, width):
    rows = spread.shape[0]
    line = rows + width - 1
    flat = jnp.pad(spread, ((0, 0), (0, 1))).reshape(-1)
    return flat[rows - 1 : rows - 1 + rows * line].reshape(rows, line)[:, :width]


def skew_out(dense):
    rows, width = dense.shape
    line = rows + width - 1
    padded = jnp.pad(dense, ((0, 0), (0, rows - 1))).reshape(-1)
    flat = jnp.pad(padded, (rows - 1, 1))
    return flat.reshape(rows, line + 1)[:, :line]


def tile_scores(
    query_rows, key_rows, pos_keys, pos_queries, ahead_onehot, behind_onehot, score_scale
):
    content = contract(query_rows, key_rows, 1, 1)
    ahead_band = contract(ahead_onehot, pos_keys, 1, 0).astype(jnp.bfloat16)
    behind_band = contract(behind_onehot, pos_queries, 1, 0).astype(jnp.bfloat16)
    query_term = skew_in(contract(query_rows, ahead_band, 1, 1), key_rows.shape[0])
    key_term = skew_in(contract(key_rows, behind_band, 1, 1), query_rows.shape[0]).T
    return score_scale * (content + query_term + key_term)


def query_side(
    query_rows,
    key_rows,
    value_rows,
    grad_rows,
    pos_keys,
    pos_queries,
    same_doc,
    tables,
    score_scale,
):
    tile_rows = query_rows.shape[0]
    tile_count = key_rows.shape[0] // tile_rows
    pieces = []
    for tile in range(tile_count):
        key_tile = key_rows[tile * tile_rows : (tile + 1) * tile_rows]
        pieces.append(
            tile_scores(
                query_rows,
                key_tile,
                pos_keys,
                pos_queries,
                tables[tile][2],
                tables[tile][3],
                score_scale,
            )
        )
    scores = jnp.where(same_doc, jnp.concatenate(pieces, 1), masked_score)
    row_max = jnp.max(scores, axis=1, keepdims=True)
    expd = jnp.where(same_doc, jnp.exp(scores - row_max), 0.0)
    row_sum = jnp.sum(expd, axis=1, keepdims=True)
    probs = expd / row_sum
    dprobs = contract(grad_rows, value_rows, 1, 1)
    row_dot = jnp.sum(probs * dprobs, axis=1, keepdims=True)
    dscores = probs * (dprobs - row_dot)
    dscores_low = dscores.astype(jnp.bfloat16)
    ahead_grad = jnp.zeros((tile_rows, pos_keys.shape[0]), jnp.float32)
    for tile in range(tile_count):
        band = dscores_low[:, tile * tile_rows : (tile + 1) * tile_rows]
        ahead_grad = ahead_grad + contract(skew_out(band), tables[tile][2], 1, 0)
    ahead_low = ahead_grad.astype(jnp.bfloat16)
    query_grad = score_scale * (
        contract(dscores_low, key_rows, 1, 0) + contract(ahead_low, pos_keys, 1, 0)
    )
    bucket_key = score_scale * contract(ahead_low, query_rows, 0, 0)
    probs_low = probs.astype(jnp.bfloat16)
    behind_parts = []
    for tile in range(tile_count):
        band = dscores_low[:, tile * tile_rows : (tile + 1) * tile_rows]
        behind_parts.append(contract(skew_out(band.T), tables[tile][3], 1, 0).astype(jnp.bfloat16))
    behind_low = jnp.concatenate(behind_parts, 0)
    key_grad = score_scale * (
        contract(dscores_low, query_rows, 0, 0) + contract(behind_low, pos_queries, 1, 0)
    )
    value_grad = contract(probs_low, grad_rows, 0, 0)
    bucket_query = score_scale * contract(behind_low, key_rows, 0, 0)
    return (query_grad, key_grad, value_grad, bucket_key, bucket_query)


def split_heads(matrix):
    return matrix.reshape(matrix.shape[0], matrix.shape[1] // HD, HD).transpose(1, 0, 2)


def join_heads(stacked):
    return stacked.transpose(1, 0, 2).reshape(stacked.shape[1], stacked.shape[0] * HD)


def body(queries, keys, values, out_grad, rel_emb, w_query, w_key, doc_lengths, bucket_table):
    tokens_dev = queries.shape[0]
    seq_count = lax.axis_size("seq")
    neighbours = min(SPAN, seq_count // 4)
    extent = tokens_dev * seq_count
    seq_index = lax.axis_index("seq")
    first_token = seq_index * tokens_dev
    score_scale = 1.0 / math.sqrt(3.0 * HD)
    pos_key = jnp.dot(rel_emb, w_key, preferred_element_type=jnp.float32).astype(jnp.bfloat16)
    pos_query = jnp.dot(rel_emb, w_query, preferred_element_type=jnp.float32).astype(jnp.bfloat16)
    doc_ends = jnp.cumsum(doc_lengths)
    buckets = rel_emb.shape[0]
    tables = [
        tile_tables(bucket_table, (neighbours - tile) * tokens_dev, tokens_dev, buckets)
        for tile in range(2 * neighbours + 1)
    ]
    hop_list = list(range(neighbours, 0, -1)) + list(range(-1, -neighbours - 1, -1))
    fetched = []
    for distance in hop_list:
        fetched.append(shifted((keys, values), "seq", distance))
    lower_side = fetched[:neighbours]
    upper_side = fetched[neighbours:]
    key_window = jnp.concatenate(
        [pair[0] for pair in lower_side] + [keys] + [pair[0] for pair in upper_side], 0
    )
    value_window = jnp.concatenate(
        [pair[1] for pair in lower_side] + [values] + [pair[1] for pair in upper_side], 0
    )
    window = key_window.shape[0]
    query_pos = first_token + jnp.arange(tokens_dev, dtype=jnp.int32)
    window_pos = first_token - neighbours * tokens_dev + jnp.arange(window, dtype=jnp.int32)
    same_doc = same_document(query_pos, window_pos, doc_ends, extent)
    query_heads = split_heads(queries)
    grad_heads = split_heads(out_grad)
    pos_key_heads = split_heads(pos_key)
    pos_query_heads = split_heads(pos_query)

    def every_pair(operands):
        query_rows, key_rows, value_rows, grad_rows, pos_keys, pos_queries = operands
        return query_side(
            query_rows,
            key_rows,
            value_rows,
            grad_rows,
            pos_keys,
            pos_queries,
            same_doc,
            tables,
            score_scale,
        )

    query_grad, key_part, value_part, bucket_key, bucket_query = lax.map(
        every_pair,
        (
            query_heads,
            split_heads(key_window),
            split_heads(value_window),
            grad_heads,
            pos_key_heads,
            pos_query_heads,
        ),
    )
    key_flat = join_heads(key_part)
    value_flat = join_heads(value_part)
    key_total = key_flat[neighbours * tokens_dev : (neighbours + 1) * tokens_dev]
    value_total = value_flat[neighbours * tokens_dev : (neighbours + 1) * tokens_dev]
    for distance in hop_list:
        segment = neighbours - distance
        returned = (
            key_flat[segment * tokens_dev : (segment + 1) * tokens_dev],
            value_flat[segment * tokens_dev : (segment + 1) * tokens_dev],
        )
        arrived = shifted((returned[0], returned[1]), "seq", -distance)
        key_total = key_total + arrived[0]
        value_total = value_total + arrived[1]
    key_grad = key_total.astype(jnp.bfloat16)
    value_grad = value_total.astype(jnp.bfloat16)
    query_out = join_heads(query_grad).astype(jnp.bfloat16)
    summed = lax.psum((join_heads(bucket_key), join_heads(bucket_query)), "seq")
    bucket_key_low = summed[0].astype(jnp.bfloat16)
    bucket_query_low = summed[1].astype(jnp.bfloat16)
    rows_dev = rel_emb.shape[1] // seq_count
    rel_columns = lax.dynamic_slice_in_dim(rel_emb, seq_index * rows_dev, rows_dev, 1)
    w_key_grad = contract(rel_columns, bucket_key_low, 0, 0)
    w_query_grad = contract(rel_columns, bucket_query_low, 0, 0)
    rel_partial = contract(bucket_key_low, w_key, 1, 1) + contract(bucket_query_low, w_query, 1, 1)
    rel_emb_grad = lax.psum_scatter(
        rel_partial.astype(jnp.bfloat16), "head", scatter_dimension=1, tiled=True
    ).astype(jnp.float32)
    return (query_out, key_grad, value_grad, rel_emb_grad, w_query_grad, w_key_grad)


def nn(left, right):
    return contract(left, right, 1, 0)


def nt(left, right):
    return contract(left, right, 1, 1)


def grid_of(shape):
    return (
        lax.broadcasted_iota(jnp.int32, shape, 0),
        lax.broadcasted_iota(jnp.int32, shape, 1),
    )


def pack_kernel(q_ref, g_ref, k_ref, v_ref, out_ref, held, pieces, came, left):
    heads = out_ref.shape[0]
    wide = 2 * HD
    loads = []
    for g in range(heads // 2):
        cols = pl.ds(g * wide, wide)
        loads.append(
            [
                pltpu.make_async_copy(ref.at[:, cols], held.at[i, :, cols], came.at[g, i])
                for i, ref in enumerate((q_ref, g_ref, k_ref, v_ref))
            ]
        )
        for load in loads[g]:
            load.start()
    stores = []
    for g in range(heads // 2):
        for load in loads[g]:
            load.wait()
        for head in (2 * g, 2 * g + 1):
            cols = slice(head * HD, (head + 1) * HD)
            pieces[head] = jnp.concatenate([held[i, :, cols] for i in range(4)], 1)
        two = pl.ds(2 * g, 2)
        stores.append(pltpu.make_async_copy(pieces.at[two], out_ref.at[two], left.at[g]))
        stores[g].start()
    for store in stores:
        store.wait()


def table_kernel(scalars_ref, pos_ref, table_ref, onehot, expanded):
    buckets, valid = onehot.shape
    for part in range(buckets // TILE):
        ids = lax.broadcasted_iota(jnp.int32, (TILE, valid), 0) + part * TILE
        onehot[pl.ds(part * TILE, TILE), :] = jnp.where(ids == table_ref[...], 1.0, 0.0).astype(BF)
    pos_t = pos_ref[...].astype(F32).T.astype(BF)
    expanded[...] = nn(pos_t, onehot[...]).astype(BF)


def cut_kernel(own_ref, expanded, out_ref):
    out_ref[...] = own_ref[:, :, 2 * HD :]


def head_kernel(
    scalars_ref, own_ref, other_ref, onehot, expanded,
    send_ref, keep_ref, bucket_ref, query_ref,
    pk, pq, kvs, acc, acc_pos, g_key, g_query, k_t, s_q, st, dp, dtile, pairs, dq_nat, dq_pos,
):
    blocks = own_ref.shape[0]
    tiles = 2 * blocks
    buckets, valid = onehot.shape
    halo = valid // 2 // TILE
    longest = 2 * halo + 1
    scale = 1.0 / math.sqrt(3.0 * HD)
    valid0 = (halo + 1) * TILE
    docs = scalars_ref.shape[0] - 1
    half = scalars_ref[docs]
    row, col = grid_of((TILE, TILE))
    swap = jnp.where(row + col == TILE - 1, 1.0, 0.0).astype(BF)
    wrap = row + col >= TILE - 1
    keep = jnp.where(col >= row, 1.0, 0.0).astype(BF)
    keep_keys = jnp.where(wrap, 1.0, 0.0).astype(BF)
    low = col < HD
    for table, part in ((pk, expanded[:HD]), (pq, expanded[HD:])):
        table[...] = jnp.zeros_like(table)
        table[:, valid0 : valid0 + valid] = part
    acc[...] = jnp.zeros_like(acc)
    acc_pos[...] = jnp.zeros_like(acc_pos)
    g_key[...] = jnp.zeros_like(g_key)
    g_query[...] = jnp.zeros_like(g_query)

    for b in range(blocks):
        for kv, tile in (
            (own_ref[b, :, 2 * HD : 4 * HD], 2 * b + half),
            (other_ref[b], 2 * b + 1 - half),
        ):
            kvs[tile] = kv
            start = pl.multiple_of(tile * TILE, TILE)
            k_t[:, pl.ds(start, TILE)] = kv.astype(F32).T[:HD].astype(BF)

    def unskew(tile):
        moved = jnp.concatenate(
            [
                pltpu.roll(tile[r : r + 8], TILE - 8 - r, 1) if r < TILE - 8 else tile[r : r + 8]
                for r in range(0, TILE, 8)
            ],
            0,
        )
        for step in (4, 2, 1):
            moved = jnp.where((row & step) == 0, pltpu.roll(moved, step, 1), moved)
        return moved

    def block(b, carry):
        own = 2 * b + half
        token = own * TILE

        def next_end(d, state):
            end, start, stop = state
            stop = jnp.where(end < token + TILE, end + scalars_ref[d], stop)
            end = end + scalars_ref[d]
            start = jnp.where(end <= token, end, start)
            return (end, start, stop)

        zero = jnp.int32(0)
        _, reach_low, reach_high = lax.fori_loop(
            0, docs, next_end, (zero, zero, zero), unroll=docs <= 16
        )
        lowest = reach_low // TILE
        count = (reach_high + TILE - 1) // TILE - lowest
        shorter = 0
        for span in SPANS:
            if span < longest:
                pl.when((count > shorter) & (count <= span))(
                    lambda span=span: work(b, own, lowest, span)
                )
                shorter = span
        pl.when(count > shorter)(lambda: work(b, own, lowest, longest))
        return carry

    def work(b, own, lowest, span):
        first = jnp.clip(lowest, 0, tiles - span)
        delta = (own - first) * TILE
        qd = own_ref[b, :, 0 : 2 * HD]
        turned = qd.astype(F32).T
        upper = row < HD
        right = jnp.concatenate(
            [jnp.where(upper, turned, 0.0), jnp.where(upper, 0.0, turned)], 1
        ).astype(BF)
        q_rev = nn(turned[:HD].astype(BF), swap).astype(BF)

        position = own * TILE + lax.broadcasted_iota(jnp.int32, (1, TILE), 1)

        def next_doc(d, state):
            end, start, stop = state
            stop = jnp.where(end <= position, end + scalars_ref[d], stop)
            end = end + scalars_ref[d]
            start = jnp.where(end <= position, end, start)
            return (end, start, stop)

        nothing = jnp.zeros((1, TILE), jnp.int32)
        _, start, stop = lax.fori_loop(
            0, docs, next_doc, (jnp.int32(0), nothing, nothing), unroll=docs <= 16
        )
        start = start - first * TILE
        stop = stop - first * TILE

        key_x = pl.multiple_of(halo * 2 * TILE - delta, TILE)
        s_q[:, 0 : (span + 1) * TILE] = nn(qd[:, :HD], pk[:, pl.ds(key_x, (span + 1) * TILE)])
        best = jnp.full((8, TILE), masked_score, F32)
        window_kv = kvs[pl.ds(first, span)].reshape(span * TILE, 2 * HD)
        contents = nn(window_kv, right)
        for t in range(span):
            kv = window_kv[t * TILE : (t + 1) * TILE]
            both = contents[t * TILE : (t + 1) * TILE]
            query_x = pl.multiple_of(2 * halo * TILE + delta - t * TILE, TILE)
            s_k = nn(kv[:, :HD], pq[:, pl.ds(query_x, 2 * TILE)])
            key_term = pltpu.roll(
                jnp.where(wrap, s_k[:, :TILE], s_k[:, TILE:]), 1, 1, stride=1, stride_axis=0
            )
            query_term = pltpu.roll(
                jnp.where(
                    wrap,
                    s_q[:, t * TILE : (t + 1) * TILE],
                    s_q[:, (t + 1) * TILE : (t + 2) * TILE],
                ),
                1,
                1,
                stride=1,
                stride_axis=0,
            )
            score = both[:, :TILE] + key_term + query_term.T
            inside = (row >= start - t * TILE) & (row < stop - t * TILE)
            score = jnp.where(inside, score, masked_score)
            st[t] = score
            dp[t] = both[:, TILE:]
            best = jnp.maximum(best, jnp.max(score.reshape(TILE // 8, 8, TILE), 0))
        top = jnp.max(best, 0, keepdims=True)
        total = jnp.zeros((8, TILE), F32)
        dot = jnp.zeros((8, TILE), F32)
        for t in range(span):
            expd = jnp.exp2((st[t] - top) * (scale * math.log2(math.e)))
            st[t] = expd
            total = total + jnp.sum(expd.reshape(TILE // 8, 8, TILE), 0)
            dot = dot + jnp.sum((expd * dp[t]).reshape(TILE // 8, 8, TILE), 0)
        inverse = 1.0 / jnp.sum(total, 0, keepdims=True)
        row_dot = jnp.sum(dot, 0, keepdims=True) * inverse

        lows = jnp.where(low, qd, jnp.zeros_like(qd))
        pair = jnp.concatenate(
            [
                jnp.concatenate([lows, swap], 1),
                jnp.concatenate([qd - lows, jnp.zeros_like(swap)], 1),
            ],
            0,
        )
        near = held = None
        for t in range(span):
            prob = st[t] * inverse
            exact = prob * (dp[t] - row_dot)
            pairs[t] = jnp.concatenate([exact.astype(BF), prob.astype(BF)], 1)
            query_x = pl.multiple_of(2 * halo * TILE + delta - t * TILE, TILE)
            y = unskew(exact).astype(BF)
            last = near
            near = y * keep_keys
            far = y - near
            g_query[:, pl.ds(query_x, 2 * TILE)] += nn(
                k_t[:, pl.ds(pl.multiple_of((first + t) * TILE, TILE), TILE)],
                jnp.concatenate([near, far], 1),
            )
            chunk = pq[:, pl.ds(query_x + TILE, TILE)]
            if t == 0:
                held = nt(chunk, far)
            else:
                back = nt(chunk, jnp.concatenate([last, far], 0))
                acc_pos[first + t - 1] += held + back[:, :TILE]
                held = back[:, TILE:]
        acc_pos[first + span - 1] += held + nt(pq[:, pl.ds(query_x, TILE)], near)
        lines = span * TILE
        every = pairs[0:span].reshape(lines, 2 * TILE)
        result = nn(every, pair)
        acc[pl.ds(first, span)] += result[:, : 2 * HD].reshape(span, TILE, 2 * HD)
        keys_t = k_t[:, pl.ds(pl.multiple_of(first * TILE, TILE), lines)]
        dq_nat[b] = nn(keys_t, every[:, :TILE])
        before = jnp.zeros((TILE, TILE), BF)
        for t in range(span):
            turned = result[t * TILE : (t + 1) * TILE, 2 * HD :].T
            z = pltpu.roll(turned, 0, 1, stride=1, stride_axis=0).astype(BF)
            here = z * keep
            dtile[:, t * TILE : (t + 1) * TILE] = here + before
            before = z - here
        dtile[:, span * TILE : (span + 1) * TILE] = before
        spread_q = dtile[:, 0 : (span + 1) * TILE]
        window = pl.ds(key_x, (span + 1) * TILE)
        g_key[:, window] += nn(q_rev, spread_q)
        dq_pos[b] = nt(pk[:, window], spread_q)

    lax.fori_loop(0, blocks, block, 0)

    parts = []
    for g in (g_key, g_query):
        band = g[:, valid0 : valid0 + valid]
        high = band.astype(BF)
        parts += [high, (band - high.astype(F32)).astype(BF)]
    summed = nt(jnp.concatenate(parts, 0), onehot[...])
    bucket_t = scale * jnp.concatenate(
        [summed[:HD] + summed[HD : 2 * HD], summed[2 * HD : 3 * HD] + summed[3 * HD :]], 0
    )
    bucket = bucket_t.T.astype(BF)
    bucket_ref[...] = bucket
    send_ref[blocks * TILE :, :] = bucket
    factor = jnp.where(low, scale, 1.0)

    def unreverse(ref):
        part = ref[...].reshape(ref.shape[0] * HD, TILE)
        high = part.astype(BF)
        low_part = (part - high.astype(F32)).astype(BF)
        ref[...] = (nn(high, swap) + nn(low_part, swap)).reshape(ref.shape)

    unreverse(dq_pos)

    def gradients(tile):
        extra = acc_pos[tile].T
        extra = jnp.concatenate([extra, jnp.zeros_like(extra)], 1)
        return (acc[tile] + extra) * factor

    for b in range(blocks):
        keep_ref[b] = gradients(2 * b + half)
        send_ref[b * TILE : (b + 1) * TILE, :] = gradients(2 * b + 1 - half).astype(BF)
        grad = scale * (dq_nat[b] + dq_pos[b]).T
        query_ref[b] = jnp.concatenate([grad[: TILE // 2], grad[TILE // 2 :]], 1).astype(BF)


def join_kernel(half_ref, keep_ref, bucket_ref, query_ref, came_ref, rel_ref, out_ref, weight, bucket):
    blocks = keep_ref.shape[0]
    tiles = 2 * blocks
    half = half_ref[0]
    w_rows = weight.shape[0] // tiles
    b_rows = bucket.shape[0] // tiles
    base_w = TILE + TILE // 2
    base_b = base_w + w_rows
    total = bucket_ref[...].astype(F32) + came_ref[blocks * TILE :, :].astype(F32)
    bucket[...] = total
    weight[...] = nn(total.T.astype(BF), rel_ref[...]).T
    for b in range(blocks):
        came = came_ref[b * TILE : (b + 1) * TILE, :].astype(F32)
        tile = 2 * b + half
        out_ref[b, 0:TILE, :] = (keep_ref[b] + came).astype(BF)
        out_ref[b, TILE:base_w, :] = query_ref[b]
        out_ref[b, base_w:base_b, :] = weight[pl.ds(tile * w_rows, w_rows), :].astype(BF)
        out_ref[b, base_b:, :] = bucket[pl.ds(tile * b_rows, b_rows), :].astype(BF)


def weave_kernel(half_ref, near_ref, far_ref, out_ref):
    shards, rows, _ = near_ref.shape
    half = half_ref[0]
    for shard in range(shards):
        for ref, place in ((near_ref, half), (far_ref, 1 - half)):
            start = pl.multiple_of((2 * shard + place) * rows, rows)
            out_ref[pl.ds(start, rows), :] = ref[shard].astype(F32)


def rel_kernel(side_ref, got_ref, wk_ref, wq_ref, kept_ref, away_ref):
    heads = range(got_ref.shape[0])
    rows, width = kept_ref.shape
    base_b = got_ref.shape[1] - rows
    rel = nt(jnp.concatenate([got_ref[h, base_b:, :HD] for h in heads], 1), wk_ref[...]) + nt(
        jnp.concatenate([got_ref[h, base_b:, HD:] for h in heads], 1), wq_ref[...]
    )
    left, right = rel[:, :width], rel[:, width:]
    first = jnp.full(left.shape, side_ref[0], jnp.int32) == 0
    kept_ref[...] = jnp.where(first, left, right).astype(BF)
    away_ref[...] = jnp.where(first, right, left).astype(BF)


def total_kernel(kept_ref, came_ref, after_ref, out_ref):
    total = (kept_ref[...].astype(F32) + came_ref[...].astype(F32)).astype(BF)
    for shard in range(out_ref.shape[0]):
        out_ref[shard] = total


def unpack_kernel(got_ref, dq_ref, dk_ref, dv_ref, dwq_ref, dwk_ref, done_ref):
    done_ref[...] = jnp.zeros_like(done_ref)
    base_w = TILE + TILE // 2
    base_b = base_w + dwk_ref.shape[0]
    for g in range(got_ref.shape[0] // 2):
        cols = slice(2 * g * HD, 2 * (g + 1) * HD)
        two = [got_ref[2 * g], got_ref[2 * g + 1]]
        dq_ref[:, cols] = jnp.concatenate(
            [
                jnp.concatenate([one[TILE:base_w, :HD], one[TILE:base_w, HD:]], 0)
                for one in two
            ],
            1,
        )
        dk_ref[:, cols] = jnp.concatenate([one[:TILE, :HD] for one in two], 1)
        dv_ref[:, cols] = jnp.concatenate([one[:TILE, HD:] for one in two], 1)
        dwk_ref[:, cols] = jnp.concatenate([one[base_w:base_b, :HD] for one in two], 1).astype(F32)
        dwq_ref[:, cols] = jnp.concatenate([one[base_w:base_b, HD:] for one in two], 1).astype(F32)


VMEM = pl.BlockSpec(memory_space=pltpu.VMEM)
SMEM = pl.BlockSpec(memory_space=pltpu.SMEM)
HBM = pl.BlockSpec(memory_space=pltpu.HBM)


def whole_call(kernel, inputs, outputs, scratch=(), scalars=0, source=VMEM, target=VMEM, limit=48):
    return pl.pallas_call(
        kernel,
        out_shape=outputs,
        in_specs=[SMEM] * scalars + [source] * (len(inputs) - scalars),
        out_specs=jax.tree.map(lambda _: target, outputs),
        scratch_shapes=list(scratch),
        compiler_params=pltpu.CompilerParams(vmem_limit_bytes=limit << 20),
    )(*inputs)


def head_body(queries, keys, values, out_grad, rel_emb, w_query, w_key, doc_lengths, bucket_table):
    tokens_dev, width = queries.shape
    heads = width // HD
    seq_count = lax.axis_size("seq")
    seq_index = lax.axis_index("seq")
    buckets, depth = rel_emb.shape
    halo = bucket_table.shape[0] // 2 // TILE
    span = 2 * halo + 1
    mine = seq_index // 2
    half = lax.rem(seq_index, 2).astype(jnp.int32).reshape(1)
    halves = [list(range(0, seq_count, 2)), list(range(1, seq_count, 2))]
    partners = [(i, i ^ 1) for i in range(seq_count)]
    shape = jax.ShapeDtypeStruct
    vm = pltpu.VMEM

    def spread(pieces):
        return lax.all_to_all(pieces, "seq", 0, 0, axis_index_groups=halves, tiled=True)

    packed = whole_call(
        pack_kernel,
        (queries, out_grad, keys, values),
        shape((heads, tokens_dev, 4 * HD), BF),
        [
            vm((4, tokens_dev, width), BF),
            vm((heads, tokens_dev, 4 * HD), BF),
            pltpu.SemaphoreType.DMA((heads // 2, 4)),
            pltpu.SemaphoreType.DMA((heads // 2,)),
        ],
        source=HBM,
        target=HBM,
        limit=64,
    )
    own = spread(packed)
    w_own = jnp.concatenate(
        [
            lax.dynamic_slice_in_dim(w_key, mine * HD, HD, 1),
            lax.dynamic_slice_in_dim(w_query, mine * HD, HD, 1),
        ],
        1,
    )
    pos = nn(rel_emb, w_own).astype(BF)
    table = jnp.flip(bucket_table).reshape(1, -1)
    w_rows, b_rows = depth // seq_count, buckets // seq_count
    rows = TILE + TILE // 2 + w_rows + b_rows
    line = 2 * span * TILE
    scalars = jnp.concatenate([doc_lengths, half])
    onehot, expanded = whole_call(
        table_kernel,
        (scalars, pos, table),
        [shape((buckets, table.shape[1]), BF), shape((2 * HD, table.shape[1]), BF)],
        scalars=1,
    )
    other = lax.ppermute(
        whole_call(cut_kernel, (own, expanded), shape((heads, tokens_dev, 2 * HD), BF)),
        "seq",
        partners,
    )
    sent, kept, bucket, query = whole_call(
        head_kernel,
        (scalars, own, other, onehot, expanded),
        [
            shape((heads * TILE + buckets, 2 * HD), BF),
            shape((heads, TILE, 2 * HD), F32),
            shape((buckets, 2 * HD), BF),
            shape((heads, TILE // 2, 2 * HD), BF),
        ],
        [
            vm((HD, line), BF),
            vm((HD, line), BF),
            vm((seq_count, TILE, 2 * HD), BF),
            vm((seq_count, TILE, 2 * HD), F32),
            vm((seq_count, HD, TILE), F32),
            vm((HD, line), F32),
            vm((HD, line), F32),
            vm((HD, seq_count * TILE), BF),
            vm((TILE, (span + 1) * TILE), F32),
            vm((span, TILE, TILE), F32),
            vm((span, TILE, TILE), F32),
            vm((TILE, (span + 1) * TILE), BF),
            vm((span, TILE, 2 * TILE), BF),
            vm((heads, HD, TILE), F32),
            vm((heads, HD, TILE), F32),
        ],
        scalars=1,
    )
    came = lax.ppermute(sent, "seq", partners)
    joined = whole_call(
        join_kernel,
        (half, kept, bucket, query, came, rel_emb),
        shape((heads, rows, 2 * HD), BF),
        [vm((depth, 2 * HD), F32), vm((buckets, 2 * HD), F32)],
        scalars=1,
    )
    returned = spread(joined)
    side = lax.axis_index("head").astype(jnp.int32).reshape(1)
    rel_half = shape((b_rows, width), BF)
    kept_rel, away_rel = whole_call(
        rel_kernel, (side, returned, w_key, w_query), [rel_half, rel_half], scalars=1
    )
    came_rel = lax.ppermute(away_rel, "head", [(0, 1), (1, 0)])
    tokens = shape((tokens_dev, width), BF)
    weights = shape((w_rows, width), F32)
    query_grad, key_grad, value_grad, w_query_grad, w_key_grad, done = whole_call(
        unpack_kernel,
        (returned,),
        [tokens, tokens, tokens, weights, weights, shape((8, TILE), F32)],
    )
    totals = whole_call(
        total_kernel, (kept_rel, came_rel, done), shape((heads, b_rows, width), BF)
    )
    near = spread(totals)
    far = lax.ppermute(near, "seq", partners)
    rel_emb_grad = whole_call(
        weave_kernel, (half, near, far), shape((buckets, width), F32), scalars=1
    )
    return (query_grad, key_grad, value_grad, rel_emb_grad, w_query_grad, w_key_grad)


def fits_heads(mesh, queries, rel_emb, bucket_table):
    seq, head = mesh.shape["seq"], mesh.shape["head"]
    heads = queries.shape[1] // HD // head
    return (
        head == 2
        and seq == 2 * heads
        and heads % 2 == 0
        and queries.shape[0] == seq * TILE
        and bucket_table.shape[0] % (2 * TILE) == 0
        and seq >= bucket_table.shape[0] // TILE + 1
        and rel_emb.shape[0] % (16 * seq) == 0
        and rel_emb.shape[1] % (16 * seq) == 0
        and rel_emb.shape[0] % TILE == 0
    )


def solution(mesh):
    in_specs = (
        P("seq", "head"),
        P("seq", "head"),
        P("seq", "head"),
        P("seq", "head"),
        P(),
        P(None, "head"),
        P(None, "head"),
        P(),
        P(),
    )
    out_specs = (
        P("seq", "head"),
        P("seq", "head"),
        P("seq", "head"),
        P(None, "head"),
        P("seq", "head"),
        P("seq", "head"),
    )

    def run(queries, keys, values, out_grad, rel_emb, w_query, w_key, doc_lengths, bucket_table):
        chosen = head_body if fits_heads(mesh, queries, rel_emb, bucket_table) else body
        return jax.shard_map(
            chosen, mesh=mesh, in_specs=in_specs, out_specs=out_specs, check_vma=False
        )(queries, keys, values, out_grad, rel_emb, w_query, w_key, doc_lengths, bucket_table)

    return run
```

```python
import math

import jax
import jax.numpy as jnp
from jax import lax
from jax.experimental import pallas as pl
from jax.experimental.pallas import tpu as pltpu
from jax.sharding import PartitionSpec as P

HD = 64
SPAN = 4
TILE = 128
SPANS = (2, 3, 4, 5, 6, 7)
BF = jnp.bfloat16
F32 = jnp.float32


masked_score = -1e30


def shifted(block, axis, distance):
    devices = range(lax.axis_size(axis))
    route = [(i - distance, i) for i in devices if i - distance in devices]
    return lax.ppermute(block, axis, route)


def contract(left, right, left_dim, right_dim):
    return lax.dot_general(
        left, right, (((left_dim,), (right_dim,)), ((), ())), preferred_element_type=jnp.float32
    )


def doc_index(position, doc_ends, extent):
    inside = (position >= 0) & (position < extent)
    owner = jnp.sum((doc_ends[None, :] <= position[:, None]).astype(jnp.int32), axis=1)
    return jnp.where(inside, owner, -1)


def same_document(row_pos, col_pos, doc_ends, extent):
    return (
        doc_index(row_pos, doc_ends, extent)[:, None]
        == doc_index(col_pos, doc_ends, extent)[None, :]
    )


def tile_tables(bucket_table, shift, rows, buckets):
    offset_span = bucket_table.shape[0] // 2
    spread = jnp.arange(2 * rows - 1, dtype=jnp.int32) - (rows - 1)
    ahead_index = bucket_table[jnp.clip(shift - spread + offset_span, 0, 2 * offset_span - 1)]
    behind_index = bucket_table[jnp.clip(offset_span - shift - spread, 0, 2 * offset_span - 1)]
    bucket_ids = jnp.arange(buckets, dtype=jnp.int32)[None, :]
    ahead_onehot = (ahead_index[:, None] == bucket_ids).astype(jnp.bfloat16)
    behind_onehot = (behind_index[:, None] == bucket_ids).astype(jnp.bfloat16)
    return (ahead_index, behind_index, ahead_onehot, behind_onehot)


def skew_in(spread, width):
    rows = spread.shape[0]
    line = rows + width - 1
    flat = jnp.pad(spread, ((0, 0), (0, 1))).reshape(-1)
    return flat[rows - 1 : rows - 1 + rows * line].reshape(rows, line)[:, :width]


def skew_out(dense):
    rows, width = dense.shape
    line = rows + width - 1
    padded = jnp.pad(dense, ((0, 0), (0, rows - 1))).reshape(-1)
    flat = jnp.pad(padded, (rows - 1, 1))
    return flat.reshape(rows, line + 1)[:, :line]


def tile_scores(
    query_rows, key_rows, pos_keys, pos_queries, ahead_onehot, behind_onehot, score_scale
):
    content = contract(query_rows, key_rows, 1, 1)
    ahead_band = contract(ahead_onehot, pos_keys, 1, 0).astype(jnp.bfloat16)
    behind_band = contract(behind_onehot, pos_queries, 1, 0).astype(jnp.bfloat16)
    query_term = skew_in(contract(query_rows, ahead_band, 1, 1), key_rows.shape[0])
    key_term = skew_in(contract(key_rows, behind_band, 1, 1), query_rows.shape[0]).T
    return score_scale * (content + query_term + key_term)


def query_side(
    query_rows,
    key_rows,
    value_rows,
    grad_rows,
    pos_keys,
    pos_queries,
    same_doc,
    tables,
    score_scale,
):
    tile_rows = query_rows.shape[0]
    tile_count = key_rows.shape[0] // tile_rows
    pieces = []
    for tile in range(tile_count):
        key_tile = key_rows[tile * tile_rows : (tile + 1) * tile_rows]
        pieces.append(
            tile_scores(
                query_rows,
                key_tile,
                pos_keys,
                pos_queries,
                tables[tile][2],
                tables[tile][3],
                score_scale,
            )
        )
    scores = jnp.where(same_doc, jnp.concatenate(pieces, 1), masked_score)
    row_max = jnp.max(scores, axis=1, keepdims=True)
    expd = jnp.where(same_doc, jnp.exp(scores - row_max), 0.0)
    row_sum = jnp.sum(expd, axis=1, keepdims=True)
    probs = expd / row_sum
    dprobs = contract(grad_rows, value_rows, 1, 1)
    row_dot = jnp.sum(probs * dprobs, axis=1, keepdims=True)
    dscores = probs * (dprobs - row_dot)
    dscores_low = dscores.astype(jnp.bfloat16)
    ahead_grad = jnp.zeros((tile_rows, pos_keys.shape[0]), jnp.float32)
    for tile in range(tile_count):
        band = dscores_low[:, tile * tile_rows : (tile + 1) * tile_rows]
        ahead_grad = ahead_grad + contract(skew_out(band), tables[tile][2], 1, 0)
    ahead_low = ahead_grad.astype(jnp.bfloat16)
    query_grad = score_scale * (
        contract(dscores_low, key_rows, 1, 0) + contract(ahead_low, pos_keys, 1, 0)
    )
    bucket_key = score_scale * contract(ahead_low, query_rows, 0, 0)
    probs_low = probs.astype(jnp.bfloat16)
    behind_parts = []
    for tile in range(tile_count):
        band = dscores_low[:, tile * tile_rows : (tile + 1) * tile_rows]
        behind_parts.append(contract(skew_out(band.T), tables[tile][3], 1, 0).astype(jnp.bfloat16))
    behind_low = jnp.concatenate(behind_parts, 0)
    key_grad = score_scale * (
        contract(dscores_low, query_rows, 0, 0) + contract(behind_low, pos_queries, 1, 0)
    )
    value_grad = contract(probs_low, grad_rows, 0, 0)
    bucket_query = score_scale * contract(behind_low, key_rows, 0, 0)
    return (query_grad, key_grad, value_grad, bucket_key, bucket_query)


def split_heads(matrix):
    return matrix.reshape(matrix.shape[0], matrix.shape[1] // HD, HD).transpose(1, 0, 2)


def join_heads(stacked):
    return stacked.transpose(1, 0, 2).reshape(stacked.shape[1], stacked.shape[0] * HD)


def body(queries, keys, values, out_grad, rel_emb, w_query, w_key, doc_lengths, bucket_table):
    tokens_dev = queries.shape[0]
    seq_count = lax.axis_size("seq")
    neighbours = min(SPAN, seq_count // 4)
    extent = tokens_dev * seq_count
    seq_index = lax.axis_index("seq")
    first_token = seq_index * tokens_dev
    score_scale = 1.0 / math.sqrt(3.0 * HD)
    pos_key = jnp.dot(rel_emb, w_key, preferred_element_type=jnp.float32).astype(jnp.bfloat16)
    pos_query = jnp.dot(rel_emb, w_query, preferred_element_type=jnp.float32).astype(jnp.bfloat16)
    doc_ends = jnp.cumsum(doc_lengths)
    buckets = rel_emb.shape[0]
    tables = [
        tile_tables(bucket_table, (neighbours - tile) * tokens_dev, tokens_dev, buckets)
        for tile in range(2 * neighbours + 1)
    ]
    hop_list = list(range(neighbours, 0, -1)) + list(range(-1, -neighbours - 1, -1))
    fetched = []
    for distance in hop_list:
        fetched.append(shifted((keys, values), "seq", distance))
    lower_side = fetched[:neighbours]
    upper_side = fetched[neighbours:]
    key_window = jnp.concatenate(
        [pair[0] for pair in lower_side] + [keys] + [pair[0] for pair in upper_side], 0
    )
    value_window = jnp.concatenate(
        [pair[1] for pair in lower_side] + [values] + [pair[1] for pair in upper_side], 0
    )
    window = key_window.shape[0]
    query_pos = first_token + jnp.arange(tokens_dev, dtype=jnp.int32)
    window_pos = first_token - neighbours * tokens_dev + jnp.arange(window, dtype=jnp.int32)
    same_doc = same_document(query_pos, window_pos, doc_ends, extent)
    query_heads = split_heads(queries)
    grad_heads = split_heads(out_grad)
    pos_key_heads = split_heads(pos_key)
    pos_query_heads = split_heads(pos_query)

    def every_pair(operands):
        query_rows, key_rows, value_rows, grad_rows, pos_keys, pos_queries = operands
        return query_side(
            query_rows,
            key_rows,
            value_rows,
            grad_rows,
            pos_keys,
            pos_queries,
            same_doc,
            tables,
            score_scale,
        )

    query_grad, key_part, value_part, bucket_key, bucket_query = lax.map(
        every_pair,
        (
            query_heads,
            split_heads(key_window),
            split_heads(value_window),
            grad_heads,
            pos_key_heads,
            pos_query_heads,
        ),
    )
    key_flat = join_heads(key_part)
    value_flat = join_heads(value_part)
    key_total = key_flat[neighbours * tokens_dev : (neighbours + 1) * tokens_dev]
    value_total = value_flat[neighbours * tokens_dev : (neighbours + 1) * tokens_dev]
    for distance in hop_list:
        segment = neighbours - distance
        returned = (
            key_flat[segment * tokens_dev : (segment + 1) * tokens_dev],
            value_flat[segment * tokens_dev : (segment + 1) * tokens_dev],
        )
        arrived = shifted((returned[0], returned[1]), "seq", -distance)
        key_total = key_total + arrived[0]
        value_total = value_total + arrived[1]
    key_grad = key_total.astype(jnp.bfloat16)
    value_grad = value_total.astype(jnp.bfloat16)
    query_out = join_heads(query_grad).astype(jnp.bfloat16)
    summed = lax.psum((join_heads(bucket_key), join_heads(bucket_query)), "seq")
    bucket_key_low = summed[0].astype(jnp.bfloat16)
    bucket_query_low = summed[1].astype(jnp.bfloat16)
    rows_dev = rel_emb.shape[1] // seq_count
    rel_columns = lax.dynamic_slice_in_dim(rel_emb, seq_index * rows_dev, rows_dev, 1)
    w_key_grad = contract(rel_columns, bucket_key_low, 0, 0)
    w_query_grad = contract(rel_columns, bucket_query_low, 0, 0)
    rel_partial = contract(bucket_key_low, w_key, 1, 1) + contract(bucket_query_low, w_query, 1, 1)
    rel_emb_grad = lax.psum_scatter(
        rel_partial.astype(jnp.bfloat16), "head", scatter_dimension=1, tiled=True
    ).astype(jnp.float32)
    return (query_out, key_grad, value_grad, rel_emb_grad, w_query_grad, w_key_grad)


def nn(left, right):
    return contract(left, right, 1, 0)


def nt(left, right):
    return contract(left, right, 1, 1)


def grid_of(shape):
    return (
        lax.broadcasted_iota(jnp.int32, shape, 0),
        lax.broadcasted_iota(jnp.int32, shape, 1),
    )


def pack_kernel(q_ref, g_ref, k_ref, v_ref, out_ref, held, pieces, came, left):
    heads = out_ref.shape[0]
    wide = 2 * HD
    loads = []
    for g in range(heads // 2):
        cols = pl.ds(g * wide, wide)
        loads.append(
            [
                pltpu.make_async_copy(ref.at[:, cols], held.at[i, :, cols], came.at[g, i])
                for i, ref in enumerate((q_ref, g_ref, k_ref, v_ref))
            ]
        )
        for load in loads[g]:
            load.start()
    stores = []
    for g in range(heads // 2):
        for load in loads[g]:
            load.wait()
        for head in (2 * g, 2 * g + 1):
            cols = slice(head * HD, (head + 1) * HD)
            pieces[head] = jnp.concatenate([held[i, :, cols] for i in range(4)], 1)
        two = pl.ds(2 * g, 2)
        stores.append(pltpu.make_async_copy(pieces.at[two], out_ref.at[two], left.at[g]))
        stores[g].start()
    for store in stores:
        store.wait()


def table_kernel(scalars_ref, pos_ref, table_ref, onehot, expanded):
    buckets, valid = onehot.shape
    for part in range(buckets // TILE):
        ids = lax.broadcasted_iota(jnp.int32, (TILE, valid), 0) + part * TILE
        onehot[pl.ds(part * TILE, TILE), :] = jnp.where(ids == table_ref[...], 1.0, 0.0).astype(BF)
    pos_t = pos_ref[...].astype(F32).T.astype(BF)
    expanded[...] = nn(pos_t, onehot[...]).astype(BF)


def cut_kernel(own_ref, expanded, out_ref):
    out_ref[...] = own_ref[:, :, 2 * HD :]


def head_kernel(
    scalars_ref, own_ref, other_ref, onehot, expanded,
    send_ref, keep_ref, bucket_ref, query_ref,
    pk, pq, kvs, acc, acc_pos, g_key, g_query, k_t, k_rev, s_q, st, dp, dtile, pairs, dq_nat, dq_pos,
):
    blocks = own_ref.shape[0]
    tiles = 2 * blocks
    buckets, valid = onehot.shape
    halo = valid // 2 // TILE
    longest = 2 * halo + 1
    scale = 1.0 / math.sqrt(3.0 * HD)
    valid0 = (halo + 1) * TILE
    docs = scalars_ref.shape[0] - 1
    half = scalars_ref[docs]
    row, col = grid_of((TILE, TILE))
    swap = jnp.where(row + col == TILE - 1, 1.0, 0.0).astype(BF)
    wrap = row + col >= TILE - 1
    keep = jnp.where(col >= row, 1.0, 0.0).astype(BF)
    low = col < HD
    for table, part in ((pk, expanded[:HD]), (pq, expanded[HD:])):
        table[:, 0:valid0] = jnp.zeros((HD, valid0), BF)
        table[:, valid0 : valid0 + valid] = part
        rest = table.shape[1] - valid0 - valid
        table[:, valid0 + valid :] = jnp.zeros((HD, rest), BF)
    acc[...] = jnp.zeros_like(acc)
    acc_pos[...] = jnp.zeros_like(acc_pos)
    for g in (g_key, g_query):
        g[:, valid0 : valid0 + valid] = jnp.zeros((HD, valid), F32)

    for b in range(blocks):
        for kv, tile in (
            (own_ref[b, :, 2 * HD : 4 * HD], 2 * b + half),
            (other_ref[b], 2 * b + 1 - half),
        ):
            kvs[tile] = kv
            k_t[tile] = kv[:, :HD].astype(F32).T.astype(BF)
    k_rev[...] = (
        nn(k_t[...].reshape(tiles * HD, TILE), swap).astype(BF).reshape(tiles, HD, TILE)
    )

    def block(b, carry):
        own = 2 * b + half
        token = own * TILE

        def next_end(d, state):
            end, start, stop = state
            stop = jnp.where(end < token + TILE, end + scalars_ref[d], stop)
            end = end + scalars_ref[d]
            start = jnp.where(end <= token, end, start)
            return (end, start, stop)

        zero = jnp.int32(0)
        _, reach_low, reach_high = lax.fori_loop(
            0, docs, next_end, (zero, zero, zero), unroll=docs <= 16
        )
        lowest = reach_low // TILE
        count = (reach_high + TILE - 1) // TILE - lowest
        shorter = 0
        for span in SPANS:
            if span < longest:
                pl.when((count > shorter) & (count <= span))(
                    lambda span=span: work(b, own, lowest, span)
                )
                shorter = span
        pl.when(count > shorter)(lambda: work(b, own, lowest, longest))
        return carry

    def work(b, own, lowest, span):
        first = jnp.clip(lowest, 0, tiles - span)
        delta = (own - first) * TILE
        qd = own_ref[b, :, 0 : 2 * HD]
        turned = qd.astype(F32).T
        upper = row < HD
        right = jnp.concatenate(
            [jnp.where(upper, turned, 0.0), jnp.where(upper, 0.0, turned)], 1
        ).astype(BF)
        q_rev = nn(turned[:HD].astype(BF), swap).astype(BF)

        position = own * TILE + lax.broadcasted_iota(jnp.int32, (1, TILE), 1)

        def next_doc(d, state):
            end, start, stop = state
            stop = jnp.where(end <= position, end + scalars_ref[d], stop)
            end = end + scalars_ref[d]
            start = jnp.where(end <= position, end, start)
            return (end, start, stop)

        nothing = jnp.zeros((1, TILE), jnp.int32)
        _, start, stop = lax.fori_loop(
            0, docs, next_doc, (jnp.int32(0), nothing, nothing), unroll=docs <= 16
        )
        start = start - first * TILE
        stop = stop - first * TILE

        key_x = pl.multiple_of(halo * 2 * TILE - delta, TILE)
        s_q[:, 0 : (span + 1) * TILE] = nn(qd[:, :HD], pk[:, pl.ds(key_x, (span + 1) * TILE)])
        best = jnp.full((8, TILE), masked_score, F32)
        window_kv = kvs[pl.ds(first, span)].reshape(span * TILE, 2 * HD)
        contents = nn(window_kv, right)
        for t in range(span):
            kv = window_kv[t * TILE : (t + 1) * TILE]
            both = contents[t * TILE : (t + 1) * TILE]
            query_x = pl.multiple_of(2 * halo * TILE + delta - t * TILE, TILE)
            s_k = nn(kv[:, :HD], pq[:, pl.ds(query_x, 2 * TILE)])
            key_term = pltpu.roll(
                jnp.where(wrap, s_k[:, :TILE], s_k[:, TILE:]), 1, 1, stride=1, stride_axis=0
            )
            query_term = pltpu.roll(
                jnp.where(
                    wrap,
                    s_q[:, t * TILE : (t + 1) * TILE],
                    s_q[:, (t + 1) * TILE : (t + 2) * TILE],
                ),
                1,
                1,
                stride=1,
                stride_axis=0,
            )
            score = both[:, :TILE] + key_term + query_term.T
            inside = (row >= start - t * TILE) & (row < stop - t * TILE)
            score = jnp.where(inside, score, masked_score)
            st[t] = score
            dp[t] = both[:, TILE:]
            best = jnp.maximum(best, jnp.max(score.reshape(TILE // 8, 8, TILE), 0))
        top = jnp.max(best, 0, keepdims=True)
        total = jnp.zeros((8, TILE), F32)
        dot = jnp.zeros((8, TILE), F32)
        for t in range(span):
            expd = jnp.exp2((st[t] - top) * (scale * math.log2(math.e)))
            st[t] = expd
            total = total + jnp.sum(expd.reshape(TILE // 8, 8, TILE), 0)
            dot = dot + jnp.sum((expd * dp[t]).reshape(TILE // 8, 8, TILE), 0)
        inverse = 1.0 / jnp.sum(total, 0, keepdims=True)
        row_dot = jnp.sum(dot, 0, keepdims=True) * inverse

        lows = jnp.where(low, qd, jnp.zeros_like(qd))
        pair = jnp.concatenate([lows, jnp.where(low, jnp.zeros_like(qd), qd)], 0)
        dq_t = jnp.zeros((HD, TILE), F32)
        before = jnp.zeros((TILE, TILE), BF)
        near = held = None
        for t in range(span):
            prob = st[t] * inverse
            dscore = (prob * (dp[t] - row_dot)).astype(BF)
            pairs[t] = jnp.concatenate([dscore, prob.astype(BF)], 1)
            stacked = nn(
                jnp.concatenate([k_t[first + t], swap], 0),
                jnp.concatenate([dscore, dscore.T], 1),
            )
            dq_t = dq_t + stacked[:HD, :TILE]
            query_x = pl.multiple_of(2 * halo * TILE + delta - t * TILE, TILE)
            y = pltpu.roll(stacked[HD:, :TILE], 0, 1, stride=1, stride_axis=0).astype(BF)
            last = near
            near = y * keep
            far = y - near
            g_query[:, pl.ds(query_x, 2 * TILE)] += nn(
                k_rev[first + t], jnp.concatenate([near, far], 1)
            )
            chunk = pq[:, pl.ds(query_x + TILE, TILE)]
            if t == 0:
                held = nt(chunk, far)
            else:
                back = nt(chunk, jnp.concatenate([last, far], 0))
                acc_pos[first + t - 1] += held + back[:, :TILE]
                held = back[:, TILE:]
            z = pltpu.roll(stacked[HD:, TILE:], 0, 1, stride=1, stride_axis=0).astype(BF)
            here = z * keep
            dtile[:, t * TILE : (t + 1) * TILE] = here + before
            before = z - here
        acc_pos[first + span - 1] += held + nt(pq[:, pl.ds(query_x, TILE)], near)
        acc[pl.ds(first, span)] += nn(
            pairs[0:span].reshape(span * TILE, 2 * TILE), pair
        ).reshape(span, TILE, 2 * HD)
        dtile[:, span * TILE : (span + 1) * TILE] = before
        spread_q = dtile[:, 0 : (span + 1) * TILE]
        window = pl.ds(key_x, (span + 1) * TILE)
        g_key[:, window] += nn(q_rev, spread_q)
        dq_pos[b] = nt(pk[:, window], spread_q)
        dq_nat[b] = dq_t

    lax.fori_loop(0, blocks, block, 0)

    parts = []
    for g in (g_key, g_query):
        band = g[:, valid0 : valid0 + valid]
        high = band.astype(BF)
        parts += [high, (band - high.astype(F32)).astype(BF)]
    summed = nt(jnp.concatenate(parts, 0), onehot[...])
    bucket_t = scale * jnp.concatenate(
        [summed[:HD] + summed[HD : 2 * HD], summed[2 * HD : 3 * HD] + summed[3 * HD :]], 0
    )
    bucket = bucket_t.T.astype(BF)
    bucket_ref[...] = bucket
    send_ref[blocks * TILE :, :] = bucket
    factor = jnp.where(low, scale, 1.0)

    def unreverse(ref):
        part = ref[...].reshape(ref.shape[0] * HD, TILE)
        high = part.astype(BF)
        low_part = (part - high.astype(F32)).astype(BF)
        ref[...] = (nn(high, swap) + nn(low_part, swap)).reshape(ref.shape)

    unreverse(acc_pos)
    unreverse(dq_pos)

    def gradients(tile):
        extra = acc_pos[tile].T
        extra = jnp.concatenate([extra, jnp.zeros_like(extra)], 1)
        return (acc[tile] + extra) * factor

    for b in range(blocks):
        keep_ref[b] = gradients(2 * b + half)
        send_ref[b * TILE : (b + 1) * TILE, :] = gradients(2 * b + 1 - half).astype(BF)
        grad = scale * (dq_nat[b] + dq_pos[b]).T
        query_ref[b] = jnp.concatenate([grad[: TILE // 2], grad[TILE // 2 :]], 1).astype(BF)


def join_kernel(
    half_ref, keep_ref, bucket_ref, query_ref, came_ref, rel_ref, out_ref, weight, bucket, pieces, sems
):
    blocks = keep_ref.shape[0]
    tiles = 2 * blocks
    half = half_ref[0]
    w_rows = weight.shape[0] // tiles
    b_rows = bucket.shape[0] // tiles
    base_w = TILE + TILE // 2
    base_b = base_w + w_rows
    for b in range(blocks):
        came = came_ref[b * TILE : (b + 1) * TILE, :].astype(F32)
        pieces[b, 0:TILE, :] = (keep_ref[b] + came).astype(BF)
        pieces[b, TILE:base_w, :] = query_ref[b]
    rows = (pl.ds(0, base_w), pl.ds(base_w, w_rows + b_rows))
    stores = [
        pltpu.make_async_copy(pieces.at[:, part], out_ref.at[:, part], sems.at[i])
        for i, part in enumerate(rows)
    ]
    stores[0].start()
    total = bucket_ref[...].astype(F32) + came_ref[blocks * TILE :, :].astype(F32)
    bucket[...] = total
    weight[...] = nn(total.T.astype(BF), rel_ref[...]).T
    for b in range(blocks):
        tile = 2 * b + half
        pieces[b, base_w:base_b, :] = weight[pl.ds(tile * w_rows, w_rows), :].astype(BF)
        pieces[b, base_b:, :] = bucket[pl.ds(tile * b_rows, b_rows), :].astype(BF)
    stores[1].start()
    for store in stores:
        store.wait()


def weave_kernel(half_ref, near_ref, far_ref, out_ref):
    shards, rows, _ = near_ref.shape
    half = half_ref[0]
    for shard in range(shards):
        for ref, place in ((near_ref, half), (far_ref, 1 - half)):
            start = pl.multiple_of((2 * shard + place) * rows, rows)
            out_ref[pl.ds(start, rows), :] = ref[shard].astype(F32)


def rel_kernel(side_ref, got_ref, wk_ref, wq_ref, kept_ref, away_ref):
    heads = range(got_ref.shape[0])
    rows, width = kept_ref.shape
    base_b = got_ref.shape[1] - rows
    rel = nt(jnp.concatenate([got_ref[h, base_b:, :HD] for h in heads], 1), wk_ref[...]) + nt(
        jnp.concatenate([got_ref[h, base_b:, HD:] for h in heads], 1), wq_ref[...]
    )
    left, right = rel[:, :width], rel[:, width:]
    first = jnp.full(left.shape, side_ref[0], jnp.int32) == 0
    kept_ref[...] = jnp.where(first, left, right).astype(BF)
    away_ref[...] = jnp.where(first, right, left).astype(BF)


def total_kernel(kept_ref, came_ref, after_ref, out_ref):
    total = (kept_ref[...].astype(F32) + came_ref[...].astype(F32)).astype(BF)
    for shard in range(out_ref.shape[0]):
        out_ref[shard] = total


def unpack_kernel(got_ref, dq_ref, dk_ref, dv_ref, dwq_ref, dwk_ref, done_ref):
    done_ref[...] = jnp.zeros_like(done_ref)
    base_w = TILE + TILE // 2
    base_b = base_w + dwk_ref.shape[0]
    for g in range(got_ref.shape[0] // 2):
        cols = slice(2 * g * HD, 2 * (g + 1) * HD)
        two = [got_ref[2 * g], got_ref[2 * g + 1]]
        dq_ref[:, cols] = jnp.concatenate(
            [
                jnp.concatenate([one[TILE:base_w, :HD], one[TILE:base_w, HD:]], 0)
                for one in two
            ],
            1,
        )
        dk_ref[:, cols] = jnp.concatenate([one[:TILE, :HD] for one in two], 1)
        dv_ref[:, cols] = jnp.concatenate([one[:TILE, HD:] for one in two], 1)
        dwk_ref[:, cols] = jnp.concatenate([one[base_w:base_b, :HD] for one in two], 1).astype(F32)
        dwq_ref[:, cols] = jnp.concatenate([one[base_w:base_b, HD:] for one in two], 1).astype(F32)


VMEM = pl.BlockSpec(memory_space=pltpu.VMEM)
SMEM = pl.BlockSpec(memory_space=pltpu.SMEM)
HBM = pl.BlockSpec(memory_space=pltpu.HBM)


def whole_call(kernel, inputs, outputs, scratch=(), scalars=0, source=VMEM, target=VMEM, limit=48):
    return pl.pallas_call(
        kernel,
        out_shape=outputs,
        in_specs=[SMEM] * scalars + [source] * (len(inputs) - scalars),
        out_specs=jax.tree.map(lambda _: target, outputs),
        scratch_shapes=list(scratch),
        compiler_params=pltpu.CompilerParams(vmem_limit_bytes=limit << 20),
    )(*inputs)


def head_body(queries, keys, values, out_grad, rel_emb, w_query, w_key, doc_lengths, bucket_table):
    tokens_dev, width = queries.shape
    heads = width // HD
    seq_count = lax.axis_size("seq")
    seq_index = lax.axis_index("seq")
    buckets, depth = rel_emb.shape
    halo = bucket_table.shape[0] // 2 // TILE
    span = 2 * halo + 1
    mine = seq_index // 2
    half = lax.rem(seq_index, 2).astype(jnp.int32).reshape(1)
    halves = [list(range(0, seq_count, 2)), list(range(1, seq_count, 2))]
    partners = [(i, i ^ 1) for i in range(seq_count)]
    shape = jax.ShapeDtypeStruct
    vm = pltpu.VMEM

    def spread(pieces):
        return lax.all_to_all(pieces, "seq", 0, 0, axis_index_groups=halves, tiled=True)

    packed = whole_call(
        pack_kernel,
        (queries, out_grad, keys, values),
        shape((heads, tokens_dev, 4 * HD), BF),
        [
            vm((4, tokens_dev, width), BF),
            vm((heads, tokens_dev, 4 * HD), BF),
            pltpu.SemaphoreType.DMA((heads // 2, 4)),
            pltpu.SemaphoreType.DMA((heads // 2,)),
        ],
        source=HBM,
        target=HBM,
        limit=64,
    )
    own = spread(packed)
    w_own = jnp.concatenate(
        [
            lax.dynamic_slice_in_dim(w_key, mine * HD, HD, 1),
            lax.dynamic_slice_in_dim(w_query, mine * HD, HD, 1),
        ],
        1,
    )
    pos = nn(rel_emb, w_own).astype(BF)
    table = jnp.flip(bucket_table).reshape(1, -1)
    w_rows, b_rows = depth // seq_count, buckets // seq_count
    rows = TILE + TILE // 2 + w_rows + b_rows
    line = 2 * span * TILE
    scalars = jnp.concatenate([doc_lengths, half])
    onehot, expanded = whole_call(
        table_kernel,
        (scalars, pos, table),
        [shape((buckets, table.shape[1]), BF), shape((2 * HD, table.shape[1]), BF)],
        scalars=1,
    )
    other = lax.ppermute(
        whole_call(cut_kernel, (own, expanded), shape((heads, tokens_dev, 2 * HD), BF)),
        "seq",
        partners,
    )
    sent, kept, bucket, query = whole_call(
        head_kernel,
        (scalars, own, other, onehot, expanded),
        [
            shape((heads * TILE + buckets, 2 * HD), BF),
            shape((heads, TILE, 2 * HD), F32),
            shape((buckets, 2 * HD), BF),
            shape((heads, TILE // 2, 2 * HD), BF),
        ],
        [
            vm((HD, line), BF),
            vm((HD, line), BF),
            vm((seq_count, TILE, 2 * HD), BF),
            vm((seq_count, TILE, 2 * HD), F32),
            vm((seq_count, HD, TILE), F32),
            vm((HD, line), F32),
            vm((HD, line), F32),
            vm((seq_count, HD, TILE), BF),
            vm((seq_count, HD, TILE), BF),
            vm((TILE, (span + 1) * TILE), F32),
            vm((span, TILE, TILE), F32),
            vm((span, TILE, TILE), F32),
            vm((TILE, (span + 1) * TILE), BF),
            vm((span, TILE, 2 * TILE), BF),
            vm((heads, HD, TILE), F32),
            vm((heads, HD, TILE), F32),
        ],
        scalars=1,
    )
    came = lax.ppermute(sent, "seq", partners)
    joined = whole_call(
        join_kernel,
        (half, kept, bucket, query, came, rel_emb),
        shape((heads, rows, 2 * HD), BF),
        [
            vm((depth, 2 * HD), F32),
            vm((buckets, 2 * HD), F32),
            vm((heads, rows, 2 * HD), BF),
            pltpu.SemaphoreType.DMA((2,)),
        ],
        scalars=1,
        target=HBM,
    )
    returned = spread(joined)
    side = lax.axis_index("head").astype(jnp.int32).reshape(1)
    rel_half = shape((b_rows, width), BF)
    kept_rel, away_rel = whole_call(
        rel_kernel, (side, returned, w_key, w_query), [rel_half, rel_half], scalars=1
    )
    came_rel = lax.ppermute(away_rel, "head", [(0, 1), (1, 0)])
    tokens = shape((tokens_dev, width), BF)
    weights = shape((w_rows, width), F32)
    query_grad, key_grad, value_grad, w_query_grad, w_key_grad, done = whole_call(
        unpack_kernel,
        (returned,),
        [tokens, tokens, tokens, weights, weights, shape((8, TILE), F32)],
    )
    totals = whole_call(
        total_kernel, (kept_rel, came_rel, done), shape((heads, b_rows, width), BF)
    )
    near = spread(totals)
    far = lax.ppermute(near, "seq", partners)
    rel_emb_grad = whole_call(
        weave_kernel, (half, near, far), shape((buckets, width), F32), scalars=1
    )
    return (query_grad, key_grad, value_grad, rel_emb_grad, w_query_grad, w_key_grad)


def fits_heads(mesh, queries, rel_emb, bucket_table):
    seq, head = mesh.shape["seq"], mesh.shape["head"]
    heads = queries.shape[1] // HD // head
    return (
        head == 2
        and seq == 2 * heads
        and heads % 2 == 0
        and queries.shape[0] == seq * TILE
        and bucket_table.shape[0] % (2 * TILE) == 0
        and seq >= bucket_table.shape[0] // TILE + 1
        and rel_emb.shape[0] % (16 * seq) == 0
        and rel_emb.shape[1] % (16 * seq) == 0
        and rel_emb.shape[0] % TILE == 0
    )


def solution(mesh):
    in_specs = (
        P("seq", "head"),
        P("seq", "head"),
        P("seq", "head"),
        P("seq", "head"),
        P(),
        P(None, "head"),
        P(None, "head"),
        P(),
        P(),
    )
    out_specs = (
        P("seq", "head"),
        P("seq", "head"),
        P("seq", "head"),
        P(None, "head"),
        P("seq", "head"),
        P("seq", "head"),
    )

    def run(queries, keys, values, out_grad, rel_emb, w_query, w_key, doc_lengths, bucket_table):
        chosen = head_body if fits_heads(mesh, queries, rel_emb, bucket_table) else body
        return jax.shard_map(
            chosen, mesh=mesh, in_specs=in_specs, out_specs=out_specs, check_vma=False
        )(queries, keys, values, out_grad, rel_emb, w_query, w_key, doc_lengths, bucket_table)

    return run
```

```python
import math

import jax
import jax.numpy as jnp
from jax import lax
from jax.experimental import pallas as pl
from jax.experimental.pallas import tpu as pltpu
from jax.sharding import PartitionSpec as P

HD = 64
SPAN = 4
TILE = 128
SPANS = (2, 3, 4, 5, 6, 7)
BF = jnp.bfloat16
F32 = jnp.float32


masked_score = -1e30


def shifted(block, axis, distance):
    devices = range(lax.axis_size(axis))
    route = [(i - distance, i) for i in devices if i - distance in devices]
    return lax.ppermute(block, axis, route)


def contract(left, right, left_dim, right_dim):
    return lax.dot_general(
        left, right, (((left_dim,), (right_dim,)), ((), ())), preferred_element_type=jnp.float32
    )


def doc_index(position, doc_ends, extent):
    inside = (position >= 0) & (position < extent)
    owner = jnp.sum((doc_ends[None, :] <= position[:, None]).astype(jnp.int32), axis=1)
    return jnp.where(inside, owner, -1)


def same_document(row_pos, col_pos, doc_ends, extent):
    return (
        doc_index(row_pos, doc_ends, extent)[:, None]
        == doc_index(col_pos, doc_ends, extent)[None, :]
    )


def tile_tables(bucket_table, shift, rows, buckets):
    offset_span = bucket_table.shape[0] // 2
    spread = jnp.arange(2 * rows - 1, dtype=jnp.int32) - (rows - 1)
    ahead_index = bucket_table[jnp.clip(shift - spread + offset_span, 0, 2 * offset_span - 1)]
    behind_index = bucket_table[jnp.clip(offset_span - shift - spread, 0, 2 * offset_span - 1)]
    bucket_ids = jnp.arange(buckets, dtype=jnp.int32)[None, :]
    ahead_onehot = (ahead_index[:, None] == bucket_ids).astype(jnp.bfloat16)
    behind_onehot = (behind_index[:, None] == bucket_ids).astype(jnp.bfloat16)
    return (ahead_index, behind_index, ahead_onehot, behind_onehot)


def skew_in(spread, width):
    rows = spread.shape[0]
    line = rows + width - 1
    flat = jnp.pad(spread, ((0, 0), (0, 1))).reshape(-1)
    return flat[rows - 1 : rows - 1 + rows * line].reshape(rows, line)[:, :width]


def skew_out(dense):
    rows, width = dense.shape
    line = rows + width - 1
    padded = jnp.pad(dense, ((0, 0), (0, rows - 1))).reshape(-1)
    flat = jnp.pad(padded, (rows - 1, 1))
    return flat.reshape(rows, line + 1)[:, :line]


def tile_scores(
    query_rows, key_rows, pos_keys, pos_queries, ahead_onehot, behind_onehot, score_scale
):
    content = contract(query_rows, key_rows, 1, 1)
    ahead_band = contract(ahead_onehot, pos_keys, 1, 0).astype(jnp.bfloat16)
    behind_band = contract(behind_onehot, pos_queries, 1, 0).astype(jnp.bfloat16)
    query_term = skew_in(contract(query_rows, ahead_band, 1, 1), key_rows.shape[0])
    key_term = skew_in(contract(key_rows, behind_band, 1, 1), query_rows.shape[0]).T
    return score_scale * (content + query_term + key_term)


def query_side(
    query_rows,
    key_rows,
    value_rows,
    grad_rows,
    pos_keys,
    pos_queries,
    same_doc,
    tables,
    score_scale,
):
    tile_rows = query_rows.shape[0]
    tile_count = key_rows.shape[0] // tile_rows
    pieces = []
    for tile in range(tile_count):
        key_tile = key_rows[tile * tile_rows : (tile + 1) * tile_rows]
        pieces.append(
            tile_scores(
                query_rows,
                key_tile,
                pos_keys,
                pos_queries,
                tables[tile][2],
                tables[tile][3],
                score_scale,
            )
        )
    scores = jnp.where(same_doc, jnp.concatenate(pieces, 1), masked_score)
    row_max = jnp.max(scores, axis=1, keepdims=True)
    expd = jnp.where(same_doc, jnp.exp(scores - row_max), 0.0)
    row_sum = jnp.sum(expd, axis=1, keepdims=True)
    probs = expd / row_sum
    dprobs = contract(grad_rows, value_rows, 1, 1)
    row_dot = jnp.sum(probs * dprobs, axis=1, keepdims=True)
    dscores = probs * (dprobs - row_dot)
    dscores_low = dscores.astype(jnp.bfloat16)
    ahead_grad = jnp.zeros((tile_rows, pos_keys.shape[0]), jnp.float32)
    for tile in range(tile_count):
        band = dscores_low[:, tile * tile_rows : (tile + 1) * tile_rows]
        ahead_grad = ahead_grad + contract(skew_out(band), tables[tile][2], 1, 0)
    ahead_low = ahead_grad.astype(jnp.bfloat16)
    query_grad = score_scale * (
        contract(dscores_low, key_rows, 1, 0) + contract(ahead_low, pos_keys, 1, 0)
    )
    bucket_key = score_scale * contract(ahead_low, query_rows, 0, 0)
    probs_low = probs.astype(jnp.bfloat16)
    behind_parts = []
    for tile in range(tile_count):
        band = dscores_low[:, tile * tile_rows : (tile + 1) * tile_rows]
        behind_parts.append(contract(skew_out(band.T), tables[tile][3], 1, 0).astype(jnp.bfloat16))
    behind_low = jnp.concatenate(behind_parts, 0)
    key_grad = score_scale * (
        contract(dscores_low, query_rows, 0, 0) + contract(behind_low, pos_queries, 1, 0)
    )
    value_grad = contract(probs_low, grad_rows, 0, 0)
    bucket_query = score_scale * contract(behind_low, key_rows, 0, 0)
    return (query_grad, key_grad, value_grad, bucket_key, bucket_query)


def split_heads(matrix):
    return matrix.reshape(matrix.shape[0], matrix.shape[1] // HD, HD).transpose(1, 0, 2)


def join_heads(stacked):
    return stacked.transpose(1, 0, 2).reshape(stacked.shape[1], stacked.shape[0] * HD)


def body(queries, keys, values, out_grad, rel_emb, w_query, w_key, doc_lengths, bucket_table):
    tokens_dev = queries.shape[0]
    seq_count = lax.axis_size("seq")
    neighbours = min(SPAN, seq_count // 4)
    extent = tokens_dev * seq_count
    seq_index = lax.axis_index("seq")
    first_token = seq_index * tokens_dev
    score_scale = 1.0 / math.sqrt(3.0 * HD)
    pos_key = jnp.dot(rel_emb, w_key, preferred_element_type=jnp.float32).astype(jnp.bfloat16)
    pos_query = jnp.dot(rel_emb, w_query, preferred_element_type=jnp.float32).astype(jnp.bfloat16)
    doc_ends = jnp.cumsum(doc_lengths)
    buckets = rel_emb.shape[0]
    tables = [
        tile_tables(bucket_table, (neighbours - tile) * tokens_dev, tokens_dev, buckets)
        for tile in range(2 * neighbours + 1)
    ]
    hop_list = list(range(neighbours, 0, -1)) + list(range(-1, -neighbours - 1, -1))
    fetched = []
    for distance in hop_list:
        fetched.append(shifted((keys, values), "seq", distance))
    lower_side = fetched[:neighbours]
    upper_side = fetched[neighbours:]
    key_window = jnp.concatenate(
        [pair[0] for pair in lower_side] + [keys] + [pair[0] for pair in upper_side], 0
    )
    value_window = jnp.concatenate(
        [pair[1] for pair in lower_side] + [values] + [pair[1] for pair in upper_side], 0
    )
    window = key_window.shape[0]
    query_pos = first_token + jnp.arange(tokens_dev, dtype=jnp.int32)
    window_pos = first_token - neighbours * tokens_dev + jnp.arange(window, dtype=jnp.int32)
    same_doc = same_document(query_pos, window_pos, doc_ends, extent)
    query_heads = split_heads(queries)
    grad_heads = split_heads(out_grad)
    pos_key_heads = split_heads(pos_key)
    pos_query_heads = split_heads(pos_query)

    def every_pair(operands):
        query_rows, key_rows, value_rows, grad_rows, pos_keys, pos_queries = operands
        return query_side(
            query_rows,
            key_rows,
            value_rows,
            grad_rows,
            pos_keys,
            pos_queries,
            same_doc,
            tables,
            score_scale,
        )

    query_grad, key_part, value_part, bucket_key, bucket_query = lax.map(
        every_pair,
        (
            query_heads,
            split_heads(key_window),
            split_heads(value_window),
            grad_heads,
            pos_key_heads,
            pos_query_heads,
        ),
    )
    key_flat = join_heads(key_part)
    value_flat = join_heads(value_part)
    key_total = key_flat[neighbours * tokens_dev : (neighbours + 1) * tokens_dev]
    value_total = value_flat[neighbours * tokens_dev : (neighbours + 1) * tokens_dev]
    for distance in hop_list:
        segment = neighbours - distance
        returned = (
            key_flat[segment * tokens_dev : (segment + 1) * tokens_dev],
            value_flat[segment * tokens_dev : (segment + 1) * tokens_dev],
        )
        arrived = shifted((returned[0], returned[1]), "seq", -distance)
        key_total = key_total + arrived[0]
        value_total = value_total + arrived[1]
    key_grad = key_total.astype(jnp.bfloat16)
    value_grad = value_total.astype(jnp.bfloat16)
    query_out = join_heads(query_grad).astype(jnp.bfloat16)
    summed = lax.psum((join_heads(bucket_key), join_heads(bucket_query)), "seq")
    bucket_key_low = summed[0].astype(jnp.bfloat16)
    bucket_query_low = summed[1].astype(jnp.bfloat16)
    rows_dev = rel_emb.shape[1] // seq_count
    rel_columns = lax.dynamic_slice_in_dim(rel_emb, seq_index * rows_dev, rows_dev, 1)
    w_key_grad = contract(rel_columns, bucket_key_low, 0, 0)
    w_query_grad = contract(rel_columns, bucket_query_low, 0, 0)
    rel_partial = contract(bucket_key_low, w_key, 1, 1) + contract(bucket_query_low, w_query, 1, 1)
    rel_emb_grad = lax.psum_scatter(
        rel_partial.astype(jnp.bfloat16), "head", scatter_dimension=1, tiled=True
    ).astype(jnp.float32)
    return (query_out, key_grad, value_grad, rel_emb_grad, w_query_grad, w_key_grad)


def nn(left, right):
    return contract(left, right, 1, 0)


def nt(left, right):
    return contract(left, right, 1, 1)


def grid_of(shape):
    return (
        lax.broadcasted_iota(jnp.int32, shape, 0),
        lax.broadcasted_iota(jnp.int32, shape, 1),
    )


def pack_kernel(q_ref, g_ref, k_ref, v_ref, out_ref, held, pieces, came, left):
    heads = out_ref.shape[0]
    wide = 2 * HD
    loads = []
    for g in range(heads // 2):
        cols = pl.ds(g * wide, wide)
        loads.append(
            [
                pltpu.make_async_copy(ref.at[:, cols], held.at[i, :, cols], came.at[g, i])
                for i, ref in enumerate((q_ref, g_ref, k_ref, v_ref))
            ]
        )
        for load in loads[g]:
            load.start()
    stores = []
    for g in range(heads // 2):
        for load in loads[g]:
            load.wait()
        for head in (2 * g, 2 * g + 1):
            cols = slice(head * HD, (head + 1) * HD)
            pieces[head] = jnp.concatenate([held[i, :, cols] for i in range(4)], 1)
        two = pl.ds(2 * g, 2)
        stores.append(pltpu.make_async_copy(pieces.at[two], out_ref.at[two], left.at[g]))
        stores[g].start()
    for store in stores:
        store.wait()


def table_kernel(scalars_ref, pos_ref, table_ref, onehot, expanded):
    buckets, valid = onehot.shape
    for part in range(buckets // TILE):
        ids = lax.broadcasted_iota(jnp.int32, (TILE, valid), 0) + part * TILE
        onehot[pl.ds(part * TILE, TILE), :] = jnp.where(ids == table_ref[...], 1.0, 0.0).astype(BF)
    pos_t = pos_ref[...].astype(F32).T.astype(BF)
    expanded[...] = nn(pos_t, onehot[...]).astype(BF)


def cut_kernel(own_ref, expanded, out_ref):
    out_ref[...] = own_ref[:, :, 2 * HD :]


def head_kernel(
    scalars_ref, own_ref, other_ref, onehot, expanded,
    send_ref, keep_ref, bucket_ref, query_ref,
    pk, pq, kvs, acc, acc_pos, g_key, g_query, k_t, k_rev, s_q, st, dp, dtile, pairs, dq_nat, dq_pos,
):
    blocks = own_ref.shape[0]
    tiles = 2 * blocks
    buckets, valid = onehot.shape
    halo = valid // 2 // TILE
    longest = 2 * halo + 1
    scale = 1.0 / math.sqrt(3.0 * HD)
    valid0 = (halo + 1) * TILE
    docs = scalars_ref.shape[0] - 1
    half = scalars_ref[docs]
    row, col = grid_of((TILE, TILE))
    swap = jnp.where(row + col == TILE - 1, 1.0, 0.0).astype(BF)
    wrap = row + col >= TILE - 1
    keep = jnp.where(col >= row, 1.0, 0.0).astype(BF)
    low = col < HD
    for table, part in ((pk, expanded[:HD]), (pq, expanded[HD:])):
        table[...] = jnp.zeros_like(table)
        table[:, valid0 : valid0 + valid] = part
    acc[...] = jnp.zeros_like(acc)
    acc_pos[...] = jnp.zeros_like(acc_pos)
    g_key[...] = jnp.zeros_like(g_key)
    g_query[...] = jnp.zeros_like(g_query)

    for b in range(blocks):
        for kv, tile in (
            (own_ref[b, :, 2 * HD : 4 * HD], 2 * b + half),
            (other_ref[b], 2 * b + 1 - half),
        ):
            kvs[tile] = kv
            k_t[tile] = kv.astype(F32).T[:HD].astype(BF)
    k_rev[...] = (
        nn(k_t[...].reshape(tiles * HD, TILE), swap).astype(BF).reshape(tiles, HD, TILE)
    )

    def block(b, carry):
        own = 2 * b + half
        token = own * TILE

        def next_end(d, state):
            end, start, stop = state
            stop = jnp.where(end < token + TILE, end + scalars_ref[d], stop)
            end = end + scalars_ref[d]
            start = jnp.where(end <= token, end, start)
            return (end, start, stop)

        zero = jnp.int32(0)
        _, reach_low, reach_high = lax.fori_loop(
            0, docs, next_end, (zero, zero, zero), unroll=docs <= 16
        )
        lowest = reach_low // TILE
        count = (reach_high + TILE - 1) // TILE - lowest
        shorter = 0
        for span in SPANS:
            if span < longest:
                pl.when((count > shorter) & (count <= span))(
                    lambda span=span: work(b, own, lowest, span)
                )
                shorter = span
        pl.when(count > shorter)(lambda: work(b, own, lowest, longest))
        return carry

    def work(b, own, lowest, span):
        first = jnp.clip(lowest, 0, tiles - span)
        delta = (own - first) * TILE
        qd = own_ref[b, :, 0 : 2 * HD]
        turned = qd.astype(F32).T
        upper = row < HD
        right = jnp.concatenate(
            [jnp.where(upper, turned, 0.0), jnp.where(upper, 0.0, turned)], 1
        ).astype(BF)
        q_rev = nn(turned[:HD].astype(BF), swap).astype(BF)

        position = own * TILE + lax.broadcasted_iota(jnp.int32, (1, TILE), 1)

        def next_doc(d, state):
            end, start, stop = state
            stop = jnp.where(end <= position, end + scalars_ref[d], stop)
            end = end + scalars_ref[d]
            start = jnp.where(end <= position, end, start)
            return (end, start, stop)

        nothing = jnp.zeros((1, TILE), jnp.int32)
        _, start, stop = lax.fori_loop(
            0, docs, next_doc, (jnp.int32(0), nothing, nothing), unroll=docs <= 16
        )
        start = start - first * TILE
        stop = stop - first * TILE

        key_x = pl.multiple_of(halo * 2 * TILE - delta, TILE)
        s_q[:, 0 : (span + 1) * TILE] = nn(qd[:, :HD], pk[:, pl.ds(key_x, (span + 1) * TILE)])
        best = jnp.full((8, TILE), masked_score, F32)
        window_kv = kvs[pl.ds(first, span)].reshape(span * TILE, 2 * HD)
        dp[0 : span * TILE, :] = nn(window_kv, right)
        for t in range(span):
            kv = window_kv[t * TILE : (t + 1) * TILE]
            query_x = pl.multiple_of(2 * halo * TILE + delta - t * TILE, TILE)
            s_k = nn(kv[:, :HD], pq[:, pl.ds(query_x, 2 * TILE)])
            key_term = pltpu.roll(
                jnp.where(wrap, s_k[:, :TILE], s_k[:, TILE:]), 1, 1, stride=1, stride_axis=0
            )
            query_term = pltpu.roll(
                jnp.where(
                    wrap,
                    s_q[:, t * TILE : (t + 1) * TILE],
                    s_q[:, (t + 1) * TILE : (t + 2) * TILE],
                ),
                1,
                1,
                stride=1,
                stride_axis=0,
            )
            score = dp[t * TILE : (t + 1) * TILE, :TILE] + key_term + query_term.T
            inside = (row >= start - t * TILE) & (row < stop - t * TILE)
            score = jnp.where(inside, score, masked_score)
            st[t] = score
            best = jnp.maximum(best, jnp.max(score.reshape(TILE // 8, 8, TILE), 0))
        top = jnp.max(best, 0, keepdims=True)
        total = jnp.zeros((8, TILE), F32)
        dot = jnp.zeros((8, TILE), F32)
        for t in range(span):
            expd = jnp.exp2((st[t] - top) * (scale * math.log2(math.e)))
            st[t] = expd
            total = total + jnp.sum(expd.reshape(TILE // 8, 8, TILE), 0)
            dot = dot + jnp.sum((expd * dp[t * TILE : (t + 1) * TILE, TILE:]).reshape(TILE // 8, 8, TILE), 0)
        inverse = 1.0 / jnp.sum(total, 0, keepdims=True)
        row_dot = jnp.sum(dot, 0, keepdims=True) * inverse

        lows = jnp.where(low, qd, jnp.zeros_like(qd))
        pair = jnp.concatenate([lows, jnp.where(low, jnp.zeros_like(qd), qd)], 0)
        dq_t = jnp.zeros((HD, TILE), F32)
        before = jnp.zeros((TILE, TILE), BF)
        near = held = None
        for t in range(span):
            prob = st[t] * inverse
            dscore = (prob * (dp[t * TILE : (t + 1) * TILE, TILE:] - row_dot)).astype(BF)
            pairs[t] = jnp.concatenate([dscore, prob.astype(BF)], 1)
            stacked = nn(
                jnp.concatenate([k_t[first + t], swap], 0),
                jnp.concatenate([dscore, dscore.T], 1),
            )
            dq_t = dq_t + stacked[:HD, :TILE]
            query_x = pl.multiple_of(2 * halo * TILE + delta - t * TILE, TILE)
            y = pltpu.roll(stacked[HD:, :TILE], 0, 1, stride=1, stride_axis=0).astype(BF)
            last = near
            near = y * keep
            far = y - near
            g_query[:, pl.ds(query_x, 2 * TILE)] += nn(
                k_rev[first + t], jnp.concatenate([near, far], 1)
            )
            chunk = pq[:, pl.ds(query_x + TILE, TILE)]
            if t == 0:
                held = nt(chunk, far)
            else:
                back = nt(chunk, jnp.concatenate([last, far], 0))
                acc_pos[first + t - 1] += held + back[:, :TILE]
                held = back[:, TILE:]
            z = pltpu.roll(stacked[HD:, TILE:], 0, 1, stride=1, stride_axis=0).astype(BF)
            here = z * keep
            dtile[:, t * TILE : (t + 1) * TILE] = here + before
            before = z - here
        acc_pos[first + span - 1] += held + nt(pq[:, pl.ds(query_x, TILE)], near)
        acc[pl.ds(first, span)] += nn(
            pairs[0:span].reshape(span * TILE, 2 * TILE), pair
        ).reshape(span, TILE, 2 * HD)
        dtile[:, span * TILE : (span + 1) * TILE] = before
        spread_q = dtile[:, 0 : (span + 1) * TILE]
        window = pl.ds(key_x, (span + 1) * TILE)
        g_key[:, window] += nn(q_rev, spread_q)
        dq_pos[b] = nt(pk[:, window], spread_q)
        dq_nat[b] = dq_t

    lax.fori_loop(0, blocks, block, 0)

    parts = []
    for g in (g_key, g_query):
        band = g[:, valid0 : valid0 + valid]
        high = band.astype(BF)
        parts += [high, (band - high.astype(F32)).astype(BF)]
    summed = nt(jnp.concatenate(parts, 0), onehot[...])
    bucket_t = scale * jnp.concatenate(
        [summed[:HD] + summed[HD : 2 * HD], summed[2 * HD : 3 * HD] + summed[3 * HD :]], 0
    )
    bucket = bucket_t.T.astype(BF)
    bucket_ref[...] = bucket
    send_ref[blocks * TILE :, :] = bucket
    factor = jnp.where(low, scale, 1.0)

    def unreverse(ref):
        part = ref[...].reshape(ref.shape[0] * HD, TILE)
        high = part.astype(BF)
        low_part = (part - high.astype(F32)).astype(BF)
        ref[...] = (nn(high, swap) + nn(low_part, swap)).reshape(ref.shape)

    unreverse(acc_pos)
    unreverse(dq_pos)

    def gradients(tile):
        extra = acc_pos[tile].T
        extra = jnp.concatenate([extra, jnp.zeros_like(extra)], 1)
        return (acc[tile] + extra) * factor

    for b in range(blocks):
        keep_ref[b] = gradients(2 * b + half)
        send_ref[b * TILE : (b + 1) * TILE, :] = gradients(2 * b + 1 - half).astype(BF)
        grad = scale * (dq_nat[b] + dq_pos[b]).T
        query_ref[b] = jnp.concatenate([grad[: TILE // 2], grad[TILE // 2 :]], 1).astype(BF)


def join_kernel(half_ref, keep_ref, bucket_ref, query_ref, came_ref, rel_ref, out_ref, weight, bucket):
    blocks = keep_ref.shape[0]
    tiles = 2 * blocks
    half = half_ref[0]
    w_rows = weight.shape[0] // tiles
    b_rows = bucket.shape[0] // tiles
    base_w = TILE + TILE // 2
    base_b = base_w + w_rows
    total = bucket_ref[...].astype(F32) + came_ref[blocks * TILE :, :].astype(F32)
    bucket[...] = total
    weight[...] = nn(total.T.astype(BF), rel_ref[...]).T
    for b in range(blocks):
        came = came_ref[b * TILE : (b + 1) * TILE, :].astype(F32)
        tile = 2 * b + half
        out_ref[b, 0:TILE, :] = (keep_ref[b] + came).astype(BF)
        out_ref[b, TILE:base_w, :] = query_ref[b]
        out_ref[b, base_w:base_b, :] = weight[pl.ds(tile * w_rows, w_rows), :].astype(BF)
        out_ref[b, base_b:, :] = bucket[pl.ds(tile * b_rows, b_rows), :].astype(BF)


def weave_kernel(half_ref, near_ref, far_ref, out_ref):
    shards, rows, _ = near_ref.shape
    half = half_ref[0]
    for shard in range(shards):
        for ref, place in ((near_ref, half), (far_ref, 1 - half)):
            start = pl.multiple_of((2 * shard + place) * rows, rows)
            out_ref[pl.ds(start, rows), :] = ref[shard].astype(F32)


def rel_kernel(side_ref, got_ref, wk_ref, wq_ref, kept_ref, away_ref):
    heads = range(got_ref.shape[0])
    rows, width = kept_ref.shape
    base_b = got_ref.shape[1] - rows
    rel = nt(jnp.concatenate([got_ref[h, base_b:, :HD] for h in heads], 1), wk_ref[...]) + nt(
        jnp.concatenate([got_ref[h, base_b:, HD:] for h in heads], 1), wq_ref[...]
    )
    left, right = rel[:, :width], rel[:, width:]
    first = jnp.full(left.shape, side_ref[0], jnp.int32) == 0
    kept_ref[...] = jnp.where(first, left, right).astype(BF)
    away_ref[...] = jnp.where(first, right, left).astype(BF)


def total_kernel(kept_ref, came_ref, after_ref, out_ref):
    total = (kept_ref[...].astype(F32) + came_ref[...].astype(F32)).astype(BF)
    for shard in range(out_ref.shape[0]):
        out_ref[shard] = total


def unpack_kernel(got_ref, dq_ref, dk_ref, dv_ref, dwq_ref, dwk_ref, done_ref):
    done_ref[...] = jnp.zeros_like(done_ref)
    base_w = TILE + TILE // 2
    base_b = base_w + dwk_ref.shape[0]
    for g in range(got_ref.shape[0] // 2):
        cols = slice(2 * g * HD, 2 * (g + 1) * HD)
        two = [got_ref[2 * g], got_ref[2 * g + 1]]
        dq_ref[:, cols] = jnp.concatenate(
            [
                jnp.concatenate([one[TILE:base_w, :HD], one[TILE:base_w, HD:]], 0)
                for one in two
            ],
            1,
        )
        dk_ref[:, cols] = jnp.concatenate([one[:TILE, :HD] for one in two], 1)
        dv_ref[:, cols] = jnp.concatenate([one[:TILE, HD:] for one in two], 1)
        dwk_ref[:, cols] = jnp.concatenate([one[base_w:base_b, :HD] for one in two], 1).astype(F32)
        dwq_ref[:, cols] = jnp.concatenate([one[base_w:base_b, HD:] for one in two], 1).astype(F32)


VMEM = pl.BlockSpec(memory_space=pltpu.VMEM)
SMEM = pl.BlockSpec(memory_space=pltpu.SMEM)
HBM = pl.BlockSpec(memory_space=pltpu.HBM)


def whole_call(kernel, inputs, outputs, scratch=(), scalars=0, source=VMEM, target=VMEM, limit=48):
    return pl.pallas_call(
        kernel,
        out_shape=outputs,
        in_specs=[SMEM] * scalars + [source] * (len(inputs) - scalars),
        out_specs=jax.tree.map(lambda _: target, outputs),
        scratch_shapes=list(scratch),
        compiler_params=pltpu.CompilerParams(vmem_limit_bytes=limit << 20),
    )(*inputs)


def head_body(queries, keys, values, out_grad, rel_emb, w_query, w_key, doc_lengths, bucket_table):
    tokens_dev, width = queries.shape
    heads = width // HD
    seq_count = lax.axis_size("seq")
    seq_index = lax.axis_index("seq")
    buckets, depth = rel_emb.shape
    halo = bucket_table.shape[0] // 2 // TILE
    span = 2 * halo + 1
    mine = seq_index // 2
    half = lax.rem(seq_index, 2).astype(jnp.int32).reshape(1)
    halves = [list(range(0, seq_count, 2)), list(range(1, seq_count, 2))]
    partners = [(i, i ^ 1) for i in range(seq_count)]
    shape = jax.ShapeDtypeStruct
    vm = pltpu.VMEM

    def spread(pieces):
        return lax.all_to_all(pieces, "seq", 0, 0, axis_index_groups=halves, tiled=True)

    packed = whole_call(
        pack_kernel,
        (queries, out_grad, keys, values),
        shape((heads, tokens_dev, 4 * HD), BF),
        [
            vm((4, tokens_dev, width), BF),
            vm((heads, tokens_dev, 4 * HD), BF),
            pltpu.SemaphoreType.DMA((heads // 2, 4)),
            pltpu.SemaphoreType.DMA((heads // 2,)),
        ],
        source=HBM,
        target=HBM,
        limit=64,
    )
    own = spread(packed)
    w_own = jnp.concatenate(
        [
            lax.dynamic_slice_in_dim(w_key, mine * HD, HD, 1),
            lax.dynamic_slice_in_dim(w_query, mine * HD, HD, 1),
        ],
        1,
    )
    pos = nn(rel_emb, w_own).astype(BF)
    table = jnp.flip(bucket_table).reshape(1, -1)
    w_rows, b_rows = depth // seq_count, buckets // seq_count
    rows = TILE + TILE // 2 + w_rows + b_rows
    line = 2 * span * TILE
    scalars = jnp.concatenate([doc_lengths, half])
    onehot, expanded = whole_call(
        table_kernel,
        (scalars, pos, table),
        [shape((buckets, table.shape[1]), BF), shape((2 * HD, table.shape[1]), BF)],
        scalars=1,
    )
    other = lax.ppermute(
        whole_call(cut_kernel, (own, expanded), shape((heads, tokens_dev, 2 * HD), BF)),
        "seq",
        partners,
    )
    sent, kept, bucket, query = whole_call(
        head_kernel,
        (scalars, own, other, onehot, expanded),
        [
            shape((heads * TILE + buckets, 2 * HD), BF),
            shape((heads, TILE, 2 * HD), F32),
            shape((buckets, 2 * HD), BF),
            shape((heads, TILE // 2, 2 * HD), BF),
        ],
        [
            vm((HD, line), BF),
            vm((HD, line), BF),
            vm((seq_count, TILE, 2 * HD), BF),
            vm((seq_count, TILE, 2 * HD), F32),
            vm((seq_count, HD, TILE), F32),
            vm((HD, line), F32),
            vm((HD, line), F32),
            vm((seq_count, HD, TILE), BF),
            vm((seq_count, HD, TILE), BF),
            vm((TILE, (span + 1) * TILE), F32),
            vm((span, TILE, TILE), F32),
            vm((span * TILE, 2 * TILE), F32),
            vm((TILE, (span + 1) * TILE), BF),
            vm((span, TILE, 2 * TILE), BF),
            vm((heads, HD, TILE), F32),
            vm((heads, HD, TILE), F32),
        ],
        scalars=1,
    )
    came = lax.ppermute(sent, "seq", partners)
    joined = whole_call(
        join_kernel,
        (half, kept, bucket, query, came, rel_emb),
        shape((heads, rows, 2 * HD), BF),
        [vm((depth, 2 * HD), F32), vm((buckets, 2 * HD), F32)],
        scalars=1,
    )
    returned = spread(joined)
    side = lax.axis_index("head").astype(jnp.int32).reshape(1)
    rel_half = shape((b_rows, width), BF)
    kept_rel, away_rel = whole_call(
        rel_kernel, (side, returned, w_key, w_query), [rel_half, rel_half], scalars=1
    )
    came_rel = lax.ppermute(away_rel, "head", [(0, 1), (1, 0)])
    tokens = shape((tokens_dev, width), BF)
    weights = shape((w_rows, width), F32)
    query_grad, key_grad, value_grad, w_query_grad, w_key_grad, done = whole_call(
        unpack_kernel,
        (returned,),
        [tokens, tokens, tokens, weights, weights, shape((8, TILE), F32)],
    )
    totals = whole_call(
        total_kernel, (kept_rel, came_rel, done), shape((heads, b_rows, width), BF)
    )
    near = spread(totals)
    far = lax.ppermute(near, "seq", partners)
    rel_emb_grad = whole_call(
        weave_kernel, (half, near, far), shape((buckets, width), F32), scalars=1
    )
    return (query_grad, key_grad, value_grad, rel_emb_grad, w_query_grad, w_key_grad)


def fits_heads(mesh, queries, rel_emb, bucket_table):
    seq, head = mesh.shape["seq"], mesh.shape["head"]
    heads = queries.shape[1] // HD // head
    return (
        head == 2
        and seq == 2 * heads
        and heads % 2 == 0
        and queries.shape[0] == seq * TILE
        and bucket_table.shape[0] % (2 * TILE) == 0
        and seq >= bucket_table.shape[0] // TILE + 1
        and rel_emb.shape[0] % (16 * seq) == 0
        and rel_emb.shape[1] % (16 * seq) == 0
        and rel_emb.shape[0] % TILE == 0
    )


def solution(mesh):
    in_specs = (
        P("seq", "head"),
        P("seq", "head"),
        P("seq", "head"),
        P("seq", "head"),
        P(),
        P(None, "head"),
        P(None, "head"),
        P(),
        P(),
    )
    out_specs = (
        P("seq", "head"),
        P("seq", "head"),
        P("seq", "head"),
        P(None, "head"),
        P("seq", "head"),
        P("seq", "head"),
    )

    def run(queries, keys, values, out_grad, rel_emb, w_query, w_key, doc_lengths, bucket_table):
        chosen = head_body if fits_heads(mesh, queries, rel_emb, bucket_table) else body
        return jax.shard_map(
            chosen, mesh=mesh, in_specs=in_specs, out_specs=out_specs, check_vma=False
        )(queries, keys, values, out_grad, rel_emb, w_query, w_key, doc_lengths, bucket_table)

    return run
```
